512 devices in a mesh: serve: 64 (over z, y), tensor: 8 (over x, core).
Axes of the slice: x: 4, y: 4, z: 16, core: 2. Of those that a mesh axis runs over, the one named last changes fastest.
Arguments:
- queries: bfloat16 [256, 4, 56, 128], P('serve', None, 'tensor'), may hold values from -4.5 to 4.5
- new_keys: bfloat16 [256, 4, 8, 128], P('serve', None, 'tensor'), may hold values from -4.5 to 4.5
- new_values: bfloat16 [256, 4, 8, 128], P('serve', None, 'tensor'), may hold values from -6 to 6
- key_cache: bfloat16 [2304, 256, 8, 128], P('serve', None, 'tensor'), may hold values from -4.5 to 4.5
- value_cache: bfloat16 [2304, 256, 8, 128], P('serve', None, 'tensor'), may hold values from -6 to 6
- lengths: int32 [256], P('serve'), may hold values from 1 to 8448, as said below
- block_owner: int32 [2304], P('serve'), may hold values from 0 to 255, as said below
- block_number: int32 [2304], P('serve'), may hold values from 0 to 32
Outputs:
- attended: bfloat16 [1024, 7168], P(('serve', 'tensor'))
The draws below stay inside these ranges and needn't reach their ends.
Inputs may be any that keep to these rules, and one draw needn't show every extreme that they name: `lengths`: the 4 sequences of each index of serve hold exactly one longer than 256, of length above 8192; the others are at most 256. Pool block p holds positions block_number[p] * 256 onward of sequence block_owner[p]. Each block 0 to ceil(length / 256) - 1 of every sequence is in the pool exactly once, and every pool block is such a block. Block 0 of a sequence lies on the index of serve that holds the sequence; a block on any other index belongs to the long sequence of the index that holds it, and each index holds at most one block of any other index's long sequence.
All inputs are finite; a program needn't handle non-finite values.
Results may differ from the reference program's by a relative error of at most 0.005.
Values may be sent and summed in bfloat16 or wider, within the bound.
No kernel may reach another device: no remote copies, remote signals or barrier semaphores. Data moves between devices by JAX's collectives and lax.ppermute only.
A program may use at most 64 MiB of HBM per device.

```python
import jax
import jax.numpy as jnp
from jax import lax

QH = 56
KVH = 8
HD = 128
NEW = 4
BLOCK = 256
SEQ_DEV = 4
HELP = 32
BLK_DEV = 36
SEQS = 256
POOL = 2304
N_SERVE = 64


def layout_tables(key):
    key = jax.random.fold_in(key, 5)
    candidates = jnp.arange(1, N_SERVE, dtype=jnp.int32)
    priority = jax.random.randint(jax.random.fold_in(key, 1), (N_SERVE - 1,), 0, 1 << 20) * N_SERVE + candidates
    forced = (candidates == N_SERVE - 1) | (candidates == N_SERVE // 2)
    priority = jnp.where(forced, candidates - N_SERVE, priority)
    offsets = jnp.take(candidates, jnp.argsort(priority))[:HELP].astype(jnp.int32)
    long_local = jax.random.randint(jax.random.fold_in(key, 2), (N_SERVE,), 0, SEQ_DEV).astype(jnp.int32)
    device = jnp.arange(N_SERVE, dtype=jnp.int32)[:, None]
    home_owner = device * SEQ_DEV + jnp.arange(SEQ_DEV, dtype=jnp.int32)[None, :]
    home_number = jnp.zeros((N_SERVE, SEQ_DEV), jnp.int32)
    source = (device - offsets[None, :]) % N_SERVE
    far_owner = source * SEQ_DEV + jnp.take(long_local, source)
    far_number = 1 + jnp.arange(HELP, dtype=jnp.int32)[None, :] + 0 * device
    owner = jnp.concatenate([home_owner, far_owner], axis=1)
    number = jnp.concatenate([home_number, far_number], axis=1)
    scores = jax.random.randint(jax.random.fold_in(key, 3), (N_SERVE, BLK_DEV), 0, 1 << 20) * BLK_DEV
    scores = scores + jnp.arange(BLK_DEV, dtype=jnp.int32)[None, :]
    order = jnp.argsort(scores, axis=1)
    owner = jnp.take_along_axis(owner, order, axis=1).reshape(-1)
    number = jnp.take_along_axis(number, order, axis=1).reshape(-1)
    return (owner.astype(jnp.int32), number.astype(jnp.int32), long_local)


def draw_lengths(key, part):
    owner, number, long_local = layout_tables(key)
    key = jax.random.fold_in(key, 11)
    short = jax.random.randint(jax.random.fold_in(key, 1), (N_SERVE, SEQ_DEV), 1, BLOCK + 1)
    tail = jax.random.randint(jax.random.fold_in(key, 2), (N_SERVE,), 1, BLOCK + 1)
    tail = jnp.where(jnp.arange(N_SERVE) == 0, BLOCK, tail)
    long_len = HELP * BLOCK + tail
    picked = jnp.arange(SEQ_DEV)[None, :] == long_local[:, None]
    return jnp.where(picked, long_len[:, None], short).reshape(-1).astype(jnp.int32)


def draw_block_owner(key, part):
    owner, number, long_local = layout_tables(key)
    return owner


def draw_block_number(key, part):
    owner, number, long_local = layout_tables(key)
    return number


def draw_key_cache(key, part):
    key = jax.random.fold_in(key, 21)
    base = jax.random.normal(jax.random.fold_in(key, 1), (POOL, BLOCK, KVH, HD), jnp.float32)
    base = jnp.clip(base, -4.5, 4.5)
    return base.astype(jnp.bfloat16)


def draw_new_keys(key, part):
    key = jax.random.fold_in(key, 31)
    base = jax.random.normal(jax.random.fold_in(key, 1), (SEQS, NEW, KVH, HD), jnp.float32)
    base = jnp.clip(base, -4.5, 4.5)
    return base.astype(jnp.bfloat16)


def draw_queries(key, part):
    key = jax.random.fold_in(key, 41)
    base = jax.random.normal(jax.random.fold_in(key, 1), (SEQS, NEW, QH, HD), jnp.float32)
    base = jnp.clip(base, -4.5, 4.5)
    return base.astype(jnp.bfloat16)


def block_levels(stream_key, extent, shards, smallest, largest):
    level, own = 1.0, jax.random.fold_in(stream_key, 6)
    for dim, blocks in shards:
        steps = jnp.exp(jax.random.uniform(jax.random.fold_in(own, dim), (blocks,), jnp.float32, smallest / len(shards), largest / len(shards)))
        level = level * jnp.repeat(steps, extent[dim] // blocks).reshape([-1 if axis == dim else 1 for axis in range(len(extent))])
    return level


def centred(key, dims, deviation, bound, split=(), held_as=jnp.bfloat16):
    entries = deviation * jax.random.normal(key, dims, jnp.float32)
    if split:
        entries = entries * block_levels(key, dims, split, -0.22, 0.18)
    return jnp.clip(entries, -bound, bound).astype(held_as)


def setup_inputs(seed: int = 0) -> dict:
    splits = jax.random.split(jax.random.key(seed), 9)
    return {
        "queries": draw_queries(jax.random.fold_in(splits[8], 71), 0),
        "new_keys": draw_new_keys(jax.random.fold_in(splits[8], 71), 0),
        "new_values": centred(splits[2], (SEQS, NEW, KVH, HD), 1.0, 6.0, ((0, 64), (2, 8))),
        "key_cache": draw_key_cache(jax.random.fold_in(splits[8], 71), 0),
        "value_cache": centred(splits[4], (POOL, BLOCK, KVH, HD), 1.0, 6.0, ((0, 64), (2, 8))),
        "lengths": draw_lengths(jax.random.fold_in(splits[8], 71), 0),
        "block_owner": draw_block_owner(jax.random.fold_in(splits[8], 71), 0),
        "block_number": draw_block_number(jax.random.fold_in(splits[8], 71), 0),
    }


neg_fill = -1.0e30


def block_partial(query_rows, keys, values, visible, score_scale):
    scores = jnp.einsum("bskgh,btkh->bkgst", query_rows.astype(jnp.float32), keys.astype(jnp.float32)) * score_scale
    scores = jnp.where(visible, scores, neg_fill)
    block_top = jnp.max(scores, axis=-1)
    weights = jnp.where(visible, jnp.exp(scores - block_top[..., None]), 0.0).astype(jnp.bfloat16)
    block_sum = jnp.sum(weights.astype(jnp.float32), axis=-1)
    block_out = jnp.einsum("bkgst,btkh->bkgsh", weights.astype(jnp.float32), values.astype(jnp.float32))
    return block_top, block_sum, block_out


def reference(queries, new_keys, new_values, key_cache, value_cache, lengths, block_owner, block_number):
    score_scale = HD ** -0.5
    groups = QH // KVH
    query_grid = queries.reshape(SEQS, NEW, KVH, groups, HD)

    def per_device(index):
        start = (index * BLK_DEV).astype(jnp.int32)
        owners = lax.dynamic_slice_in_dim(block_owner, start, BLK_DEV)
        numbers = lax.dynamic_slice_in_dim(block_number, start, BLK_DEV)
        keys = lax.dynamic_slice_in_dim(key_cache, start, BLK_DEV)
        values = lax.dynamic_slice_in_dim(value_cache, start, BLK_DEV)
        query_rows = jnp.take(query_grid, owners, axis=0)
        positions = numbers[:, None] * BLOCK + jnp.arange(BLOCK, dtype=jnp.int32)[None, :]
        visible = (positions < jnp.take(lengths, owners)[:, None])[:, None, None, None, :]
        return block_partial(query_rows, keys, values, visible, score_scale)

    tops, sums, outs = lax.map(per_device, jnp.arange(N_SERVE, dtype=jnp.int32))
    tops = tops.reshape((POOL,) + tops.shape[2:])
    sums = sums.reshape((POOL,) + sums.shape[2:])
    outs = outs.reshape((POOL,) + outs.shape[2:])
    seg_top = jax.ops.segment_max(tops, block_owner, num_segments=SEQS)
    factor = jnp.exp(tops - jnp.take(seg_top, block_owner, axis=0))
    seg_sum = jax.ops.segment_sum(factor * sums, block_owner, num_segments=SEQS)
    seg_out = jax.ops.segment_sum(factor[..., None] * outs, block_owner, num_segments=SEQS)
    causal = jnp.arange(NEW)[None, :] <= jnp.arange(NEW)[:, None]
    new_top, new_sum, new_out = block_partial(query_grid, new_keys, new_values, causal[None, None, None], score_scale)
    overall = jnp.maximum(seg_top, new_top)
    cache_factor = jnp.exp(seg_top - overall)
    new_factor = jnp.exp(new_top - overall)
    total = cache_factor * seg_sum + new_factor * new_sum
    combined = cache_factor[..., None] * seg_out + new_factor[..., None] * new_out
    result = (combined / total[..., None]).astype(jnp.bfloat16)
    return jnp.transpose(result, (0, 3, 1, 2, 4)).reshape(SEQS * NEW, QH * HD)
```

```python
import functools
import math

import jax
import jax.numpy as jnp
from jax import lax
from jax.experimental import pallas as pl
from jax.experimental.pallas import tpu as pltpu
from jax.sharding import PartitionSpec as P

neg_fill = -1e30
PAD = 32
F32 = jnp.float32
BF16 = jnp.bfloat16


def iota(shape, dim):
    return lax.broadcasted_iota(jnp.int32, shape, dim)


def prep_kernel(lengths, queries, own, message, padded):
    slots, groups, steps, head_dim = queries.shape
    rows = groups * steps
    long_slot = jnp.int32(0)
    for slot in range(slots):
        long_slot = long_slot + jnp.where(lengths[slot] > 256, slot, 0)
        length = lengths[slot]
        for g in range(groups):
            padded[slot, g * steps : (g + 1) * steps, :] = queries[slot, g].astype(F32)
        row = iota((PAD - rows, head_dim), 0)
        high = lax.shift_right_logical(length, 6).astype(F32)
        low = lax.bitwise_and(length, 63).astype(F32)
        padded[slot, rows:PAD, :] = jnp.where(row == 0, high, jnp.where(row == 1, low, 0.0))
        own[slot] = padded[slot].astype(BF16)
    tile = padded[long_slot].astype(BF16)
    message[...] = jnp.broadcast_to(tile[None], message.shape)


def main_kernel(
    chunk, scale2, owners, numbers, far, own, new_keys, new_values, key_cache, value_cache,
    back, local_out, local_lse,
    keys, values, block_out, block_lse, sems,
):
    blocks, span, head_dim = keys.shape
    slots = own.shape[0]
    steps = new_keys.shape[1]
    rows = 28
    me = lax.axis_index("serve")
    copies = []
    for c in range(blocks // chunk):
        part = pl.ds(c * chunk, chunk)
        pair = (
            pltpu.make_async_copy(key_cache.at[part], keys.at[part], sems.at[0, c]),
            pltpu.make_async_copy(value_cache.at[part], values.at[part], sems.at[1, c]),
        )
        for copy in pair:
            copy.start()
        copies.append(pair)

    row = iota((PAD, head_dim), 0)
    lane = iota((PAD, head_dim), 1)
    offset = lax.bitwise_and(me, 3) * PAD
    diagonal = jnp.logical_and(lane == offset + row, row < rows)
    in_span = jnp.logical_and(lane >= offset, lane < offset + rows)
    empty = jnp.where(jnp.logical_and(row == rows, in_span), neg_fill, 0.0).astype(BF16)
    back[...] = jnp.broadcast_to(empty[None], back.shape)

    all_rows = own[...].reshape(slots * PAD, head_dim)
    nk = new_keys[...].astype(F32).reshape(slots * steps, head_dim).astype(BF16)
    nv = new_values[...].astype(F32).reshape(slots * steps, head_dim).astype(BF16)
    scores = lax.dot_general(all_rows, nk, (((1,), (1,)), ((), ())), preferred_element_type=F32)
    r2, c2 = iota(scores.shape, 0), iota(scores.shape, 1)
    seen = jnp.logical_and(r2 // PAD == c2 // steps, c2 % steps <= r2 % steps)
    scores = jnp.where(seen, scores, neg_fill)
    top = jnp.max(scores, axis=1, keepdims=True)
    weights = jnp.where(seen, jnp.exp2((scores - top) * scale2), 0.0).astype(BF16)
    total = jnp.sum(weights.astype(F32), axis=1, keepdims=True)
    out = lax.dot_general(weights, nv, (((1,), (0,)), ((), ())), preferred_element_type=F32)
    out = out / total
    lse = jnp.broadcast_to(top * scale2 + jnp.log2(total), out.shape)
    local_out[...] = out.reshape(local_out.shape)
    local_lse[...] = lse.reshape(local_lse.shape)

    position = iota((PAD, span), 1)
    for c in range(blocks // chunk):
        for copy in copies[c]:
            copy.wait()
        ids = range(c * chunk, (c + 1) * chunk)
        owner = [owners[p] for p in ids]
        device = [lax.shift_right_logical(o, 2) for o in owner]
        mine = [d == me for d in device]
        raw = []
        for k, p in enumerate(ids):
            slot = lax.bitwise_and(owner[k], 3)
            query = jnp.where(mine[k], own[slot], far[device[k]])
            lens = query[rows : rows + 2, :].astype(F32)
            length = lens[0:1, 0:1] * 64.0 + lens[1:2, 0:1]
            score = lax.dot_general(
                query, keys[p], (((1,), (1,)), ((), ())), preferred_element_type=F32
            )
            limit = length - (numbers[p] * span).astype(F32)
            raw.append(jnp.where(position.astype(F32) < limit, score, neg_fill))
        raw = jnp.concatenate(raw, axis=0)
        top = jnp.max(raw, axis=1, keepdims=True)
        weights = jnp.exp2((raw - top) * scale2).astype(BF16)
        total = jnp.sum(weights.astype(F32), axis=1, keepdims=True)
        lse = top * scale2 + jnp.log2(total)
        inverse = 1.0 / total
        for k, p in enumerate(ids):
            part = slice(k * PAD, (k + 1) * PAD)
            out = lax.dot_general(
                weights[part], values[p], (((1,), (0,)), ((), ())), preferred_element_type=F32
            )
            out = out * inverse[part]
            column = jnp.broadcast_to(lse[part], out.shape)
            block_out[p] = out
            block_lse[p] = column
            flat = jnp.sum(jnp.where(diagonal, column, 0.0), axis=0, keepdims=True)
            high = flat.astype(BF16).astype(F32)
            rest = flat - high
            middle = rest.astype(BF16).astype(F32)
            low = rest - middle
            stats = jnp.where(
                row == rows,
                high,
                jnp.where(row == rows + 1, middle, jnp.where(row == rows + 2, low, 0.0)),
            )
            back[device[k]] = jnp.where(row < rows, out, stats).astype(BF16)
    back[me] = empty

    def merge(p, carry):
        owner = owners[p]

        @pl.when(lax.shift_right_logical(owner, 2) == me)
        def _():
            slot = lax.bitwise_and(owner, 3)
            old, new = local_lse[slot], block_lse[p]
            overall = jnp.maximum(old, new)
            a, b = jnp.exp2(old - overall), jnp.exp2(new - overall)
            total = a + b
            local_out[slot] = (a * local_out[slot] + b * block_out[p]) / total
            local_lse[slot] = overall + jnp.log2(total)

        return carry

    lax.fori_loop(0, blocks, merge, 0)


def combine_kernel(lengths, got, local_out, local_lse, result):
    devices, _, head_dim = got.shape
    slots = local_out.shape[0]
    steps, groups, rows = 4, 7, 28
    depth = devices * PAD
    many = devices // 4
    flat = got[...].reshape(depth, head_dim)
    g2, k2 = iota((many, depth), 0), iota((many, depth), 1)
    in_row = jnp.logical_and(k2 % PAD >= rows, k2 % PAD < rows + 3)
    pick = jnp.logical_and(k2 // (4 * PAD) == g2, in_row)
    lse = lax.dot_general(
        jnp.where(pick, 1.0, 0.0).astype(BF16), flat, (((1,), (0,)), ((), ())),
        preferred_element_type=F32,
    )
    top = jnp.max(lse, axis=0, keepdims=True)
    top = jnp.broadcast_to(top, (8, head_dim))
    top = jnp.maximum(top, pltpu.roll(top, 2 * PAD, 1))
    top = jnp.maximum(top, pltpu.roll(top, PAD, 1))
    weight = jnp.exp2(lse - top[0:1])
    row, lane = iota((PAD, head_dim), 0), iota((PAD, head_dim), 1)
    same = jnp.logical_and(lane % PAD == row, row < rows)
    spread = jnp.concatenate(
        [jnp.where(same, weight[g : g + 1], 0.0) for g in range(many)], axis=1
    )
    high = spread.astype(BF16)
    low = (spread - high.astype(F32)).astype(BF16)
    both = jnp.concatenate([high, low], axis=0)
    out = lax.dot_general(both, flat, (((1,), (0,)), ((), ())), preferred_element_type=F32)
    out = out[:PAD] + out[PAD:]
    total = jnp.sum(spread, axis=1, keepdims=True)
    total = jnp.where(row[:, 0:1] < rows, total, 1.0)
    first = jnp.logical_and(lane == row, row < rows)
    column = jnp.sum(jnp.where(first, top[0:1], 0.0), axis=1, keepdims=True)
    far_out = out / total
    far_lse = jnp.broadcast_to(column + jnp.log2(total), far_out.shape)
    for slot in range(slots):
        far_here = jnp.where(lengths[slot] > 256, far_lse, neg_fill)
        near = local_lse[slot]
        overall = jnp.maximum(far_here, near)
        a, b = jnp.exp2(far_here - overall), jnp.exp2(near - overall)
        final = ((a * far_out + b * local_out[slot]) / (a + b)).astype(BF16)
        for g in range(groups):
            result[slot * steps : (slot + 1) * steps, g * head_dim : (g + 1) * head_dim] = final[
                g * steps : (g + 1) * steps
            ]


VMEM = pl.BlockSpec(memory_space=pltpu.VMEM)
SMEM = pl.BlockSpec(memory_space=pltpu.SMEM)
ANY = pl.BlockSpec(memory_space=pl.ANY)


def shards(
    queries, new_keys, new_values, key_cache, value_cache, lengths, block_owner, block_number
):
    slots, steps, groups, head_dim = queries.shape
    blocks, span = key_cache.shape[:2]
    devices = lax.axis_size("serve")
    chunk = 6
    scale2 = head_dim**-0.5 * math.log2(math.e)
    queries = jnp.transpose(queries, (0, 2, 1, 3))
    new_keys = new_keys.reshape(slots, steps, head_dim)
    new_values = new_values.reshape(slots, steps, head_dim)
    key_cache = key_cache.reshape(blocks, span, head_dim)
    value_cache = value_cache.reshape(blocks, span, head_dim)

    own, message = pl.pallas_call(
        prep_kernel,
        out_shape=(
            jax.ShapeDtypeStruct((slots, PAD, head_dim), BF16),
            jax.ShapeDtypeStruct((devices, PAD, head_dim), BF16),
        ),
        in_specs=[SMEM, VMEM],
        out_specs=(VMEM, VMEM),
        scratch_shapes=[pltpu.VMEM((slots, PAD, head_dim), F32)],
        name="prep",
    )(lengths, queries)
    far = lax.all_to_all(message, "serve", split_axis=0, concat_axis=0, tiled=True)
    back, local_out, local_lse = pl.pallas_call(
        functools.partial(main_kernel, chunk, scale2),
        out_shape=(
            jax.ShapeDtypeStruct((devices, PAD, head_dim), BF16),
            jax.ShapeDtypeStruct((slots, PAD, head_dim), F32),
            jax.ShapeDtypeStruct((slots, PAD, head_dim), F32),
        ),
        in_specs=[SMEM, SMEM, VMEM, VMEM, VMEM, VMEM, ANY, ANY],
        out_specs=(VMEM, VMEM, VMEM),
        scratch_shapes=[
            pltpu.VMEM((blocks, span, head_dim), BF16),
            pltpu.VMEM((blocks, span, head_dim), BF16),
            pltpu.VMEM((blocks, PAD, head_dim), F32),
            pltpu.VMEM((blocks, PAD, head_dim), F32),
            pltpu.SemaphoreType.DMA((2, blocks // chunk)),
        ],
        compiler_params=pltpu.CompilerParams(vmem_limit_bytes=24 << 20),
        name="blocks",
    )(block_owner, block_number, far, own, new_keys, new_values, key_cache, value_cache)
    got = lax.all_to_all(back, "serve", split_axis=0, concat_axis=0, tiled=True)
    rows_out = pl.pallas_call(
        combine_kernel,
        out_shape=jax.ShapeDtypeStruct((slots * steps, groups * head_dim), BF16),
        in_specs=[SMEM, VMEM, VMEM, VMEM],
        out_specs=VMEM,
        name="combine",
    )(lengths, got, local_out, local_lse)
    return lax.all_to_all(rows_out, "tensor", split_axis=0, concat_axis=1, tiled=True)


def solution(mesh):
    placed = (
        P("serve", None, "tensor", None),
        P("serve", None, "tensor", None),
        P("serve", None, "tensor", None),
        P("serve", None, "tensor", None),
        P("serve", None, "tensor", None),
        P("serve"),
        P("serve"),
        P("serve"),
    )
    return jax.shard_map(
        shards, mesh=mesh, in_specs=placed, out_specs=P(("serve", "tensor"), None), check_vma=False
    )
```

```python
import functools
import math

import jax
import jax.numpy as jnp
from jax import lax
from jax.experimental import pallas as pl
from jax.experimental.pallas import tpu as pltpu
from jax.sharding import PartitionSpec as P

neg_fill = -1e30
PAD = 32
F32 = jnp.float32
BF16 = jnp.bfloat16


def iota(shape, dim):
    return lax.broadcasted_iota(jnp.int32, shape, dim)


def column_first(device):
    return lax.bitwise_and(device, 3) * 16 + lax.shift_right_logical(device, 2)


def message_of(out, lse, rows):
    row = iota(out.shape, 0)
    high = lse.astype(BF16).astype(F32)
    rest = lse - high
    middle = rest.astype(BF16).astype(F32)
    low = rest - middle
    stats = jnp.where(
        row == rows,
        high,
        jnp.where(row == rows + 1, middle, jnp.where(row == rows + 2, low, 0.0)),
    )
    return jnp.where(row < rows, out, stats).astype(BF16)


def prep_kernel(lengths, queries, own, message, padded):
    slots, groups, steps, head_dim = queries.shape
    rows = groups * steps
    long_slot = jnp.int32(0)
    for slot in range(slots):
        long_slot = long_slot + jnp.where(lengths[slot] > 256, slot, 0)
        length = lengths[slot]
        for g in range(groups):
            padded[slot, g * steps : (g + 1) * steps, :] = queries[slot, g].astype(F32)
        row = iota((PAD - rows, head_dim), 0)
        high = lax.shift_right_logical(length, 6).astype(F32)
        low = lax.bitwise_and(length, 63).astype(F32)
        padded[slot, rows:PAD, :] = jnp.where(row == 0, high, jnp.where(row == 1, low, 0.0))
        own[slot] = padded[slot].astype(BF16)
    tile = padded[long_slot].astype(BF16)
    message[...] = jnp.broadcast_to(tile[None], message.shape)


def main_kernel(
    chunk, scale2, owners, numbers, far, own, new_keys, new_values, key_cache, value_cache,
    back, local_out, local_lse,
    keys, values, block_out, block_lse, sems,
):
    blocks, span, head_dim = keys.shape
    slots = own.shape[0]
    steps = new_keys.shape[1]
    rows = 28
    me = lax.axis_index("serve")
    copies = []
    for c in range(blocks // chunk):
        part = pl.ds(c * chunk, chunk)
        pair = (
            pltpu.make_async_copy(key_cache.at[part], keys.at[part], sems.at[0, c]),
            pltpu.make_async_copy(value_cache.at[part], values.at[part], sems.at[1, c]),
        )
        for copy in pair:
            copy.start()
        copies.append(pair)

    row = iota((PAD, head_dim), 0)
    lane = iota((PAD, head_dim), 1)
    offset = lax.bitwise_and(me, 3) * PAD
    diagonal = jnp.logical_and(lane == offset + row, row < rows)
    in_span = jnp.logical_and(lane >= offset, lane < offset + rows)
    empty = jnp.where(jnp.logical_and(row == rows, in_span), neg_fill, 0.0).astype(BF16)
    back[...] = jnp.broadcast_to(empty[None], back.shape)

    all_rows = own[...].reshape(slots * PAD, head_dim)
    nk = new_keys[...].astype(F32).reshape(slots * steps, head_dim).astype(BF16)
    nv = new_values[...].astype(F32).reshape(slots * steps, head_dim).astype(BF16)
    scores = lax.dot_general(all_rows, nk, (((1,), (1,)), ((), ())), preferred_element_type=F32)
    r2, c2 = iota(scores.shape, 0), iota(scores.shape, 1)
    seen = jnp.logical_and(r2 // PAD == c2 // steps, c2 % steps <= r2 % steps)
    scores = jnp.where(seen, scores, neg_fill)
    top = jnp.max(scores, axis=1, keepdims=True)
    weights = jnp.where(seen, jnp.exp2((scores - top) * scale2), 0.0).astype(BF16)
    total = jnp.sum(weights.astype(F32), axis=1, keepdims=True)
    out = lax.dot_general(weights, nv, (((1,), (0,)), ((), ())), preferred_element_type=F32)
    out = out / total
    lse = jnp.broadcast_to(top * scale2 + jnp.log2(total), out.shape)
    local_out[...] = out.reshape(local_out.shape)
    local_lse[...] = lse.reshape(local_lse.shape)

    position = iota((PAD, span), 1)
    for c in range(blocks // chunk):
        for copy in copies[c]:
            copy.wait()
        ids = range(c * chunk, (c + 1) * chunk)
        owner = [owners[p] for p in ids]
        device = [lax.shift_right_logical(o, 2) for o in owner]
        mine = [d == me for d in device]
        place = [column_first(d) for d in device]
        raw = []
        for k, p in enumerate(ids):
            slot = lax.bitwise_and(owner[k], 3)
            query = jnp.where(mine[k], own[slot], far[place[k]])
            lens = query[rows : rows + 2, :].astype(F32)
            length = lens[0:1, 0:1] * 64.0 + lens[1:2, 0:1]
            score = lax.dot_general(
                query, keys[p], (((1,), (1,)), ((), ())), preferred_element_type=F32
            )
            limit = length - (numbers[p] * span).astype(F32)
            raw.append(jnp.where(position.astype(F32) < limit, score, neg_fill))
        raw = jnp.concatenate(raw, axis=0)
        top = jnp.max(raw, axis=1, keepdims=True)
        weights = jnp.exp2((raw - top) * scale2).astype(BF16)
        total = jnp.sum(weights.astype(F32), axis=1, keepdims=True)
        lse = top * scale2 + jnp.log2(total)
        inverse = 1.0 / total
        for k, p in enumerate(ids):
            part = slice(k * PAD, (k + 1) * PAD)
            out = lax.dot_general(
                weights[part], values[p], (((1,), (0,)), ((), ())), preferred_element_type=F32
            )
            out = out * inverse[part]
            column = jnp.broadcast_to(lse[part], out.shape)
            block_out[p] = out
            block_lse[p] = column
            flat = jnp.sum(jnp.where(diagonal, column, 0.0), axis=0, keepdims=True)
            back[place[k]] = message_of(out, flat, rows)
    back[column_first(me)] = empty

    def merge(p, carry):
        owner = owners[p]

        @pl.when(lax.shift_right_logical(owner, 2) == me)
        def _():
            slot = lax.bitwise_and(owner, 3)
            old, new = local_lse[slot], block_lse[p]
            overall = jnp.maximum(old, new)
            a, b = jnp.exp2(old - overall), jnp.exp2(new - overall)
            total = a + b
            local_out[slot] = (a * local_out[slot] + b * block_out[p]) / total
            local_lse[slot] = overall + jnp.log2(total)

        return carry

    lax.fori_loop(0, blocks, merge, 0)


def four_fold(x, op):
    x = op(x, pltpu.roll(x, 2 * PAD, 1))
    return op(x, pltpu.roll(x, PAD, 1))


def stage_kernel(got, onward):
    sources, many, _, head_dim = got.shape
    rows = 28
    me = lax.axis_index("serve")
    depth = sources * many * PAD
    flat = got[...].reshape(depth, head_dim)
    g2, k2 = iota((many, depth), 0), iota((many, depth), 1)
    in_row = jnp.logical_and(k2 % PAD >= rows, k2 % PAD < rows + 3)
    pick = jnp.logical_and((k2 // PAD) % many == g2, in_row)
    lse = lax.dot_general(
        jnp.where(pick, 1.0, 0.0).astype(BF16), flat, (((1,), (0,)), ((), ())),
        preferred_element_type=F32,
    )
    top = four_fold(lse, jnp.maximum)
    weight = jnp.exp2(lse - top)
    total = four_fold(weight, jnp.add)
    weight = weight / total
    row, lane = iota((PAD, head_dim), 0), iota((PAD, head_dim), 1)
    same = jnp.logical_and(lane % PAD == row, row < rows)
    offset = lax.bitwise_and(lax.shift_right_logical(me, 2), 3) * PAD
    lane = iota((many, head_dim), 1)
    in_span = jnp.logical_and(lane >= offset, lane < offset + rows)
    lse = jnp.where(in_span, top + jnp.log2(total), 0.0)
    for m in range(many):
        spread = jnp.where(same, weight[m : m + 1], 0.0)
        high = spread.astype(BF16)
        low = (spread - high.astype(F32)).astype(BF16)
        both = jnp.concatenate([high, low], axis=0)
        block = got[:, m].reshape(sources * PAD, head_dim)
        out = lax.dot_general(both, block, (((1,), (0,)), ((), ())), preferred_element_type=F32)
        onward[m] = message_of(out[:PAD] + out[PAD:], lse[m : m + 1], rows)


def combine_kernel(lengths, got, local_out, local_lse, result):
    devices, _, head_dim = got.shape
    slots = local_out.shape[0]
    steps, groups, rows = 4, 7, 28
    depth = devices * PAD
    many = devices // 4
    flat = got[...].reshape(depth, head_dim)
    g2, k2 = iota((many, depth), 0), iota((many, depth), 1)
    in_row = jnp.logical_and(k2 % PAD >= rows, k2 % PAD < rows + 3)
    pick = jnp.logical_and(k2 // (4 * PAD) == g2, in_row)
    lse = lax.dot_general(
        jnp.where(pick, 1.0, 0.0).astype(BF16), flat, (((1,), (0,)), ((), ())),
        preferred_element_type=F32,
    )
    top = jnp.max(lse, axis=0, keepdims=True)
    top = jnp.broadcast_to(top, (8, head_dim))
    top = four_fold(top, jnp.maximum)
    weight = jnp.exp2(lse - top[0:1])
    row, lane = iota((PAD, head_dim), 0), iota((PAD, head_dim), 1)
    same = jnp.logical_and(lane % PAD == row, row < rows)
    spread = jnp.concatenate(
        [jnp.where(same, weight[g : g + 1], 0.0) for g in range(many)], axis=1
    )
    high = spread.astype(BF16)
    low = (spread - high.astype(F32)).astype(BF16)
    both = jnp.concatenate([high, low], axis=0)
    out = lax.dot_general(both, flat, (((1,), (0,)), ((), ())), preferred_element_type=F32)
    out = out[:PAD] + out[PAD:]
    total = jnp.sum(spread, axis=1, keepdims=True)
    total = jnp.where(row[:, 0:1] < rows, total, 1.0)
    first = jnp.logical_and(lane == row, row < rows)
    column = jnp.sum(jnp.where(first, top[0:1], 0.0), axis=1, keepdims=True)
    far_out = out / total
    far_lse = jnp.broadcast_to(column + jnp.log2(total), far_out.shape)
    for slot in range(slots):
        far_here = jnp.where(lengths[slot] > 256, far_lse, neg_fill)
        near = local_lse[slot]
        overall = jnp.maximum(far_here, near)
        a, b = jnp.exp2(far_here - overall), jnp.exp2(near - overall)
        final = ((a * far_out + b * local_out[slot]) / (a + b)).astype(BF16)
        for g in range(groups):
            columns = slice(g * head_dim, (g + 1) * head_dim)
            for half in range(2):
                start = g * steps + half * 2
                result[slot * 2 + half, :, columns] = final[start : start + 2]


VMEM = pl.BlockSpec(memory_space=pltpu.VMEM)
SMEM = pl.BlockSpec(memory_space=pltpu.SMEM)
HBM = pl.BlockSpec(memory_space=pltpu.HBM)


def shards(
    queries, new_keys, new_values, key_cache, value_cache, lengths, block_owner, block_number
):
    slots, steps, groups, head_dim = queries.shape
    blocks, span = key_cache.shape[:2]
    devices = lax.axis_size("serve")
    chunk = 6
    scale2 = head_dim**-0.5 * math.log2(math.e)
    queries = jnp.transpose(queries, (0, 2, 1, 3))
    new_keys = new_keys.reshape(slots, steps, head_dim)
    new_values = new_values.reshape(slots, steps, head_dim)
    key_cache = key_cache.reshape(blocks, span, head_dim)
    value_cache = value_cache.reshape(blocks, span, head_dim)

    along_z = [[4 * z + y for z in range(16)] for y in range(4)]
    along_y = [[4 * z + y for y in range(4)] for z in range(16)]
    exchange = functools.partial(
        lax.all_to_all, axis_name="serve", split_axis=0, concat_axis=0, tiled=True
    )
    own, message = pl.pallas_call(
        prep_kernel,
        out_shape=(
            jax.ShapeDtypeStruct((slots, PAD, head_dim), BF16),
            jax.ShapeDtypeStruct((16, PAD, head_dim), BF16),
        ),
        in_specs=[SMEM, VMEM],
        out_specs=(VMEM, VMEM),
        scratch_shapes=[pltpu.VMEM((slots, PAD, head_dim), F32)],
        name="prep",
    )(lengths, queries)
    column = exchange(message, axis_index_groups=along_z)
    far = exchange(jnp.broadcast_to(column[None], (4,) + column.shape), axis_index_groups=along_y)
    back, local_out, local_lse = pl.pallas_call(
        functools.partial(main_kernel, chunk, scale2),
        out_shape=(
            jax.ShapeDtypeStruct((devices, PAD, head_dim), BF16),
            jax.ShapeDtypeStruct((slots, PAD, head_dim), F32),
            jax.ShapeDtypeStruct((slots, PAD, head_dim), F32),
        ),
        in_specs=[SMEM, SMEM, VMEM, VMEM, VMEM, VMEM, HBM, HBM],
        out_specs=(VMEM, VMEM, VMEM),
        scratch_shapes=[
            pltpu.VMEM((blocks, span, head_dim), BF16),
            pltpu.VMEM((blocks, span, head_dim), BF16),
            pltpu.VMEM((blocks, PAD, head_dim), F32),
            pltpu.VMEM((blocks, PAD, head_dim), F32),
            pltpu.SemaphoreType.DMA((2, blocks // chunk)),
        ],
        compiler_params=pltpu.CompilerParams(vmem_limit_bytes=56 << 20),
        name="blocks",
    )(
        block_owner, block_number, far.reshape(devices, PAD, head_dim), own,
        new_keys, new_values, key_cache, value_cache,
    )
    back = back.reshape(4, 16, PAD, head_dim)
    row_got = exchange(back, axis_index_groups=along_y)
    onward = pl.pallas_call(
        stage_kernel,
        out_shape=jax.ShapeDtypeStruct((16, PAD, head_dim), BF16),
        in_specs=[VMEM],
        out_specs=VMEM,
        name="stage",
    )(row_got)
    got = exchange(onward, axis_index_groups=along_z)
    rows_out = pl.pallas_call(
        combine_kernel,
        out_shape=jax.ShapeDtypeStruct((8, 2, groups * head_dim), BF16),
        in_specs=[SMEM, VMEM, VMEM, VMEM],
        out_specs=VMEM,
        name="combine",
    )(lengths, got, local_out, local_lse)
    swapped = lax.all_to_all(rows_out, "tensor", split_axis=0, concat_axis=0, tiled=True)
    return jnp.transpose(swapped, (1, 0, 2)).reshape(2, 8 * groups * head_dim)


def solution(mesh):
    placed = (
        P("serve", None, "tensor", None),
        P("serve", None, "tensor", None),
        P("serve", None, "tensor", None),
        P("serve", None, "tensor", None),
        P("serve", None, "tensor", None),
        P("serve"),
        P("serve"),
        P("serve"),
    )
    return jax.shard_map(
        shards, mesh=mesh, in_specs=placed, out_specs=P(("serve", "tensor"), None), check_vma=False
    )
```

```python
import functools
import math

import jax
import jax.numpy as jnp
from jax import lax
from jax.experimental import pallas as pl
from jax.experimental.pallas import tpu as pltpu
from jax.sharding import PartitionSpec as P

neg_fill = -1e30
PAD = 32
F32 = jnp.float32
BF16 = jnp.bfloat16


def iota(shape, dim):
    return lax.broadcasted_iota(jnp.int32, shape, dim)


def column_first(device):
    return lax.bitwise_and(device, 3) * 16 + lax.shift_right_logical(device, 2)


def message_of(out, lse, rows):
    row = iota(out.shape, 0)
    high = lse.astype(BF16).astype(F32)
    rest = lse - high
    middle = rest.astype(BF16).astype(F32)
    low = rest - middle
    stats = jnp.where(
        row == rows,
        high,
        jnp.where(row == rows + 1, middle, jnp.where(row == rows + 2, low, 0.0)),
    )
    return jnp.where(row < rows, out, stats).astype(BF16)


def pad_rows(length, query, padded):
    groups, steps, head_dim = query.shape
    rows = groups * steps
    for g in range(groups):
        padded[g * steps : (g + 1) * steps, :] = query[g].astype(F32)
    row = iota((PAD - rows, head_dim), 0)
    high = lax.shift_right_logical(length, 6).astype(F32)
    low = lax.bitwise_and(length, 63).astype(F32)
    padded[rows:PAD, :] = jnp.where(row == 0, high, jnp.where(row == 1, low, 0.0))


def fetch(pairs, sems):
    copies = [
        pltpu.make_async_copy(source, target, sems.at[i])
        for i, (source, target) in enumerate(pairs)
    ]
    for copy in copies:
        copy.start()
    return copies


def prep_kernel(lengths_hbm, queries_hbm, message, lengths, queries, padded, sems):
    copies = fetch(((lengths_hbm, lengths), (queries_hbm, queries)), sems)
    for copy in copies:
        copy.wait()
    long_slot, length = jnp.int32(0), lengths[0]
    for slot in range(1, queries.shape[0]):
        is_long = lengths[slot] > 256
        long_slot = jnp.where(is_long, slot, long_slot)
        length = jnp.where(is_long, lengths[slot], length)
    pad_rows(length, queries.at[long_slot], padded)
    message[...] = jnp.broadcast_to(padded[...].astype(BF16)[None], message.shape)


def attend(query, limit, keys, values, scale2):
    score = lax.dot_general(query, keys, (((1,), (1,)), ((), ())), preferred_element_type=F32)
    score = jnp.where(iota(score.shape, 1).astype(F32) < limit, score, neg_fill)
    top = jnp.max(score, axis=1, keepdims=True)
    weights = jnp.exp2((score - top) * scale2).astype(BF16)
    total = jnp.sum(weights.astype(F32), axis=1, keepdims=True)
    out = lax.dot_general(weights, values, (((1,), (0,)), ((), ())), preferred_element_type=F32)
    return out / total, top * scale2 + jnp.log2(total)


def local_kernel(
    scale2, lengths_hbm, owners_hbm, numbers_hbm, queries_hbm, new_keys_hbm, new_values_hbm,
    key_cache, value_cache,
    keys, table, local_out, local_lse,
    lengths, owners, numbers, queries, new_keys, new_values, padded, one_value, sems,
):
    blocks, span, head_dim = keys.shape
    slots, steps, _ = new_keys.shape
    me = lax.axis_index("serve")
    small = ((lengths_hbm, lengths), (owners_hbm, owners), (numbers_hbm, numbers),
             (queries_hbm, queries), (new_keys_hbm, new_keys), (new_values_hbm, new_values))
    copies = fetch(small + ((key_cache, keys),), sems)
    for copy in copies[: len(small)]:
        copy.wait()

    def place(p, counts):
        far_count, near_count = counts
        device = lax.shift_right_logical(owners[p], 2)
        near = device == me
        at = jnp.where(near, blocks - 1 - near_count, far_count)
        table[at] = p
        table[64 + at] = jnp.where(near, lax.bitwise_and(owners[p], 3), column_first(device))
        table[128 + at] = numbers[p] * span
        one = near.astype(jnp.int32)
        return far_count + 1 - one, near_count + one

    far_count, near_count = lax.fori_loop(0, blocks, place, (jnp.int32(0), jnp.int32(0)))
    table[192] = far_count

    for slot in range(slots):
        pad_rows(lengths[slot], queries.at[slot], padded.at[slot])
    all_rows = padded[...].astype(BF16).reshape(slots * PAD, head_dim)
    nk = new_keys[...].astype(F32).reshape(slots * steps, head_dim).astype(BF16)
    nv = new_values[...].astype(F32).reshape(slots * steps, head_dim).astype(BF16)
    scores = lax.dot_general(all_rows, nk, (((1,), (1,)), ((), ())), preferred_element_type=F32)
    r2, c2 = iota(scores.shape, 0), iota(scores.shape, 1)
    seen = jnp.logical_and(r2 // PAD == c2 // steps, c2 % steps <= r2 % steps)
    scores = jnp.where(seen, scores, neg_fill)
    top = jnp.max(scores, axis=1, keepdims=True)
    weights = jnp.where(seen, jnp.exp2((scores - top) * scale2), 0.0).astype(BF16)
    total = jnp.sum(weights.astype(F32), axis=1, keepdims=True)
    out = lax.dot_general(weights, nv, (((1,), (0,)), ((), ())), preferred_element_type=F32)
    lse = jnp.broadcast_to(top * scale2 + jnp.log2(total), out.shape)
    local_out[...] = (out / total).reshape(local_out.shape)
    local_lse[...] = lse.reshape(local_lse.shape)
    for copy in copies[len(small) :]:
        copy.wait()

    def merge(k, carry):
        p, slot = table[blocks - 1 - k], table[64 + blocks - 1 - k]
        copy = pltpu.make_async_copy(value_cache.at[p], one_value, sems.at[7])
        copy.start()
        copy.wait()
        limit = (lengths[slot] - table[128 + blocks - 1 - k]).astype(F32)
        new_out, new = attend(padded[slot].astype(BF16), limit, keys[p], one_value[...], scale2)
        old, new = local_lse[slot], jnp.broadcast_to(new, new_out.shape)
        overall = jnp.maximum(old, new)
        a, b = jnp.exp2(old - overall), jnp.exp2(new - overall)
        total = a + b
        local_out[slot] = (a * local_out[slot] + b * new_out) / total
        local_lse[slot] = overall + jnp.log2(total)
        return carry

    lax.fori_loop(0, near_count, merge, 0)


def far_kernel(chunk, scale2, table, far, keys, value_cache, back, values, sems):
    blocks, span, head_dim = keys.shape
    rows = 28
    count = blocks - 4
    me = lax.axis_index("serve")
    far_count = table[192]
    copies = fetch([(value_cache.at[table[k]], values.at[k]) for k in range(count)], sems)
    row, lane = iota((PAD, head_dim), 0), iota((PAD, head_dim), 1)
    offset = lax.bitwise_and(me, 3) * PAD
    diagonal = jnp.logical_and(lane == offset + row, row < rows)
    in_span = jnp.logical_and(lane >= offset, lane < offset + rows)
    empty = jnp.where(jnp.logical_and(row == rows, in_span), neg_fill, 0.0).astype(BF16)
    back[...] = jnp.broadcast_to(empty[None], back.shape)
    unused = column_first(me)
    position = iota((PAD, span), 1).astype(F32)
    for c in range(count // chunk):
        ids = [table[k] for k in range(c * chunk, (c + 1) * chunk)]
        places = [
            jnp.where(k < far_count, table[64 + k], unused)
            for k in range(c * chunk, (c + 1) * chunk)
        ]
        raw = []
        for k in range(chunk):
            query = far[places[k]]
            lens = query[rows : rows + 2, :].astype(F32)
            length = lens[0:1, 0:1] * 64.0 + lens[1:2, 0:1]
            score = lax.dot_general(
                query, keys[ids[k]], (((1,), (1,)), ((), ())), preferred_element_type=F32
            )
            limit = length - table[128 + c * chunk + k].astype(F32)
            raw.append(jnp.where(position < limit, score, neg_fill))
        raw = jnp.concatenate(raw, axis=0)
        top = jnp.max(raw, axis=1, keepdims=True)
        weights = jnp.exp2((raw - top) * scale2).astype(BF16)
        total = jnp.sum(weights.astype(F32), axis=1, keepdims=True)
        lse = top * scale2 + jnp.log2(total)
        inverse = 1.0 / total
        for k in range(chunk):
            part = slice(k * PAD, (k + 1) * PAD)
            copies[c * chunk + k].wait()
            out = lax.dot_general(
                weights[part], values[c * chunk + k], (((1,), (0,)), ((), ())),
                preferred_element_type=F32,
            )
            flat = jnp.sum(jnp.where(diagonal, lse[part], 0.0), axis=0, keepdims=True)
            back[places[k]] = message_of(out * inverse[part], flat, rows)
    back[unused] = empty


def four_fold(x, op):
    x = op(x, pltpu.roll(x, 2 * PAD, 1))
    return op(x, pltpu.roll(x, PAD, 1))


def stage_kernel(got, onward):
    sources, many, _, head_dim = got.shape
    rows = 28
    me = lax.axis_index("serve")
    depth = sources * many * PAD
    flat = got[...].reshape(depth, head_dim)
    g2, k2 = iota((many, depth), 0), iota((many, depth), 1)
    in_row = jnp.logical_and(k2 % PAD >= rows, k2 % PAD < rows + 3)
    pick = jnp.logical_and((k2 // PAD) % many == g2, in_row)
    lse = lax.dot_general(
        jnp.where(pick, 1.0, 0.0).astype(BF16), flat, (((1,), (0,)), ((), ())),
        preferred_element_type=F32,
    )
    top = four_fold(lse, jnp.maximum)
    weight = jnp.exp2(lse - top)
    total = four_fold(weight, jnp.add)
    weight = weight / total
    row, lane = iota((PAD, head_dim), 0), iota((PAD, head_dim), 1)
    same = jnp.logical_and(lane % PAD == row, row < rows)
    offset = lax.bitwise_and(lax.shift_right_logical(me, 2), 3) * PAD
    lane = iota((many, head_dim), 1)
    in_span = jnp.logical_and(lane >= offset, lane < offset + rows)
    lse = jnp.where(in_span, top + jnp.log2(total), 0.0)
    for m in range(many):
        spread = jnp.where(same, weight[m : m + 1], 0.0)
        high = spread.astype(BF16)
        low = (spread - high.astype(F32)).astype(BF16)
        both = jnp.concatenate([high, low], axis=0)
        block = got[:, m].reshape(sources * PAD, head_dim)
        out = lax.dot_general(both, block, (((1,), (0,)), ((), ())), preferred_element_type=F32)
        onward[m] = message_of(out[:PAD] + out[PAD:], lse[m : m + 1], rows)


def combine_kernel(lengths_hbm, got, local_out, local_lse, result, lengths, sems):
    copies = fetch(((lengths_hbm, lengths),), sems)
    devices, _, head_dim = got.shape
    slots = local_out.shape[0]
    steps, groups, rows = 4, 7, 28
    depth = devices * PAD
    many = devices // 4
    flat = got[...].reshape(depth, head_dim)
    g2, k2 = iota((many, depth), 0), iota((many, depth), 1)
    in_row = jnp.logical_and(k2 % PAD >= rows, k2 % PAD < rows + 3)
    pick = jnp.logical_and(k2 // (4 * PAD) == g2, in_row)
    lse = lax.dot_general(
        jnp.where(pick, 1.0, 0.0).astype(BF16), flat, (((1,), (0,)), ((), ())),
        preferred_element_type=F32,
    )
    top = jnp.max(lse, axis=0, keepdims=True)
    top = jnp.broadcast_to(top, (8, head_dim))
    top = four_fold(top, jnp.maximum)
    weight = jnp.exp2(lse - top[0:1])
    row, lane = iota((PAD, head_dim), 0), iota((PAD, head_dim), 1)
    same = jnp.logical_and(lane % PAD == row, row < rows)
    spread = jnp.concatenate(
        [jnp.where(same, weight[g : g + 1], 0.0) for g in range(many)], axis=1
    )
    high = spread.astype(BF16)
    low = (spread - high.astype(F32)).astype(BF16)
    both = jnp.concatenate([high, low], axis=0)
    out = lax.dot_general(both, flat, (((1,), (0,)), ((), ())), preferred_element_type=F32)
    out = out[:PAD] + out[PAD:]
    total = jnp.sum(spread, axis=1, keepdims=True)
    total = jnp.where(row[:, 0:1] < rows, total, 1.0)
    first = jnp.logical_and(lane == row, row < rows)
    column = jnp.sum(jnp.where(first, top[0:1], 0.0), axis=1, keepdims=True)
    far_out = out / total
    far_lse = jnp.broadcast_to(column + jnp.log2(total), far_out.shape)
    copies[0].wait()
    for slot in range(slots):
        far_here = jnp.where(lengths[slot] > 256, far_lse, neg_fill)
        near = local_lse[slot]
        overall = jnp.maximum(far_here, near)
        a, b = jnp.exp2(far_here - overall), jnp.exp2(near - overall)
        final = ((a * far_out + b * local_out[slot]) / (a + b)).astype(BF16)
        for g in range(groups):
            columns = slice(g * head_dim, (g + 1) * head_dim)
            for half in range(2):
                start = g * steps + half * 2
                result[slot * 2 + half, :, columns] = final[start : start + 2]


VMEM = pl.BlockSpec(memory_space=pltpu.VMEM)
SMEM = pl.BlockSpec(memory_space=pltpu.SMEM)
HBM = pl.BlockSpec(memory_space=pltpu.HBM)


def shards(
    queries, new_keys, new_values, key_cache, value_cache, lengths, block_owner, block_number
):
    slots, steps, groups, head_dim = queries.shape
    blocks, span = key_cache.shape[:2]
    devices = lax.axis_size("serve")
    chunk = 8
    scale2 = head_dim**-0.5 * math.log2(math.e)
    queries = jnp.transpose(queries, (0, 2, 1, 3))
    new_keys = new_keys.reshape(slots, steps, head_dim)
    new_values = new_values.reshape(slots, steps, head_dim)
    key_cache = key_cache.reshape(blocks, span, head_dim)
    value_cache = value_cache.reshape(blocks, span, head_dim)

    along_z = [[4 * z + y for z in range(16)] for y in range(4)]
    along_y = [[4 * z + y for y in range(4)] for z in range(16)]
    exchange = functools.partial(
        lax.all_to_all, axis_name="serve", split_axis=0, concat_axis=0, tiled=True
    )
    in_hbm = functools.partial(pltpu.with_memory_space_constraint, memory_space=pltpu.HBM)
    in_vmem = functools.partial(pltpu.with_memory_space_constraint, memory_space=pltpu.VMEM)
    queries, new_keys, new_values, key_cache, value_cache, lengths, block_owner, block_number = map(
        in_hbm,
        (queries, new_keys, new_values, key_cache, value_cache, lengths, block_owner, block_number),
    )
    small = pltpu.CompilerParams(vmem_limit_bytes=8 << 20)
    message = pl.pallas_call(
        prep_kernel,
        out_shape=jax.ShapeDtypeStruct((16, PAD, head_dim), BF16),
        in_specs=[HBM, HBM],
        out_specs=VMEM,
        scratch_shapes=[
            pltpu.SMEM((slots,), jnp.int32),
            pltpu.VMEM(queries.shape, BF16),
            pltpu.VMEM((PAD, head_dim), F32),
            pltpu.SemaphoreType.DMA((2,)),
        ],
        compiler_params=small,
        name="prep",
    )(lengths, queries)
    keys, table, local_out, local_lse = pl.pallas_call(
        functools.partial(local_kernel, scale2),
        out_shape=(
            pltpu.VMEM(key_cache.shape, BF16),
            jax.ShapeDtypeStruct((256,), jnp.int32),
            jax.ShapeDtypeStruct((slots, PAD, head_dim), F32),
            jax.ShapeDtypeStruct((slots, PAD, head_dim), F32),
        ),
        in_specs=[HBM] * 8,
        out_specs=(VMEM, SMEM, VMEM, VMEM),
        scratch_shapes=[
            pltpu.SMEM((slots,), jnp.int32),
            pltpu.SMEM((blocks,), jnp.int32),
            pltpu.SMEM((blocks,), jnp.int32),
            pltpu.VMEM(queries.shape, BF16),
            pltpu.VMEM(new_keys.shape, BF16),
            pltpu.VMEM(new_values.shape, BF16),
            pltpu.VMEM((slots, PAD, head_dim), F32),
            pltpu.VMEM((span, head_dim), BF16),
            pltpu.SemaphoreType.DMA((8,)),
        ],
        compiler_params=small,
        cost_estimate=pl.CostEstimate(
            flops=1 << 28, bytes_accessed=2 * key_cache.size * 2, transcendentals=1 << 18
        ),
        name="local",
    )(
        lengths, block_owner, block_number, queries, new_keys, new_values, key_cache, value_cache
    )
    column = exchange(message, axis_index_groups=along_z)
    far = exchange(jnp.broadcast_to(column[None], (4,) + column.shape), axis_index_groups=along_y)
    back = pl.pallas_call(
        functools.partial(far_kernel, chunk, scale2),
        out_shape=jax.ShapeDtypeStruct((devices, PAD, head_dim), BF16),
        in_specs=[SMEM, VMEM, VMEM, HBM],
        out_specs=VMEM,
        scratch_shapes=[
            pltpu.VMEM((blocks - 4, span, head_dim), BF16),
            pltpu.SemaphoreType.DMA((blocks - 4,)),
        ],
        compiler_params=small,
        name="far",
    )(table, far.reshape(devices, PAD, head_dim), in_vmem(keys), value_cache)
    back = back.reshape(4, 16, PAD, head_dim)
    row_got = exchange(back, axis_index_groups=along_y)
    onward = pl.pallas_call(
        stage_kernel,
        out_shape=jax.ShapeDtypeStruct((16, PAD, head_dim), BF16),
        in_specs=[VMEM],
        out_specs=VMEM,
        compiler_params=small,
        name="stage",
    )(row_got)
    got = exchange(onward, axis_index_groups=along_z)
    rows_out = pl.pallas_call(
        combine_kernel,
        out_shape=jax.ShapeDtypeStruct((8, 2, groups * head_dim), BF16),
        in_specs=[HBM, VMEM, VMEM, VMEM],
        out_specs=VMEM,
        scratch_shapes=[pltpu.SMEM((slots,), jnp.int32), pltpu.SemaphoreType.DMA((1,))],
        compiler_params=small,
        name="combine",
    )(lengths, got, local_out, local_lse)
    swapped = lax.all_to_all(rows_out, "tensor", split_axis=0, concat_axis=0, tiled=True)
    return jnp.transpose(swapped, (1, 0, 2)).reshape(2, 8 * groups * head_dim)


def solution(mesh):
    placed = (
        P("serve", None, "tensor", None),
        P("serve", None, "tensor", None),
        P("serve", None, "tensor", None),
        P("serve", None, "tensor", None),
        P("serve", None, "tensor", None),
        P("serve"),
        P("serve"),
        P("serve"),
    )
    return jax.shard_map(
        shards, mesh=mesh, in_specs=placed, out_specs=P(("serve", "tensor"), None), check_vma=False
    )
```

```python
import functools
import math

import jax
import jax.numpy as jnp
from jax import lax
from jax.experimental import pallas as pl
from jax.experimental.pallas import tpu as pltpu
from jax.sharding import PartitionSpec as P

neg_fill = -1e30
PAD = 32
F32 = jnp.float32
BF16 = jnp.bfloat16


def iota(shape, dim):
    return lax.broadcasted_iota(jnp.int32, shape, dim)


def column_first(device):
    return lax.bitwise_and(device, 3) * 16 + lax.shift_right_logical(device, 2)


def message_of(out, lse, rows):
    row = iota(out.shape, 0)
    high = lse.astype(BF16).astype(F32)
    rest = lse - high
    middle = rest.astype(BF16).astype(F32)
    low = rest - middle
    stats = jnp.where(
        row == rows,
        high,
        jnp.where(row == rows + 1, middle, jnp.where(row == rows + 2, low, 0.0)),
    )
    return jnp.where(row < rows, out, stats).astype(BF16)


def pad_rows(length, query, padded):
    groups, steps, head_dim = query.shape
    rows = groups * steps
    for g in range(groups):
        padded[g * steps : (g + 1) * steps, :] = query[g].astype(F32)
    row = iota((PAD - rows, head_dim), 0)
    high = lax.shift_right_logical(length, 6).astype(F32)
    low = lax.bitwise_and(length, 63).astype(F32)
    padded[rows:PAD, :] = jnp.where(row == 0, high, jnp.where(row == 1, low, 0.0))


def fetch(pairs, sems):
    copies = [
        pltpu.make_async_copy(source, target, sems.at[i])
        for i, (source, target) in enumerate(pairs)
    ]
    for copy in copies:
        copy.start()
    return copies


def prep_kernel(lengths_hbm, queries_hbm, message, lengths, queries, padded, sems):
    copies = fetch(((lengths_hbm, lengths), (queries_hbm, queries)), sems)
    for copy in copies:
        copy.wait()
    long_slot, length = jnp.int32(0), lengths[0]
    for slot in range(1, queries.shape[0]):
        is_long = lengths[slot] > 256
        long_slot = jnp.where(is_long, slot, long_slot)
        length = jnp.where(is_long, lengths[slot], length)
    pad_rows(length, queries.at[long_slot], padded)
    message[...] = jnp.broadcast_to(padded[...].astype(BF16)[None], message.shape)


def attend(query, limit, keys, values, scale2):
    score = lax.dot_general(query, keys, (((1,), (1,)), ((), ())), preferred_element_type=F32)
    score = jnp.where(iota(score.shape, 1).astype(F32) < limit, score, neg_fill)
    top = jnp.max(score, axis=1, keepdims=True)
    weights = jnp.exp2((score - top) * scale2).astype(BF16)
    total = jnp.sum(weights.astype(F32), axis=1, keepdims=True)
    out = lax.dot_general(weights, values, (((1,), (0,)), ((), ())), preferred_element_type=F32)
    return out / total, top * scale2 + jnp.log2(total)


def local_kernel(
    scale2, lengths_hbm, owners_hbm, numbers_hbm, queries_hbm, new_keys_hbm, new_values_hbm,
    key_cache, value_cache,
    keys, table, local_out, local_lse,
    lengths, owners, numbers, queries, new_keys, new_values, padded, one_value, sems,
):
    blocks, span, head_dim = keys.shape
    slots, steps, _ = new_keys.shape
    me = lax.axis_index("serve")
    small = ((lengths_hbm, lengths), (owners_hbm, owners), (numbers_hbm, numbers),
             (queries_hbm, queries), (new_keys_hbm, new_keys), (new_values_hbm, new_values))
    copies = fetch(small + ((key_cache, keys),), sems)
    for copy in copies[: len(small)]:
        copy.wait()

    def place(p, counts):
        far_count, near_count = counts
        device = lax.shift_right_logical(owners[p], 2)
        near = device == me
        at = jnp.where(near, blocks - 1 - near_count, far_count)
        table[at] = p
        table[64 + at] = jnp.where(near, lax.bitwise_and(owners[p], 3), column_first(device))
        table[128 + at] = numbers[p] * span
        one = near.astype(jnp.int32)
        return far_count + 1 - one, near_count + one

    far_count, near_count = lax.fori_loop(0, blocks, place, (jnp.int32(0), jnp.int32(0)))
    table[192] = far_count

    for slot in range(slots):
        pad_rows(lengths[slot], queries.at[slot], padded.at[slot])
    all_rows = padded[...].astype(BF16).reshape(slots * PAD, head_dim)
    nk = new_keys[...].astype(F32).reshape(slots * steps, head_dim).astype(BF16)
    nv = new_values[...].astype(F32).reshape(slots * steps, head_dim).astype(BF16)
    scores = lax.dot_general(all_rows, nk, (((1,), (1,)), ((), ())), preferred_element_type=F32)
    r2, c2 = iota(scores.shape, 0), iota(scores.shape, 1)
    seen = jnp.logical_and(r2 // PAD == c2 // steps, c2 % steps <= r2 % steps)
    scores = jnp.where(seen, scores, neg_fill)
    top = jnp.max(scores, axis=1, keepdims=True)
    weights = jnp.where(seen, jnp.exp2((scores - top) * scale2), 0.0).astype(BF16)
    total = jnp.sum(weights.astype(F32), axis=1, keepdims=True)
    out = lax.dot_general(weights, nv, (((1,), (0,)), ((), ())), preferred_element_type=F32)
    lse = jnp.broadcast_to(top * scale2 + jnp.log2(total), out.shape)
    local_out[...] = (out / total).reshape(local_out.shape)
    local_lse[...] = lse.reshape(local_lse.shape)
    for copy in copies[len(small) :]:
        copy.wait()

    def merge(k, carry):
        p, slot = table[blocks - 1 - k], table[64 + blocks - 1 - k]
        copy = pltpu.make_async_copy(value_cache.at[p], one_value, sems.at[7])
        copy.start()
        copy.wait()
        limit = (lengths[slot] - table[128 + blocks - 1 - k]).astype(F32)
        new_out, new = attend(padded[slot].astype(BF16), limit, keys[p], one_value[...], scale2)
        old, new = local_lse[slot], jnp.broadcast_to(new, new_out.shape)
        overall = jnp.maximum(old, new)
        a, b = jnp.exp2(old - overall), jnp.exp2(new - overall)
        total = a + b
        local_out[slot] = (a * local_out[slot] + b * new_out) / total
        local_lse[slot] = overall + jnp.log2(total)
        return carry

    lax.fori_loop(0, near_count, merge, 0)


def far_kernel(chunk, scale2, table, far, keys, value_cache, back, values, sems):
    blocks, span, head_dim = keys.shape
    rows = 28
    count = blocks - 4
    me = lax.axis_index("serve")
    far_count = table[192]
    parts = [pl.ds(k * (blocks // 4), blocks // 4) for k in range(4)]
    copies = fetch([(value_cache.at[part], values.at[part]) for part in parts], sems)
    row, lane = iota((PAD, head_dim), 0), iota((PAD, head_dim), 1)
    offset = lax.bitwise_and(me, 3) * PAD
    diagonal = jnp.logical_and(lane == offset + row, row < rows)
    in_span = jnp.logical_and(lane >= offset, lane < offset + rows)
    empty = jnp.where(jnp.logical_and(row == rows, in_span), neg_fill, 0.0).astype(BF16)
    back[...] = jnp.broadcast_to(empty[None], back.shape)
    unused = column_first(me)
    position = iota((PAD, span), 1).astype(F32)
    for c in range(count // chunk):
        ids = [table[k] for k in range(c * chunk, (c + 1) * chunk)]
        places = [
            jnp.where(k < far_count, table[64 + k], unused)
            for k in range(c * chunk, (c + 1) * chunk)
        ]
        raw = []
        for k in range(chunk):
            query = far[places[k]]
            lens = query[rows : rows + 2, :].astype(F32)
            length = lens[0:1, 0:1] * 64.0 + lens[1:2, 0:1]
            score = lax.dot_general(
                query, keys[ids[k]], (((1,), (1,)), ((), ())), preferred_element_type=F32
            )
            limit = length - table[128 + c * chunk + k].astype(F32)
            raw.append(jnp.where(position < limit, score, neg_fill))
        raw = jnp.concatenate(raw, axis=0)
        top = jnp.max(raw, axis=1, keepdims=True)
        weights = jnp.exp2((raw - top) * scale2).astype(BF16)
        total = jnp.sum(weights.astype(F32), axis=1, keepdims=True)
        lse = top * scale2 + jnp.log2(total)
        inverse = 1.0 / total
        if c == 0:
            for copy in copies:
                copy.wait()
        for k in range(chunk):
            part = slice(k * PAD, (k + 1) * PAD)
            out = lax.dot_general(
                weights[part], values[ids[k]], (((1,), (0,)), ((), ())),
                preferred_element_type=F32,
            )
            flat = jnp.sum(jnp.where(diagonal, lse[part], 0.0), axis=0, keepdims=True)
            back[places[k]] = message_of(out * inverse[part], flat, rows)
    back[unused] = empty


def four_fold(x, op):
    x = op(x, pltpu.roll(x, 2 * PAD, 1))
    return op(x, pltpu.roll(x, PAD, 1))


def stage_kernel(got, onward):
    sources, many, _, head_dim = got.shape
    rows = 28
    me = lax.axis_index("serve")
    depth = sources * many * PAD
    flat = got[...].reshape(depth, head_dim)
    g2, k2 = iota((many, depth), 0), iota((many, depth), 1)
    in_row = jnp.logical_and(k2 % PAD >= rows, k2 % PAD < rows + 3)
    pick = jnp.logical_and((k2 // PAD) % many == g2, in_row)
    lse = lax.dot_general(
        jnp.where(pick, 1.0, 0.0).astype(BF16), flat, (((1,), (0,)), ((), ())),
        preferred_element_type=F32,
    )
    top = four_fold(lse, jnp.maximum)
    weight = jnp.exp2(lse - top)
    total = four_fold(weight, jnp.add)
    weight = weight / total
    row, lane = iota((PAD, head_dim), 0), iota((PAD, head_dim), 1)
    same = jnp.logical_and(lane % PAD == row, row < rows)
    offset = lax.bitwise_and(lax.shift_right_logical(me, 2), 3) * PAD
    lane = iota((many, head_dim), 1)
    in_span = jnp.logical_and(lane >= offset, lane < offset + rows)
    lse = jnp.where(in_span, top + jnp.log2(total), 0.0)
    for m in range(many):
        spread = jnp.where(same, weight[m : m + 1], 0.0)
        high = spread.astype(BF16)
        low = (spread - high.astype(F32)).astype(BF16)
        both = jnp.concatenate([high, low], axis=0)
        block = got[:, m].reshape(sources * PAD, head_dim)
        out = lax.dot_general(both, block, (((1,), (0,)), ((), ())), preferred_element_type=F32)
        onward[m] = message_of(out[:PAD] + out[PAD:], lse[m : m + 1], rows)


def combine_kernel(lengths_hbm, got, local_out, local_lse, result, lengths, sems):
    copies = fetch(((lengths_hbm, lengths),), sems)
    devices, _, head_dim = got.shape
    slots = local_out.shape[0]
    steps, groups, rows = 4, 7, 28
    depth = devices * PAD
    many = devices // 4
    flat = got[...].reshape(depth, head_dim)
    g2, k2 = iota((many, depth), 0), iota((many, depth), 1)
    in_row = jnp.logical_and(k2 % PAD >= rows, k2 % PAD < rows + 3)
    pick = jnp.logical_and(k2 // (4 * PAD) == g2, in_row)
    lse = lax.dot_general(
        jnp.where(pick, 1.0, 0.0).astype(BF16), flat, (((1,), (0,)), ((), ())),
        preferred_element_type=F32,
    )
    top = jnp.max(lse, axis=0, keepdims=True)
    top = jnp.broadcast_to(top, (8, head_dim))
    top = four_fold(top, jnp.maximum)
    weight = jnp.exp2(lse - top[0:1])
    row, lane = iota((PAD, head_dim), 0), iota((PAD, head_dim), 1)
    same = jnp.logical_and(lane % PAD == row, row < rows)
    spread = jnp.concatenate(
        [jnp.where(same, weight[g : g + 1], 0.0) for g in range(many)], axis=1
    )
    high = spread.astype(BF16)
    low = (spread - high.astype(F32)).astype(BF16)
    both = jnp.concatenate([high, low], axis=0)
    out = lax.dot_general(both, flat, (((1,), (0,)), ((), ())), preferred_element_type=F32)
    out = out[:PAD] + out[PAD:]
    total = jnp.sum(spread, axis=1, keepdims=True)
    total = jnp.where(row[:, 0:1] < rows, total, 1.0)
    first = jnp.logical_and(lane == row, row < rows)
    column = jnp.sum(jnp.where(first, top[0:1], 0.0), axis=1, keepdims=True)
    far_out = out / total
    far_lse = jnp.broadcast_to(column + jnp.log2(total), far_out.shape)
    copies[0].wait()
    for slot in range(slots):
        far_here = jnp.where(lengths[slot] > 256, far_lse, neg_fill)
        near = local_lse[slot]
        overall = jnp.maximum(far_here, near)
        a, b = jnp.exp2(far_here - overall), jnp.exp2(near - overall)
        final = ((a * far_out + b * local_out[slot]) / (a + b)).astype(BF16)
        for g in range(groups):
            columns = slice(g * head_dim, (g + 1) * head_dim)
            for half in range(2):
                start = g * steps + half * 2
                result[slot * 2 + half, :, columns] = final[start : start + 2]


VMEM = pl.BlockSpec(memory_space=pltpu.VMEM)
SMEM = pl.BlockSpec(memory_space=pltpu.SMEM)
HBM = pl.BlockSpec(memory_space=pltpu.HBM)


def shards(
    queries, new_keys, new_values, key_cache, value_cache, lengths, block_owner, block_number
):
    slots, steps, groups, head_dim = queries.shape
    blocks, span = key_cache.shape[:2]
    devices = lax.axis_size("serve")
    chunk = 32
    scale2 = head_dim**-0.5 * math.log2(math.e)
    queries = jnp.transpose(queries, (0, 2, 1, 3))
    new_keys = new_keys.reshape(slots, steps, head_dim)
    new_values = new_values.reshape(slots, steps, head_dim)
    key_cache = key_cache.reshape(blocks, span, head_dim)
    value_cache = value_cache.reshape(blocks, span, head_dim)

    along_z = [[4 * z + y for z in range(16)] for y in range(4)]
    along_y = [[4 * z + y for y in range(4)] for z in range(16)]
    exchange = functools.partial(
        lax.all_to_all, axis_name="serve", split_axis=0, concat_axis=0, tiled=True
    )
    in_hbm = functools.partial(pltpu.with_memory_space_constraint, memory_space=pltpu.HBM)
    in_vmem = functools.partial(pltpu.with_memory_space_constraint, memory_space=pltpu.VMEM)
    queries, new_keys, new_values, key_cache, value_cache, lengths, block_owner, block_number = map(
        in_hbm,
        (queries, new_keys, new_values, key_cache, value_cache, lengths, block_owner, block_number),
    )
    small = pltpu.CompilerParams(vmem_limit_bytes=8 << 20)
    message = pl.pallas_call(
        prep_kernel,
        out_shape=jax.ShapeDtypeStruct((16, PAD, head_dim), BF16),
        in_specs=[HBM, HBM],
        out_specs=VMEM,
        scratch_shapes=[
            pltpu.SMEM((slots,), jnp.int32),
            pltpu.VMEM(queries.shape, BF16),
            pltpu.VMEM((PAD, head_dim), F32),
            pltpu.SemaphoreType.DMA((2,)),
        ],
        compiler_params=small,
        name="prep",
    )(lengths, queries)
    keys, table, local_out, local_lse = pl.pallas_call(
        functools.partial(local_kernel, scale2),
        out_shape=(
            pltpu.VMEM(key_cache.shape, BF16),
            jax.ShapeDtypeStruct((256,), jnp.int32),
            jax.ShapeDtypeStruct((slots, PAD, head_dim), F32),
            jax.ShapeDtypeStruct((slots, PAD, head_dim), F32),
        ),
        in_specs=[HBM] * 8,
        out_specs=(VMEM, SMEM, VMEM, VMEM),
        scratch_shapes=[
            pltpu.SMEM((slots,), jnp.int32),
            pltpu.SMEM((blocks,), jnp.int32),
            pltpu.SMEM((blocks,), jnp.int32),
            pltpu.VMEM(queries.shape, BF16),
            pltpu.VMEM(new_keys.shape, BF16),
            pltpu.VMEM(new_values.shape, BF16),
            pltpu.VMEM((slots, PAD, head_dim), F32),
            pltpu.VMEM((span, head_dim), BF16),
            pltpu.SemaphoreType.DMA((8,)),
        ],
        compiler_params=small,
        cost_estimate=pl.CostEstimate(
            flops=1 << 28, bytes_accessed=2 * key_cache.size * 2, transcendentals=1 << 18
        ),
        name="local",
    )(
        lengths, block_owner, block_number, queries, new_keys, new_values, key_cache, value_cache
    )
    column = exchange(message, axis_index_groups=along_z)
    column, keys, table = lax.optimization_barrier((column, keys, table))
    far = exchange(jnp.broadcast_to(column[None], (4,) + column.shape), axis_index_groups=along_y)
    back = pl.pallas_call(
        functools.partial(far_kernel, chunk, scale2),
        out_shape=jax.ShapeDtypeStruct((devices, PAD, head_dim), BF16),
        in_specs=[SMEM, VMEM, VMEM, HBM],
        out_specs=VMEM,
        scratch_shapes=[
            pltpu.VMEM((blocks, span, head_dim), BF16),
            pltpu.SemaphoreType.DMA((4,)),
        ],
        compiler_params=small,
        name="far",
    )(table, far.reshape(devices, PAD, head_dim), in_vmem(keys), value_cache)
    back = back.reshape(4, 16, PAD, head_dim)
    row_got = exchange(back, axis_index_groups=along_y)
    onward = pl.pallas_call(
        stage_kernel,
        out_shape=jax.ShapeDtypeStruct((16, PAD, head_dim), BF16),
        in_specs=[VMEM],
        out_specs=VMEM,
        compiler_params=small,
        name="stage",
    )(row_got)
    got = exchange(onward, axis_index_groups=along_z)
    rows_out = pl.pallas_call(
        combine_kernel,
        out_shape=jax.ShapeDtypeStruct((8, 2, groups * head_dim), BF16),
        in_specs=[HBM, VMEM, VMEM, VMEM],
        out_specs=VMEM,
        scratch_shapes=[pltpu.SMEM((slots,), jnp.int32), pltpu.SemaphoreType.DMA((1,))],
        compiler_params=small,
        name="combine",
    )(lengths, got, local_out, local_lse)
    swapped = lax.all_to_all(rows_out, "tensor", split_axis=0, concat_axis=0, tiled=True)
    return jnp.transpose(swapped, (1, 0, 2)).reshape(2, 8 * groups * head_dim)


def solution(mesh):
    placed = (
        P("serve", None, "tensor", None),
        P("serve", None, "tensor", None),
        P("serve", None, "tensor", None),
        P("serve", None, "tensor", None),
        P("serve", None, "tensor", None),
        P("serve"),
        P("serve"),
        P("serve"),
    )
    return jax.shard_map(
        shards, mesh=mesh, in_specs=placed, out_specs=P(("serve", "tensor"), None), check_vma=False
    )
```

```python
import functools
import math

import jax
import jax.numpy as jnp
from jax import lax
from jax.experimental import pallas as pl
from jax.experimental.pallas import tpu as pltpu
from jax.sharding import PartitionSpec as P

neg_fill = -1e30
PAD = 32
F32 = jnp.float32
BF16 = jnp.bfloat16


def iota(shape, dim):
    return lax.broadcasted_iota(jnp.int32, shape, dim)


def column_first(device):
    return lax.bitwise_and(device, 3) * 16 + lax.shift_right_logical(device, 2)


def message_of(out, lse, rows):
    row = iota(out.shape, 0)
    high = lse.astype(BF16).astype(F32)
    rest = lse - high
    middle = rest.astype(BF16).astype(F32)
    low = rest - middle
    stats = jnp.where(
        row == rows,
        high,
        jnp.where(row == rows + 1, middle, jnp.where(row == rows + 2, low, 0.0)),
    )
    return jnp.where(row < rows, out, stats).astype(BF16)


def pad_rows(length, query, padded):
    groups, steps, head_dim = query.shape
    rows = groups * steps
    for g in range(groups):
        padded[g * steps : (g + 1) * steps, :] = query[g].astype(F32)
    row = iota((PAD - rows, head_dim), 0)
    high = lax.shift_right_logical(length, 6).astype(F32)
    low = lax.bitwise_and(length, 63).astype(F32)
    padded[rows:PAD, :] = jnp.where(row == 0, high, jnp.where(row == 1, low, 0.0))


def fetch(pairs, sems):
    copies = [
        pltpu.make_async_copy(source, target, sems.at[i])
        for i, (source, target) in enumerate(pairs)
    ]
    for copy in copies:
        copy.start()
    return copies


def prep_kernel(lengths_hbm, queries_hbm, message, lengths, queries, padded, sems):
    copies = fetch(((lengths_hbm, lengths), (queries_hbm, queries)), sems)
    for copy in copies:
        copy.wait()
    long_slot, length = jnp.int32(0), lengths[0]
    for slot in range(1, queries.shape[0]):
        is_long = lengths[slot] > 256
        long_slot = jnp.where(is_long, slot, long_slot)
        length = jnp.where(is_long, lengths[slot], length)
    pad_rows(length, queries.at[long_slot], padded)
    message[...] = jnp.broadcast_to(padded[...].astype(BF16)[None], message.shape)


def attend(query, limit, keys, values, scale2):
    score = lax.dot_general(query, keys, (((1,), (1,)), ((), ())), preferred_element_type=F32)
    score = jnp.where(iota(score.shape, 1).astype(F32) < limit, score, neg_fill)
    top = jnp.max(score, axis=1, keepdims=True)
    weights = jnp.exp2((score - top) * scale2).astype(BF16)
    total = jnp.sum(weights.astype(F32), axis=1, keepdims=True)
    out = lax.dot_general(weights, values, (((1,), (0,)), ((), ())), preferred_element_type=F32)
    return out / total, top * scale2 + jnp.log2(total)


def local_kernel(
    scale2, lengths_hbm, owners_hbm, numbers_hbm, queries_hbm, new_keys_hbm, new_values_hbm,
    key_cache, value_cache,
    keys, table, local_out, local_lse,
    lengths, owners, numbers, queries, new_keys, new_values, padded, near_values, sems,
):
    blocks, span, head_dim = keys.shape
    slots, steps, _ = new_keys.shape
    me = lax.axis_index("serve")
    small = ((lengths_hbm, lengths), (owners_hbm, owners), (numbers_hbm, numbers),
             (queries_hbm, queries), (new_keys_hbm, new_keys), (new_values_hbm, new_values))
    all_keys, *copies = fetch(((key_cache, keys),) + small, sems)
    for copy in copies:
        copy.wait()

    far_count, near_count = jnp.int32(0), jnp.int32(0)
    for p in range(blocks):
        owner, number = owners[p], numbers[p]
        device = lax.shift_right_logical(owner, 2)
        near = device == me
        at = jnp.where(near, blocks - 1 - near_count, far_count)
        table[at] = p
        table[64 + at] = jnp.where(near, lax.bitwise_and(owner, 3), column_first(device))
        table[128 + at] = number * span
        one = near.astype(jnp.int32)
        far_count, near_count = far_count + 1 - one, near_count + one
    table[192] = far_count
    own_values = fetch(
        [(value_cache.at[table[blocks - 1 - k]], near_values.at[k]) for k in range(slots)],
        sems.at[pl.ds(8, slots)],
    )

    for slot in range(slots):
        pad_rows(lengths[slot], queries.at[slot], padded.at[slot])
    all_rows = padded[...].astype(BF16).reshape(slots * PAD, head_dim)
    nk = new_keys[...].astype(F32).reshape(slots * steps, head_dim).astype(BF16)
    nv = new_values[...].astype(F32).reshape(slots * steps, head_dim).astype(BF16)
    scores = lax.dot_general(all_rows, nk, (((1,), (1,)), ((), ())), preferred_element_type=F32)
    r2, c2 = iota(scores.shape, 0), iota(scores.shape, 1)
    seen = jnp.logical_and(r2 // PAD == c2 // steps, c2 % steps <= r2 % steps)
    scores = jnp.where(seen, scores, neg_fill)
    top = jnp.max(scores, axis=1, keepdims=True)
    weights = jnp.where(seen, jnp.exp2((scores - top) * scale2), 0.0).astype(BF16)
    total = jnp.sum(weights.astype(F32), axis=1, keepdims=True)
    out = lax.dot_general(weights, nv, (((1,), (0,)), ((), ())), preferred_element_type=F32)
    lse = jnp.broadcast_to(top * scale2 + jnp.log2(total), out.shape)
    local_out[...] = (out / total).reshape(local_out.shape)
    local_lse[...] = lse.reshape(local_lse.shape)

    def merge(slot, new_out, new):
        old = local_lse[slot]
        overall = jnp.maximum(old, new)
        a, b = jnp.exp2(old - overall), jnp.exp2(new - overall)
        total = a + b
        local_out[slot] = (a * local_out[slot] + b * new_out) / total
        local_lse[slot] = overall + jnp.log2(total)

    all_keys.wait()
    for copy in own_values:
        copy.wait()
    ats = [blocks - 1 - k for k in range(slots)]
    parts = []
    for k, at in enumerate(ats):
        slot = table[64 + at]
        limit = (lengths[slot] - table[128 + at]).astype(F32)
        parts.append(
            attend(padded[slot].astype(BF16), limit, keys[table[at]], near_values[k], scale2)
        )
    for at, (new_out, new) in zip(ats, parts):
        merge(table[64 + at], new_out, jnp.broadcast_to(new, new_out.shape))

    def more(k, carry):
        at = blocks - 1 - k
        slot = table[64 + at]
        copy = pltpu.make_async_copy(value_cache.at[table[at]], near_values.at[0], sems.at[8])
        copy.start()
        copy.wait()
        limit = (lengths[slot] - table[128 + at]).astype(F32)
        new_out, new = attend(
            padded[slot].astype(BF16), limit, keys[table[at]], near_values[0], scale2
        )
        merge(slot, new_out, jnp.broadcast_to(new, new_out.shape))
        return carry

    lax.fori_loop(slots, near_count, more, 0)


def far_kernel(chunk, scale2, table, far, keys, value_cache, back, values, sems):
    blocks, span, head_dim = keys.shape
    rows = 28
    count = blocks - 4
    me = lax.axis_index("serve")
    far_count = table[192]
    parts = [pl.ds(k * (blocks // 4), blocks // 4) for k in range(4)]
    copies = fetch([(value_cache.at[part], values.at[part]) for part in parts], sems)
    row, lane = iota((PAD, head_dim), 0), iota((PAD, head_dim), 1)
    offset = lax.bitwise_and(me, 3) * PAD
    diagonal = jnp.logical_and(lane == offset + row, row < rows)
    in_span = jnp.logical_and(lane >= offset, lane < offset + rows)
    empty = jnp.where(jnp.logical_and(row == rows, in_span), neg_fill, 0.0).astype(BF16)
    back[...] = jnp.broadcast_to(empty[None], back.shape)
    unused = column_first(me)
    position = iota((PAD, span), 1).astype(F32)
    for c in range(count // chunk):
        ids = [table[k] for k in range(c * chunk, (c + 1) * chunk)]
        places = [
            jnp.where(k < far_count, table[64 + k], unused)
            for k in range(c * chunk, (c + 1) * chunk)
        ]
        raw = []
        for k in range(chunk):
            query = far[places[k]]
            lens = query[rows : rows + 2, :].astype(F32)
            length = lens[0:1, 0:1] * 64.0 + lens[1:2, 0:1]
            score = lax.dot_general(
                query, keys[ids[k]], (((1,), (1,)), ((), ())), preferred_element_type=F32
            )
            limit = length - table[128 + c * chunk + k].astype(F32)
            raw.append(jnp.where(position < limit, score, neg_fill))
        raw = jnp.concatenate(raw, axis=0)
        top = jnp.max(raw, axis=1, keepdims=True)
        weights = jnp.exp2((raw - top) * scale2).astype(BF16)
        total = jnp.sum(weights.astype(F32), axis=1, keepdims=True)
        lse = top * scale2 + jnp.log2(total)
        inverse = 1.0 / total
        if c == 0:
            for copy in copies:
                copy.wait()
        for k in range(chunk):
            part = slice(k * PAD, (k + 1) * PAD)
            out = lax.dot_general(
                weights[part], values[ids[k]], (((1,), (0,)), ((), ())),
                preferred_element_type=F32,
            )
            flat = jnp.sum(jnp.where(diagonal, lse[part], 0.0), axis=0, keepdims=True)
            back[places[k]] = message_of(out * inverse[part], flat, rows)
    back[unused] = empty


def four_fold(x, op):
    x = op(x, pltpu.roll(x, 2 * PAD, 1))
    return op(x, pltpu.roll(x, PAD, 1))


def stage_kernel(got, onward):
    sources, many, _, head_dim = got.shape
    rows = 28
    me = lax.axis_index("serve")
    depth = sources * many * PAD
    flat = got[...].reshape(depth, head_dim)
    g2, k2 = iota((many, depth), 0), iota((many, depth), 1)
    in_row = jnp.logical_and(k2 % PAD >= rows, k2 % PAD < rows + 3)
    pick = jnp.logical_and((k2 // PAD) % many == g2, in_row)
    lse = lax.dot_general(
        jnp.where(pick, 1.0, 0.0).astype(BF16), flat, (((1,), (0,)), ((), ())),
        preferred_element_type=F32,
    )
    top = four_fold(lse, jnp.maximum)
    weight = jnp.exp2(lse - top)
    total = four_fold(weight, jnp.add)
    weight = weight / total
    row, lane = iota((PAD, head_dim), 0), iota((PAD, head_dim), 1)
    same = jnp.logical_and(lane % PAD == row, row < rows)
    offset = lax.bitwise_and(lax.shift_right_logical(me, 2), 3) * PAD
    lane = iota((many, head_dim), 1)
    in_span = jnp.logical_and(lane >= offset, lane < offset + rows)
    lse = jnp.where(in_span, top + jnp.log2(total), 0.0)
    for m in range(many):
        spread = jnp.where(same, weight[m : m + 1], 0.0)
        high = spread.astype(BF16)
        low = (spread - high.astype(F32)).astype(BF16)
        both = jnp.concatenate([high, low], axis=0)
        block = got[:, m].reshape(sources * PAD, head_dim)
        out = lax.dot_general(both, block, (((1,), (0,)), ((), ())), preferred_element_type=F32)
        onward[m] = message_of(out[:PAD] + out[PAD:], lse[m : m + 1], rows)


def combine_kernel(lengths_hbm, got, local_out, local_lse, result, lengths, sems):
    copies = fetch(((lengths_hbm, lengths),), sems)
    devices, _, head_dim = got.shape
    slots = local_out.shape[0]
    steps, groups, rows = 4, 7, 28
    depth = devices * PAD
    many = devices // 4
    flat = got[...].reshape(depth, head_dim)
    g2, k2 = iota((many, depth), 0), iota((many, depth), 1)
    in_row = jnp.logical_and(k2 % PAD >= rows, k2 % PAD < rows + 3)
    pick = jnp.logical_and(k2 // (4 * PAD) == g2, in_row)
    lse = lax.dot_general(
        jnp.where(pick, 1.0, 0.0).astype(BF16), flat, (((1,), (0,)), ((), ())),
        preferred_element_type=F32,
    )
    top = jnp.max(lse, axis=0, keepdims=True)
    top = jnp.broadcast_to(top, (8, head_dim))
    top = four_fold(top, jnp.maximum)
    weight = jnp.exp2(lse - top[0:1])
    row, lane = iota((PAD, head_dim), 0), iota((PAD, head_dim), 1)
    same = jnp.logical_and(lane % PAD == row, row < rows)
    spread = jnp.concatenate(
        [jnp.where(same, weight[g : g + 1], 0.0) for g in range(many)], axis=1
    )
    high = spread.astype(BF16)
    low = (spread - high.astype(F32)).astype(BF16)
    both = jnp.concatenate([high, low], axis=0)
    out = lax.dot_general(both, flat, (((1,), (0,)), ((), ())), preferred_element_type=F32)
    out = out[:PAD] + out[PAD:]
    total = jnp.sum(spread, axis=1, keepdims=True)
    total = jnp.where(row[:, 0:1] < rows, total, 1.0)
    first = jnp.logical_and(lane == row, row < rows)
    column = jnp.sum(jnp.where(first, top[0:1], 0.0), axis=1, keepdims=True)
    far_out = out / total
    far_lse = jnp.broadcast_to(column + jnp.log2(total), far_out.shape)
    copies[0].wait()
    for slot in range(slots):
        far_here = jnp.where(lengths[slot] > 256, far_lse, neg_fill)
        near = local_lse[slot]
        overall = jnp.maximum(far_here, near)
        a, b = jnp.exp2(far_here - overall), jnp.exp2(near - overall)
        final = ((a * far_out + b * local_out[slot]) / (a + b)).astype(BF16)
        for g in range(groups):
            columns = slice(g * head_dim, (g + 1) * head_dim)
            for half in range(2):
                start = g * steps + half * 2
                result[slot * 2 + half, :, columns] = final[start : start + 2]


VMEM = pl.BlockSpec(memory_space=pltpu.VMEM)
SMEM = pl.BlockSpec(memory_space=pltpu.SMEM)
HBM = pl.BlockSpec(memory_space=pltpu.HBM)


def shards(
    queries, new_keys, new_values, key_cache, value_cache, lengths, block_owner, block_number
):
    slots, steps, groups, head_dim = queries.shape
    blocks, span = key_cache.shape[:2]
    devices = lax.axis_size("serve")
    chunk = 32
    scale2 = head_dim**-0.5 * math.log2(math.e)
    queries = jnp.transpose(queries, (0, 2, 1, 3))
    new_keys = new_keys.reshape(slots, steps, head_dim)
    new_values = new_values.reshape(slots, steps, head_dim)
    key_cache = key_cache.reshape(blocks, span, head_dim)
    value_cache = value_cache.reshape(blocks, span, head_dim)

    along_z = [[4 * z + y for z in range(16)] for y in range(4)]
    along_y = [[4 * z + y for y in range(4)] for z in range(16)]
    exchange = functools.partial(
        lax.all_to_all, axis_name="serve", split_axis=0, concat_axis=0, tiled=True
    )
    in_hbm = functools.partial(pltpu.with_memory_space_constraint, memory_space=pltpu.HBM)
    in_vmem = functools.partial(pltpu.with_memory_space_constraint, memory_space=pltpu.VMEM)
    queries, new_keys, new_values, key_cache, value_cache, lengths, block_owner, block_number = map(
        in_hbm,
        (queries, new_keys, new_values, key_cache, value_cache, lengths, block_owner, block_number),
    )
    small = pltpu.CompilerParams(vmem_limit_bytes=8 << 20)
    message = pl.pallas_call(
        prep_kernel,
        out_shape=jax.ShapeDtypeStruct((16, PAD, head_dim), BF16),
        in_specs=[HBM, HBM],
        out_specs=VMEM,
        scratch_shapes=[
            pltpu.SMEM((slots,), jnp.int32),
            pltpu.VMEM(queries.shape, BF16),
            pltpu.VMEM((PAD, head_dim), F32),
            pltpu.SemaphoreType.DMA((2,)),
        ],
        compiler_params=small,
        name="prep",
    )(lengths, queries)
    keys, table, local_out, local_lse = pl.pallas_call(
        functools.partial(local_kernel, scale2),
        out_shape=(
            pltpu.VMEM(key_cache.shape, BF16),
            jax.ShapeDtypeStruct((256,), jnp.int32),
            jax.ShapeDtypeStruct((slots, PAD, head_dim), F32),
            jax.ShapeDtypeStruct((slots, PAD, head_dim), F32),
        ),
        in_specs=[HBM] * 8,
        out_specs=(VMEM, SMEM, VMEM, VMEM),
        scratch_shapes=[
            pltpu.SMEM((slots,), jnp.int32),
            pltpu.SMEM((blocks,), jnp.int32),
            pltpu.SMEM((blocks,), jnp.int32),
            pltpu.VMEM(queries.shape, BF16),
            pltpu.VMEM(new_keys.shape, BF16),
            pltpu.VMEM(new_values.shape, BF16),
            pltpu.VMEM((slots, PAD, head_dim), F32),
            pltpu.VMEM((slots, span, head_dim), BF16),
            pltpu.SemaphoreType.DMA((8 + slots,)),
        ],
        compiler_params=small,
        cost_estimate=pl.CostEstimate(
            flops=1 << 28, bytes_accessed=2 * key_cache.size * 2, transcendentals=1 << 18
        ),
        name="local",
    )(
        lengths, block_owner, block_number, queries, new_keys, new_values, key_cache, value_cache
    )
    column = exchange(message, axis_index_groups=along_z)
    column, keys, table = lax.optimization_barrier((column, keys, table))
    far = exchange(jnp.broadcast_to(column[None], (4,) + column.shape), axis_index_groups=along_y)
    back = pl.pallas_call(
        functools.partial(far_kernel, chunk, scale2),
        out_shape=jax.ShapeDtypeStruct((devices, PAD, head_dim), BF16),
        in_specs=[SMEM, VMEM, VMEM, HBM],
        out_specs=VMEM,
        scratch_shapes=[
            pltpu.VMEM((blocks, span, head_dim), BF16),
            pltpu.SemaphoreType.DMA((4,)),
        ],
        compiler_params=small,
        name="far",
    )(table, far.reshape(devices, PAD, head_dim), in_vmem(keys), value_cache)
    back = back.reshape(4, 16, PAD, head_dim)
    row_got = exchange(back, axis_index_groups=along_y)
    onward = pl.pallas_call(
        stage_kernel,
        out_shape=jax.ShapeDtypeStruct((16, PAD, head_dim), BF16),
        in_specs=[VMEM],
        out_specs=VMEM,
        compiler_params=small,
        name="stage",
    )(row_got)
    got = exchange(onward, axis_index_groups=along_z)
    rows_out = pl.pallas_call(
        combine_kernel,
        out_shape=jax.ShapeDtypeStruct((8, 2, groups * head_dim), BF16),
        in_specs=[HBM, VMEM, VMEM, VMEM],
        out_specs=VMEM,
        scratch_shapes=[pltpu.SMEM((slots,), jnp.int32), pltpu.SemaphoreType.DMA((1,))],
        compiler_params=small,
        name="combine",
    )(lengths, got, local_out, local_lse)
    swapped = lax.all_to_all(rows_out, "tensor", split_axis=0, concat_axis=0, tiled=True)
    return jnp.transpose(swapped, (1, 0, 2)).reshape(2, 8 * groups * head_dim)


def solution(mesh):
    placed = (
        P("serve", None, "tensor", None),
        P("serve", None, "tensor", None),
        P("serve", None, "tensor", None),
        P("serve", None, "tensor", None),
        P("serve", None, "tensor", None),
        P("serve"),
        P("serve"),
        P("serve"),
    )
    return jax.shard_map(
        shards, mesh=mesh, in_specs=placed, out_specs=P(("serve", "tensor"), None), check_vma=False
    )
```

```python
import functools
import math

import jax
import jax.numpy as jnp
from jax import lax
from jax.experimental import pallas as pl
from jax.experimental.pallas import tpu as pltpu
from jax.sharding import PartitionSpec as P

neg_fill = -1e30
PAD = 32
F32 = jnp.float32
BF16 = jnp.bfloat16


def iota(shape, dim):
    return lax.broadcasted_iota(jnp.int32, shape, dim)


def column_first(device):
    return lax.bitwise_and(device, 3) * 16 + lax.shift_right_logical(device, 2)


def message_of(out, lse, rows):
    row = iota(out.shape, 0)
    high = lse.astype(BF16).astype(F32)
    rest = lse - high
    middle = rest.astype(BF16).astype(F32)
    low = rest - middle
    stats = jnp.where(
        row == rows,
        high,
        jnp.where(row == rows + 1, middle, jnp.where(row == rows + 2, low, 0.0)),
    )
    return jnp.where(row < rows, out, stats).astype(BF16)


def pad_rows(length, query, padded):
    groups, steps, head_dim = query.shape
    rows = groups * steps
    for g in range(groups):
        padded[g * steps : (g + 1) * steps, :] = query[g].astype(F32)
    row = iota((PAD - rows, head_dim), 0)
    high = lax.shift_right_logical(length, 6).astype(F32)
    low = lax.bitwise_and(length, 63).astype(F32)
    padded[rows:PAD, :] = jnp.where(row == 0, high, jnp.where(row == 1, low, 0.0))


def fetch(pairs, sems):
    copies = [
        pltpu.make_async_copy(source, target, sems.at[i])
        for i, (source, target) in enumerate(pairs)
    ]
    for copy in copies:
        copy.start()
    return copies


def prep_kernel(lengths_hbm, queries_hbm, message, lengths, queries, padded, sems):
    copies = fetch(((lengths_hbm, lengths), (queries_hbm, queries)), sems)
    for copy in copies:
        copy.wait()
    long_slot, length = jnp.int32(0), lengths[0]
    for slot in range(1, queries.shape[0]):
        is_long = lengths[slot] > 256
        long_slot = jnp.where(is_long, slot, long_slot)
        length = jnp.where(is_long, lengths[slot], length)
    pad_rows(length, queries.at[long_slot], padded)
    message[...] = jnp.broadcast_to(padded[...].astype(BF16)[None], message.shape)


def attend(query, limit, keys, values, scale2):
    score = lax.dot_general(query, keys, (((1,), (1,)), ((), ())), preferred_element_type=F32)
    score = jnp.where(iota(score.shape, 1).astype(F32) < limit, score, neg_fill)
    top = jnp.max(score, axis=1, keepdims=True)
    weights = jnp.exp2((score - top) * scale2).astype(BF16)
    total = jnp.sum(weights.astype(F32), axis=1, keepdims=True)
    out = lax.dot_general(weights, values, (((1,), (0,)), ((), ())), preferred_element_type=F32)
    return out / total, top * scale2 + jnp.log2(total)


def local_kernel(
    scale2, lengths_hbm, owners_hbm, numbers_hbm, queries_hbm, new_keys_hbm, new_values_hbm,
    key_cache, value_cache,
    keys, table, local_out, local_lse,
    lengths, owners, numbers, queries, new_keys, new_values, padded, near_values, sems,
):
    blocks, span, head_dim = keys.shape
    slots, steps, _ = new_keys.shape
    me = lax.axis_index("serve")
    small = ((lengths_hbm, lengths), (owners_hbm, owners), (numbers_hbm, numbers),
             (queries_hbm, queries), (new_keys_hbm, new_keys), (new_values_hbm, new_values))
    all_keys, *copies = fetch(((key_cache, keys),) + small, sems)
    for copy in copies:
        copy.wait()

    far_count, near_count = jnp.int32(0), jnp.int32(0)
    for p in range(blocks):
        owner, number = owners[p], numbers[p]
        device = lax.shift_right_logical(owner, 2)
        near = device == me
        at = jnp.where(near, blocks - 1 - near_count, far_count)
        table[at] = p
        table[64 + at] = jnp.where(near, lax.bitwise_and(owner, 3), column_first(device))
        table[128 + at] = number * span
        one = near.astype(jnp.int32)
        far_count, near_count = far_count + 1 - one, near_count + one
    table[192] = far_count
    own_values = fetch(
        [(value_cache.at[table[blocks - 1 - k]], near_values.at[k]) for k in range(slots)],
        sems.at[pl.ds(8, slots)],
    )

    for slot in range(slots):
        pad_rows(lengths[slot], queries.at[slot], padded.at[slot])
    all_rows = padded[...].astype(BF16).reshape(slots * PAD, head_dim)
    nk = new_keys[...].astype(F32).reshape(slots * steps, head_dim).astype(BF16)
    nv = new_values[...].astype(F32).reshape(slots * steps, head_dim).astype(BF16)
    scores = lax.dot_general(all_rows, nk, (((1,), (1,)), ((), ())), preferred_element_type=F32)
    r2, c2 = iota(scores.shape, 0), iota(scores.shape, 1)
    seen = jnp.logical_and(r2 // PAD == c2 // steps, c2 % steps <= r2 % steps)
    scores = jnp.where(seen, scores, neg_fill)
    top = jnp.max(scores, axis=1, keepdims=True)
    weights = jnp.where(seen, jnp.exp2((scores - top) * scale2), 0.0).astype(BF16)
    total = jnp.sum(weights.astype(F32), axis=1, keepdims=True)
    out = lax.dot_general(weights, nv, (((1,), (0,)), ((), ())), preferred_element_type=F32)
    lse = jnp.broadcast_to(top * scale2 + jnp.log2(total), out.shape)
    local_out[...] = (out / total).reshape(local_out.shape)
    local_lse[...] = lse.reshape(local_lse.shape)

    def merge(slot, new_out, new):
        old = local_lse[slot]
        overall = jnp.maximum(old, new)
        a, b = jnp.exp2(old - overall), jnp.exp2(new - overall)
        total = a + b
        local_out[slot] = (a * local_out[slot] + b * new_out) / total
        local_lse[slot] = overall + jnp.log2(total)

    all_keys.wait()
    for copy in own_values:
        copy.wait()
    ats = [blocks - 1 - k for k in range(slots)]
    parts = []
    for k, at in enumerate(ats):
        slot = table[64 + at]
        limit = (lengths[slot] - table[128 + at]).astype(F32)
        parts.append(
            attend(padded[slot].astype(BF16), limit, keys[table[at]], near_values[k], scale2)
        )
    for at, (new_out, new) in zip(ats, parts):
        merge(table[64 + at], new_out, jnp.broadcast_to(new, new_out.shape))

    def more(k, carry):
        at = blocks - 1 - k
        slot = table[64 + at]
        copy = pltpu.make_async_copy(value_cache.at[table[at]], near_values.at[0], sems.at[8])
        copy.start()
        copy.wait()
        limit = (lengths[slot] - table[128 + at]).astype(F32)
        new_out, new = attend(
            padded[slot].astype(BF16), limit, keys[table[at]], near_values[0], scale2
        )
        merge(slot, new_out, jnp.broadcast_to(new, new_out.shape))
        return carry

    lax.fori_loop(slots, near_count, more, 0)


def far_kernel(chunk, scale2, table, far, keys, value_cache, back, values, sems):
    blocks, span, head_dim = keys.shape
    rows = 28
    count = blocks - 4
    me = lax.axis_index("serve")
    far_count = table[192]
    parts = [pl.ds(k * (blocks // 4), blocks // 4) for k in range(4)]
    copies = fetch([(value_cache.at[part], values.at[part]) for part in parts], sems)
    row, lane = iota((PAD, head_dim), 0), iota((PAD, head_dim), 1)
    offset = lax.bitwise_and(me, 3) * PAD
    diagonal = jnp.logical_and(lane == offset + row, row < rows)
    in_span = jnp.logical_and(lane >= offset, lane < offset + rows)
    empty = jnp.where(jnp.logical_and(row == rows, in_span), neg_fill, 0.0).astype(BF16)
    back[...] = jnp.broadcast_to(empty[None], back.shape)
    unused = column_first(me)
    position = iota((PAD, span), 1).astype(F32)
    for c in range(count // chunk):
        ids = [table[k] for k in range(c * chunk, (c + 1) * chunk)]
        places = [
            jnp.where(k < far_count, table[64 + k], unused)
            for k in range(c * chunk, (c + 1) * chunk)
        ]
        raw = []
        for k in range(chunk):
            query = far[places[k]]
            lens = query[rows : rows + 2, :].astype(F32)
            length = lens[0:1, 0:1] * 64.0 + lens[1:2, 0:1]
            score = lax.dot_general(
                query, keys[ids[k]], (((1,), (1,)), ((), ())), preferred_element_type=F32
            )
            limit = length - table[128 + c * chunk + k].astype(F32)
            raw.append(jnp.where(position < limit, score, neg_fill))
        raw = jnp.concatenate(raw, axis=0)
        top = jnp.max(raw, axis=1, keepdims=True)
        weights = jnp.exp2((raw - top) * scale2).astype(BF16)
        total = jnp.sum(weights.astype(F32), axis=1, keepdims=True)
        lse = top * scale2 + jnp.log2(total)
        inverse = 1.0 / total
        if c == 0:
            for copy in copies:
                copy.wait()
        for k in range(chunk):
            part = slice(k * PAD, (k + 1) * PAD)
            out = lax.dot_general(
                weights[part], values[ids[k]], (((1,), (0,)), ((), ())),
                preferred_element_type=F32,
            )
            flat = jnp.sum(jnp.where(diagonal, lse[part], 0.0), axis=0, keepdims=True)
            back[places[k]] = message_of(out * inverse[part], flat, rows)
    back[unused] = empty


def four_fold(x, op):
    x = op(x, pltpu.roll(x, 2 * PAD, 1))
    return op(x, pltpu.roll(x, PAD, 1))


def stage_kernel(got, onward):
    sources, many, _, head_dim = got.shape
    rows = 28
    me = lax.axis_index("serve")
    depth = sources * many * PAD
    flat = got[...].reshape(depth, head_dim)
    g2, k2 = iota((many, depth), 0), iota((many, depth), 1)
    in_row = jnp.logical_and(k2 % PAD >= rows, k2 % PAD < rows + 3)
    pick = jnp.logical_and((k2 // PAD) % many == g2, in_row)
    lse = lax.dot_general(
        jnp.where(pick, 1.0, 0.0).astype(BF16), flat, (((1,), (0,)), ((), ())),
        preferred_element_type=F32,
    )
    top = four_fold(lse, jnp.maximum)
    weight = jnp.exp2(lse - top)
    total = four_fold(weight, jnp.add)
    weight = weight / total
    row, lane = iota((PAD, head_dim), 0), iota((PAD, head_dim), 1)
    same = jnp.logical_and(lane % PAD == row, row < rows)
    offset = lax.bitwise_and(lax.shift_right_logical(me, 2), 3) * PAD
    lane = iota((many, head_dim), 1)
    in_span = jnp.logical_and(lane >= offset, lane < offset + rows)
    lse = jnp.where(in_span, top + jnp.log2(total), 0.0)
    for m in range(many):
        spread = jnp.where(same, weight[m : m + 1], 0.0)
        high = spread.astype(BF16)
        low = (spread - high.astype(F32)).astype(BF16)
        both = jnp.concatenate([high, low], axis=0)
        block = got[:, m].reshape(sources * PAD, head_dim)
        out = lax.dot_general(both, block, (((1,), (0,)), ((), ())), preferred_element_type=F32)
        onward[m] = message_of(out[:PAD] + out[PAD:], lse[m : m + 1], rows)


def combine_kernel(lengths_hbm, got, local_out, local_lse, result, lengths, sems):
    copies = fetch(((lengths_hbm, lengths),), sems)
    devices, _, head_dim = got.shape
    slots = local_out.shape[0]
    steps, groups, rows = 4, 7, 28
    depth = devices * PAD
    many = devices // 4
    flat = got[...].reshape(depth, head_dim)
    g2, k2 = iota((many, depth), 0), iota((many, depth), 1)
    in_row = jnp.logical_and(k2 % PAD >= rows, k2 % PAD < rows + 3)
    pick = jnp.logical_and(k2 // (4 * PAD) == g2, in_row)
    lse = lax.dot_general(
        jnp.where(pick, 1.0, 0.0).astype(BF16), flat, (((1,), (0,)), ((), ())),
        preferred_element_type=F32,
    )
    top = jnp.max(lse, axis=0, keepdims=True)
    top = jnp.broadcast_to(top, (8, head_dim))
    top = four_fold(top, jnp.maximum)
    weight = jnp.exp2(lse - top[0:1])
    row, lane = iota((PAD, head_dim), 0), iota((PAD, head_dim), 1)
    same = jnp.logical_and(lane % PAD == row, row < rows)
    spread = jnp.concatenate(
        [jnp.where(same, weight[g : g + 1], 0.0) for g in range(many)], axis=1
    )
    high = spread.astype(BF16)
    low = (spread - high.astype(F32)).astype(BF16)
    both = jnp.concatenate([high, low], axis=0)
    out = lax.dot_general(both, flat, (((1,), (0,)), ((), ())), preferred_element_type=F32)
    out = out[:PAD] + out[PAD:]
    total = jnp.sum(spread, axis=1, keepdims=True)
    total = jnp.where(row[:, 0:1] < rows, total, 1.0)
    first = jnp.logical_and(lane == row, row < rows)
    column = jnp.sum(jnp.where(first, top[0:1], 0.0), axis=1, keepdims=True)
    far_out = out / total
    far_lse = jnp.broadcast_to(column + jnp.log2(total), far_out.shape)
    copies[0].wait()
    for slot in range(slots):
        far_here = jnp.where(lengths[slot] > 256, far_lse, neg_fill)
        near = local_lse[slot]
        overall = jnp.maximum(far_here, near)
        a, b = jnp.exp2(far_here - overall), jnp.exp2(near - overall)
        final = ((a * far_out + b * local_out[slot]) / (a + b)).astype(BF16)
        for g in range(groups):
            columns = slice(g * head_dim, (g + 1) * head_dim)
            for half in range(2):
                start = g * steps + half * 2
                result[slot * 2 + half, :, columns] = final[start : start + 2]


VMEM = pl.BlockSpec(memory_space=pltpu.VMEM)
SMEM = pl.BlockSpec(memory_space=pltpu.SMEM)
HBM = pl.BlockSpec(memory_space=pltpu.HBM)


def shards(
    queries, new_keys, new_values, key_cache, value_cache, lengths, block_owner, block_number
):
    slots, steps, groups, head_dim = queries.shape
    blocks, span = key_cache.shape[:2]
    devices = lax.axis_size("serve")
    chunk = 32
    scale2 = head_dim**-0.5 * math.log2(math.e)
    queries = jnp.transpose(queries, (0, 2, 1, 3))
    new_keys = new_keys.reshape(slots, steps, head_dim)
    new_values = new_values.reshape(slots, steps, head_dim)
    key_cache = key_cache.reshape(blocks, span, head_dim)
    value_cache = value_cache.reshape(blocks, span, head_dim)

    along_z = [[4 * z + y for z in range(16)] for y in range(4)]
    along_y = [[4 * z + y for y in range(4)] for z in range(16)]
    exchange = functools.partial(
        lax.all_to_all, axis_name="serve", split_axis=0, concat_axis=0, tiled=True
    )
    in_hbm = functools.partial(pltpu.with_memory_space_constraint, memory_space=pltpu.HBM)
    in_vmem = functools.partial(pltpu.with_memory_space_constraint, memory_space=pltpu.VMEM)
    queries, new_keys, new_values, key_cache, value_cache, lengths, block_owner, block_number = map(
        in_hbm,
        (queries, new_keys, new_values, key_cache, value_cache, lengths, block_owner, block_number),
    )
    small = pltpu.CompilerParams(vmem_limit_bytes=8 << 20)
    message = pl.pallas_call(
        prep_kernel,
        out_shape=jax.ShapeDtypeStruct((16, PAD, head_dim), BF16),
        in_specs=[HBM, HBM],
        out_specs=VMEM,
        scratch_shapes=[
            pltpu.SMEM((slots,), jnp.int32),
            pltpu.VMEM(queries.shape, BF16),
            pltpu.VMEM((PAD, head_dim), F32),
            pltpu.SemaphoreType.DMA((2,)),
        ],
        compiler_params=small,
        name="prep",
    )(lengths, queries)
    keys, table, local_out, local_lse = pl.pallas_call(
        functools.partial(local_kernel, scale2),
        out_shape=(
            pltpu.VMEM(key_cache.shape, BF16),
            jax.ShapeDtypeStruct((256,), jnp.int32),
            jax.ShapeDtypeStruct((slots, PAD, head_dim), F32),
            jax.ShapeDtypeStruct((slots, PAD, head_dim), F32),
        ),
        in_specs=[HBM] * 8,
        out_specs=(VMEM, SMEM, VMEM, VMEM),
        scratch_shapes=[
            pltpu.SMEM((slots,), jnp.int32),
            pltpu.SMEM((blocks,), jnp.int32),
            pltpu.SMEM((blocks,), jnp.int32),
            pltpu.VMEM(queries.shape, BF16),
            pltpu.VMEM(new_keys.shape, BF16),
            pltpu.VMEM(new_values.shape, BF16),
            pltpu.VMEM((slots, PAD, head_dim), F32),
            pltpu.VMEM((slots, span, head_dim), BF16),
            pltpu.SemaphoreType.DMA((8 + slots,)),
        ],
        compiler_params=small,
        cost_estimate=pl.CostEstimate(
            flops=1 << 28, bytes_accessed=2 * key_cache.size * 2, transcendentals=1 << 18
        ),
        name="local",
    )(
        lengths, block_owner, block_number, queries, new_keys, new_values, key_cache, value_cache
    )
    column = exchange(message, axis_index_groups=along_z)
    far = exchange(jnp.broadcast_to(column[None], (4,) + column.shape), axis_index_groups=along_y)
    back = pl.pallas_call(
        functools.partial(far_kernel, chunk, scale2),
        out_shape=jax.ShapeDtypeStruct((devices, PAD, head_dim), BF16),
        in_specs=[SMEM, VMEM, VMEM, HBM],
        out_specs=VMEM,
        scratch_shapes=[
            pltpu.VMEM((blocks, span, head_dim), BF16),
            pltpu.SemaphoreType.DMA((4,)),
        ],
        compiler_params=small,
        name="far",
    )(table, far.reshape(devices, PAD, head_dim), in_vmem(keys), value_cache)
    back = back.reshape(4, 16, PAD, head_dim)
    row_got = exchange(back, axis_index_groups=along_y)
    onward = pl.pallas_call(
        stage_kernel,
        out_shape=jax.ShapeDtypeStruct((16, PAD, head_dim), BF16),
        in_specs=[VMEM],
        out_specs=VMEM,
        compiler_params=small,
        name="stage",
    )(row_got)
    got = exchange(onward, axis_index_groups=along_z)
    rows_out = pl.pallas_call(
        combine_kernel,
        out_shape=jax.ShapeDtypeStruct((8, 2, groups * head_dim), BF16),
        in_specs=[HBM, VMEM, VMEM, VMEM],
        out_specs=VMEM,
        scratch_shapes=[pltpu.SMEM((slots,), jnp.int32), pltpu.SemaphoreType.DMA((1,))],
        compiler_params=small,
        name="combine",
    )(lengths, got, local_out, local_lse)
    swapped = lax.all_to_all(rows_out, "tensor", split_axis=0, concat_axis=0, tiled=True)
    return jnp.transpose(swapped, (1, 0, 2)).reshape(2, 8 * groups * head_dim)


def solution(mesh):
    placed = (
        P("serve", None, "tensor", None),
        P("serve", None, "tensor", None),
        P("serve", None, "tensor", None),
        P("serve", None, "tensor", None),
        P("serve", None, "tensor", None),
        P("serve"),
        P("serve"),
        P("serve"),
    )
    return jax.shard_map(
        shards, mesh=mesh, in_specs=placed, out_specs=P(("serve", "tensor"), None), check_vma=False
    )
```

```python
import functools
import math

import jax
import jax.numpy as jnp
from jax import lax
from jax.experimental import pallas as pl
from jax.experimental.pallas import tpu as pltpu
from jax.sharding import PartitionSpec as P

neg_fill = -1e30
PAD = 32
F32 = jnp.float32
BF16 = jnp.bfloat16


def iota(shape, dim):
    return lax.broadcasted_iota(jnp.int32, shape, dim)


def column_first(device):
    return lax.bitwise_and(device, 3) * 16 + lax.shift_right_logical(device, 2)


def message_of(out, lse, rows):
    row = iota(out.shape, 0)
    high = lse.astype(BF16).astype(F32)
    rest = lse - high
    middle = rest.astype(BF16).astype(F32)
    low = rest - middle
    stats = jnp.where(
        row == rows,
        high,
        jnp.where(row == rows + 1, middle, jnp.where(row == rows + 2, low, 0.0)),
    )
    return jnp.where(row < rows, out, stats).astype(BF16)


def pad_rows(length, query, padded):
    groups, steps, head_dim = query.shape
    rows = groups * steps
    for g in range(groups):
        padded[g * steps : (g + 1) * steps, :] = query[g].astype(F32)
    row = iota((PAD - rows, head_dim), 0)
    high = lax.shift_right_logical(length, 6).astype(F32)
    low = lax.bitwise_and(length, 63).astype(F32)
    padded[rows:PAD, :] = jnp.where(row == 0, high, jnp.where(row == 1, low, 0.0))


def fetch(pairs, sems):
    copies = [
        pltpu.make_async_copy(source, target, sems.at[i])
        for i, (source, target) in enumerate(pairs)
    ]
    for copy in copies:
        copy.start()
    return copies


def prep_kernel(lengths_hbm, queries_hbm, message, lengths, queries, padded, sems):
    copies = fetch(((lengths_hbm, lengths), (queries_hbm, queries)), sems)
    for copy in copies:
        copy.wait()
    long_slot, length = jnp.int32(0), lengths[0]
    for slot in range(1, queries.shape[0]):
        is_long = lengths[slot] > 256
        long_slot = jnp.where(is_long, slot, long_slot)
        length = jnp.where(is_long, lengths[slot], length)
    pad_rows(length, queries.at[long_slot], padded)
    message[...] = jnp.broadcast_to(padded[...].astype(BF16)[None], message.shape)


def attend(query, limit, keys, values, scale2):
    score = lax.dot_general(query, keys, (((1,), (1,)), ((), ())), preferred_element_type=F32)
    score = jnp.where(iota(score.shape, 1).astype(F32) < limit, score, neg_fill)
    top = jnp.max(score, axis=1, keepdims=True)
    weights = jnp.exp2((score - top) * scale2).astype(BF16)
    total = jnp.sum(weights.astype(F32), axis=1, keepdims=True)
    out = lax.dot_general(weights, values, (((1,), (0,)), ((), ())), preferred_element_type=F32)
    return out / total, top * scale2 + jnp.log2(total)


def local_kernel(
    scale2, lengths_hbm, owners_hbm, numbers_hbm, queries_hbm, new_keys_hbm, new_values_hbm,
    key_cache, value_cache,
    table, local_out, local_lse,
    lengths, owners, numbers, queries, new_keys, new_values, padded, near_keys, near_values, sems,
):
    blocks, span, head_dim = key_cache.shape
    slots, steps, _ = new_keys.shape
    me = lax.axis_index("serve")
    small = ((lengths_hbm, lengths), (owners_hbm, owners), (numbers_hbm, numbers),
             (queries_hbm, queries), (new_keys_hbm, new_keys), (new_values_hbm, new_values))
    copies = fetch(small, sems)
    for copy in copies:
        copy.wait()

    far_count, near_count = jnp.int32(0), jnp.int32(0)
    for p in range(blocks):
        owner, number = owners[p], numbers[p]
        device = lax.shift_right_logical(owner, 2)
        near = device == me
        at = jnp.where(near, blocks - 1 - near_count, far_count)
        table[at] = p
        table[64 + at] = jnp.where(near, lax.bitwise_and(owner, 3), column_first(device))
        table[128 + at] = number * span
        one = near.astype(jnp.int32)
        far_count, near_count = far_count + 1 - one, near_count + one
    table[192] = far_count
    for slot in range(slots):
        table[193 + slot] = lengths[slot]
    own_blocks = fetch(
        [(key_cache.at[table[blocks - 1 - k]], near_keys.at[k]) for k in range(slots)]
        + [(value_cache.at[table[blocks - 1 - k]], near_values.at[k]) for k in range(slots)],
        sems.at[pl.ds(8, 2 * slots)],
    )

    for slot in range(slots):
        pad_rows(lengths[slot], queries.at[slot], padded.at[slot])
    all_rows = padded[...].astype(BF16).reshape(slots * PAD, head_dim)
    nk = new_keys[...].astype(F32).reshape(slots * steps, head_dim).astype(BF16)
    nv = new_values[...].astype(F32).reshape(slots * steps, head_dim).astype(BF16)
    scores = lax.dot_general(all_rows, nk, (((1,), (1,)), ((), ())), preferred_element_type=F32)
    r2, c2 = iota(scores.shape, 0), iota(scores.shape, 1)
    seen = jnp.logical_and(r2 // PAD == c2 // steps, c2 % steps <= r2 % steps)
    scores = jnp.where(seen, scores, neg_fill)
    top = jnp.max(scores, axis=1, keepdims=True)
    weights = jnp.where(seen, jnp.exp2((scores - top) * scale2), 0.0).astype(BF16)
    total = jnp.sum(weights.astype(F32), axis=1, keepdims=True)
    out = lax.dot_general(weights, nv, (((1,), (0,)), ((), ())), preferred_element_type=F32)
    lse = jnp.broadcast_to(top * scale2 + jnp.log2(total), out.shape)
    local_out[...] = (out / total).reshape(local_out.shape)
    local_lse[...] = lse.reshape(local_lse.shape)

    def merge(slot, new_out, new):
        old = local_lse[slot]
        overall = jnp.maximum(old, new)
        a, b = jnp.exp2(old - overall), jnp.exp2(new - overall)
        total = a + b
        local_out[slot] = (a * local_out[slot] + b * new_out) / total
        local_lse[slot] = overall + jnp.log2(total)

    for copy in own_blocks:
        copy.wait()
    ats = [blocks - 1 - k for k in range(slots)]
    parts = []
    for k, at in enumerate(ats):
        slot = table[64 + at]
        limit = (lengths[slot] - table[128 + at]).astype(F32)
        parts.append(
            attend(padded[slot].astype(BF16), limit, near_keys[k], near_values[k], scale2)
        )
    for at, (new_out, new) in zip(ats, parts):
        merge(table[64 + at], new_out, jnp.broadcast_to(new, new_out.shape))

    def more(k, carry):
        at = blocks - 1 - k
        slot = table[64 + at]
        block = table[at]
        pair = ((key_cache.at[block], near_keys.at[0]), (value_cache.at[block], near_values.at[0]))
        for copy in fetch(pair, sems.at[pl.ds(8, 2)]):
            copy.wait()
        limit = (lengths[slot] - table[128 + at]).astype(F32)
        new_out, new = attend(
            padded[slot].astype(BF16), limit, near_keys[0], near_values[0], scale2
        )
        merge(slot, new_out, jnp.broadcast_to(new, new_out.shape))
        return carry

    lax.fori_loop(slots, near_count, more, 0)


def far_kernel(chunk, scale2, table, far, keys, values, back):
    blocks, span, head_dim = keys.shape
    rows = 28
    count = blocks - 4
    me = lax.axis_index("serve")
    far_count = table[192]
    row, lane = iota((PAD, head_dim), 0), iota((PAD, head_dim), 1)
    offset = lax.bitwise_and(me, 3) * PAD
    diagonal = jnp.logical_and(lane == offset + row, row < rows)
    in_span = jnp.logical_and(lane >= offset, lane < offset + rows)
    empty = jnp.where(jnp.logical_and(row == rows, in_span), neg_fill, 0.0).astype(BF16)
    back[...] = jnp.broadcast_to(empty[None], back.shape)
    unused = column_first(me)
    position = iota((PAD, span), 1).astype(F32)
    for c in range(count // chunk):
        ids = [table[k] for k in range(c * chunk, (c + 1) * chunk)]
        places = [
            jnp.where(k < far_count, table[64 + k], unused)
            for k in range(c * chunk, (c + 1) * chunk)
        ]
        raw = []
        for k in range(chunk):
            query = far[places[k]]
            lens = query[rows : rows + 2, :].astype(F32)
            length = lens[0:1, 0:1] * 64.0 + lens[1:2, 0:1]
            score = lax.dot_general(
                query, keys[ids[k]], (((1,), (1,)), ((), ())), preferred_element_type=F32
            )
            limit = length - table[128 + c * chunk + k].astype(F32)
            raw.append(jnp.where(position < limit, score, neg_fill))
        raw = jnp.concatenate(raw, axis=0)
        top = jnp.max(raw, axis=1, keepdims=True)
        weights = jnp.exp2((raw - top) * scale2).astype(BF16)
        total = jnp.sum(weights.astype(F32), axis=1, keepdims=True)
        lse = top * scale2 + jnp.log2(total)
        inverse = 1.0 / total
        for k in range(chunk):
            part = slice(k * PAD, (k + 1) * PAD)
            out = lax.dot_general(
                weights[part], values[ids[k]], (((1,), (0,)), ((), ())),
                preferred_element_type=F32,
            )
            flat = jnp.sum(jnp.where(diagonal, lse[part], 0.0), axis=0, keepdims=True)
            back[places[k]] = message_of(out * inverse[part], flat, rows)
    back[unused] = empty


def spread_kernel(column, copies):
    for k in range(copies.shape[0]):
        copies[k] = column[...]


def four_fold(x, op):
    x = op(x, pltpu.roll(x, 2 * PAD, 1))
    return op(x, pltpu.roll(x, PAD, 1))


def stage_kernel(got, onward):
    sources, many, _, head_dim = got.shape
    rows = 28
    me = lax.axis_index("serve")
    depth = sources * many * PAD
    flat = got[...].reshape(depth, head_dim)
    g2, k2 = iota((many, depth), 0), iota((many, depth), 1)
    in_row = jnp.logical_and(k2 % PAD >= rows, k2 % PAD < rows + 3)
    pick = jnp.logical_and((k2 // PAD) % many == g2, in_row)
    lse = lax.dot_general(
        jnp.where(pick, 1.0, 0.0).astype(BF16), flat, (((1,), (0,)), ((), ())),
        preferred_element_type=F32,
    )
    top = four_fold(lse, jnp.maximum)
    weight = jnp.exp2(lse - top)
    total = four_fold(weight, jnp.add)
    weight = weight / total
    row, lane = iota((PAD, head_dim), 0), iota((PAD, head_dim), 1)
    same = jnp.logical_and(lane % PAD == row, row < rows)
    offset = lax.bitwise_and(lax.shift_right_logical(me, 2), 3) * PAD
    lane = iota((many, head_dim), 1)
    in_span = jnp.logical_and(lane >= offset, lane < offset + rows)
    lse = jnp.where(in_span, top + jnp.log2(total), 0.0)
    for m in range(many):
        spread = jnp.where(same, weight[m : m + 1], 0.0)
        high = spread.astype(BF16)
        low = (spread - high.astype(F32)).astype(BF16)
        both = jnp.concatenate([high, low], axis=0)
        block = got[:, m].reshape(sources * PAD, head_dim)
        out = lax.dot_general(both, block, (((1,), (0,)), ((), ())), preferred_element_type=F32)
        onward[m] = message_of(out[:PAD] + out[PAD:], lse[m : m + 1], rows)


def combine_kernel(table, got, local_out, local_lse, result):
    devices, _, head_dim = got.shape
    slots = local_out.shape[0]
    steps, groups, rows = 4, 7, 28
    depth = devices * PAD
    many = devices // 4
    flat = got[...].reshape(depth, head_dim)
    g2, k2 = iota((many, depth), 0), iota((many, depth), 1)
    in_row = jnp.logical_and(k2 % PAD >= rows, k2 % PAD < rows + 3)
    pick = jnp.logical_and(k2 // (4 * PAD) == g2, in_row)
    lse = lax.dot_general(
        jnp.where(pick, 1.0, 0.0).astype(BF16), flat, (((1,), (0,)), ((), ())),
        preferred_element_type=F32,
    )
    top = jnp.max(lse, axis=0, keepdims=True)
    top = jnp.broadcast_to(top, (8, head_dim))
    top = four_fold(top, jnp.maximum)
    weight = jnp.exp2(lse - top[0:1])
    row, lane = iota((PAD, head_dim), 0), iota((PAD, head_dim), 1)
    same = jnp.logical_and(lane % PAD == row, row < rows)
    spread = jnp.concatenate(
        [jnp.where(same, weight[g : g + 1], 0.0) for g in range(many)], axis=1
    )
    high = spread.astype(BF16)
    low = (spread - high.astype(F32)).astype(BF16)
    both = jnp.concatenate([high, low], axis=0)
    out = lax.dot_general(both, flat, (((1,), (0,)), ((), ())), preferred_element_type=F32)
    out = out[:PAD] + out[PAD:]
    total = jnp.sum(spread, axis=1, keepdims=True)
    total = jnp.where(row[:, 0:1] < rows, total, 1.0)
    first = jnp.logical_and(lane == row, row < rows)
    column = jnp.sum(jnp.where(first, top[0:1], 0.0), axis=1, keepdims=True)
    far_out = out / total
    far_lse = jnp.broadcast_to(column + jnp.log2(total), far_out.shape)
    for slot in range(slots):
        far_here = jnp.where(table[193 + slot] > 256, far_lse, neg_fill)
        near = local_lse[slot]
        overall = jnp.maximum(far_here, near)
        a, b = jnp.exp2(far_here - overall), jnp.exp2(near - overall)
        final = ((a * far_out + b * local_out[slot]) / (a + b)).astype(BF16)
        for g in range(groups):
            columns = slice(g * head_dim, (g + 1) * head_dim)
            for half in range(2):
                start = g * steps + half * 2
                result[slot * 2 + half, :, columns] = final[start : start + 2]


VMEM = pl.BlockSpec(memory_space=pltpu.VMEM)
SMEM = pl.BlockSpec(memory_space=pltpu.SMEM)
HBM = pl.BlockSpec(memory_space=pltpu.HBM)


def shards(
    queries, new_keys, new_values, key_cache, value_cache, lengths, block_owner, block_number
):
    slots, steps, groups, head_dim = queries.shape
    blocks, span = key_cache.shape[:2]
    devices = lax.axis_size("serve")
    chunk = 32
    scale2 = head_dim**-0.5 * math.log2(math.e)
    queries = jnp.transpose(queries, (0, 2, 1, 3))
    new_keys = new_keys.reshape(slots, steps, head_dim)
    new_values = new_values.reshape(slots, steps, head_dim)
    key_cache = key_cache.reshape(blocks, span, head_dim)
    value_cache = value_cache.reshape(blocks, span, head_dim)

    along_z = [[4 * z + y for z in range(16)] for y in range(4)]
    along_y = [[4 * z + y for y in range(4)] for z in range(16)]
    exchange = functools.partial(
        lax.all_to_all, axis_name="serve", split_axis=0, concat_axis=0, tiled=True
    )
    in_hbm = functools.partial(pltpu.with_memory_space_constraint, memory_space=pltpu.HBM)
    in_smem = functools.partial(pltpu.with_memory_space_constraint, memory_space=pltpu.SMEM)
    in_vmem = functools.partial(pltpu.with_memory_space_constraint, memory_space=pltpu.VMEM)
    plain_keys, plain_values = key_cache, value_cache
    queries, new_keys, new_values, key_cache, value_cache, lengths, block_owner, block_number = map(
        in_hbm,
        (queries, new_keys, new_values, key_cache, value_cache, lengths, block_owner, block_number),
    )
    small = pltpu.CompilerParams(vmem_limit_bytes=8 << 20)
    message = pl.pallas_call(
        prep_kernel,
        out_shape=jax.ShapeDtypeStruct((16, PAD, head_dim), BF16),
        in_specs=[HBM, HBM],
        out_specs=VMEM,
        scratch_shapes=[
            pltpu.SMEM((slots,), jnp.int32),
            pltpu.VMEM(queries.shape, BF16),
            pltpu.VMEM((PAD, head_dim), F32),
            pltpu.SemaphoreType.DMA((2,)),
        ],
        compiler_params=small,
        name="prep",
    )(lengths, queries)
    table, local_out, local_lse = pl.pallas_call(
        functools.partial(local_kernel, scale2),
        out_shape=(
            pltpu.SMEM((256,), jnp.int32),
            jax.ShapeDtypeStruct((slots, PAD, head_dim), F32),
            jax.ShapeDtypeStruct((slots, PAD, head_dim), F32),
        ),
        in_specs=[HBM] * 8,
        out_specs=(SMEM, VMEM, VMEM),
        scratch_shapes=[
            pltpu.SMEM((slots,), jnp.int32),
            pltpu.SMEM((blocks,), jnp.int32),
            pltpu.SMEM((blocks,), jnp.int32),
            pltpu.VMEM(queries.shape, BF16),
            pltpu.VMEM(new_keys.shape, BF16),
            pltpu.VMEM(new_values.shape, BF16),
            pltpu.VMEM((slots, PAD, head_dim), F32),
            pltpu.VMEM((slots, span, head_dim), BF16),
            pltpu.VMEM((slots, span, head_dim), BF16),
            pltpu.SemaphoreType.DMA((8 + 2 * slots,)),
        ],
        compiler_params=small,
        cost_estimate=pl.CostEstimate(
            flops=1 << 28, bytes_accessed=key_cache.size * 2, transcendentals=1 << 18
        ),
        name="local",
    )(
        lengths, block_owner, block_number, queries, new_keys, new_values, key_cache, value_cache
    )
    column = exchange(message, axis_index_groups=along_z)
    column, local_out = lax.optimization_barrier((column, local_out))
    copies = pl.pallas_call(
        spread_kernel,
        out_shape=jax.ShapeDtypeStruct((4,) + column.shape, BF16),
        in_specs=[VMEM],
        out_specs=VMEM,
        compiler_params=small,
        cost_estimate=pl.CostEstimate(
            flops=1 << 32, bytes_accessed=1 << 20, transcendentals=0
        ),
        name="spread",
    )(column)
    far = exchange(copies, axis_index_groups=along_y)
    back = pl.pallas_call(
        functools.partial(far_kernel, chunk, scale2),
        out_shape=jax.ShapeDtypeStruct((devices, PAD, head_dim), BF16),
        in_specs=[SMEM, VMEM, VMEM, VMEM],
        out_specs=VMEM,
        compiler_params=small,
        name="far",
    )(in_smem(table), far.reshape(devices, PAD, head_dim), in_vmem(plain_keys), in_vmem(plain_values))
    back = back.reshape(4, 16, PAD, head_dim)
    row_got = exchange(back, axis_index_groups=along_y)
    onward = pl.pallas_call(
        stage_kernel,
        out_shape=jax.ShapeDtypeStruct((16, PAD, head_dim), BF16),
        in_specs=[VMEM],
        out_specs=VMEM,
        compiler_params=small,
        name="stage",
    )(row_got)
    got = exchange(onward, axis_index_groups=along_z)
    rows_out = pl.pallas_call(
        combine_kernel,
        out_shape=jax.ShapeDtypeStruct((8, 2, groups * head_dim), BF16),
        in_specs=[SMEM, VMEM, VMEM, VMEM],
        out_specs=VMEM,
        compiler_params=small,
        name="combine",
    )(in_smem(table), got, local_out, local_lse)
    swapped = lax.all_to_all(rows_out, "tensor", split_axis=0, concat_axis=0, tiled=True)
    return jnp.transpose(swapped, (1, 0, 2)).reshape(2, 8 * groups * head_dim)


def solution(mesh):
    placed = (
        P("serve", None, "tensor", None),
        P("serve", None, "tensor", None),
        P("serve", None, "tensor", None),
        P("serve", None, "tensor", None),
        P("serve", None, "tensor", None),
        P("serve"),
        P("serve"),
        P("serve"),
    )
    return jax.shard_map(
        shards, mesh=mesh, in_specs=placed, out_specs=P(("serve", "tensor"), None), check_vma=False
    )
```

```python
import functools
import math

import jax
import jax.numpy as jnp
from jax import lax
from jax.experimental import pallas as pl
from jax.experimental.pallas import tpu as pltpu
from jax.sharding import PartitionSpec as P

neg_fill = -1e30
PAD = 32
F32 = jnp.float32
BF16 = jnp.bfloat16


def iota(shape, dim):
    return lax.broadcasted_iota(jnp.int32, shape, dim)


def column_first(device):
    return lax.bitwise_and(device, 3) * 16 + lax.shift_right_logical(device, 2)


def message_of(out, lse, rows):
    row = iota(out.shape, 0)
    high = lse.astype(BF16).astype(F32)
    rest = lse - high
    middle = rest.astype(BF16).astype(F32)
    low = rest - middle
    stats = jnp.where(
        row == rows,
        high,
        jnp.where(row == rows + 1, middle, jnp.where(row == rows + 2, low, 0.0)),
    )
    return jnp.where(row < rows, out, stats).astype(BF16)


def pad_rows(length, query, padded):
    groups, steps, head_dim = query.shape
    rows = groups * steps
    for g in range(groups):
        padded[g * steps : (g + 1) * steps, :] = query[g].astype(F32)
    row = iota((PAD - rows, head_dim), 0)
    high = lax.shift_right_logical(length, 6).astype(F32)
    low = lax.bitwise_and(length, 63).astype(F32)
    padded[rows:PAD, :] = jnp.where(row == 0, high, jnp.where(row == 1, low, 0.0))


def fetch(pairs, sems):
    copies = [
        pltpu.make_async_copy(source, target, sems.at[i])
        for i, (source, target) in enumerate(pairs)
    ]
    for copy in copies:
        copy.start()
    return copies


def prep_kernel(lengths_hbm, queries_hbm, message, lengths, queries, padded, sems):
    copies = fetch(((lengths_hbm, lengths), (queries_hbm, queries)), sems)
    for copy in copies:
        copy.wait()
    long_slot, length = jnp.int32(0), lengths[0]
    for slot in range(1, queries.shape[0]):
        is_long = lengths[slot] > 256
        long_slot = jnp.where(is_long, slot, long_slot)
        length = jnp.where(is_long, lengths[slot], length)
    pad_rows(length, queries.at[long_slot], padded)
    message[...] = jnp.broadcast_to(padded[...].astype(BF16)[None], message.shape)


def attend(query, limit, keys, values, scale2):
    score = lax.dot_general(query, keys, (((1,), (1,)), ((), ())), preferred_element_type=F32)
    score = jnp.where(iota(score.shape, 1).astype(F32) < limit, score, neg_fill)
    top = jnp.max(score, axis=1, keepdims=True)
    weights = jnp.exp2((score - top) * scale2).astype(BF16)
    total = jnp.sum(weights.astype(F32), axis=1, keepdims=True)
    out = lax.dot_general(weights, values, (((1,), (0,)), ((), ())), preferred_element_type=F32)
    return out / total, top * scale2 + jnp.log2(total)


def local_kernel(
    scale2, lengths_hbm, owners_hbm, numbers_hbm, queries_hbm, new_keys_hbm, new_values_hbm,
    key_cache, value_cache,
    table, local_out, local_lse,
    lengths, owners, numbers, queries, new_keys, new_values, padded, near_keys, near_values, sems,
):
    blocks, span, head_dim = key_cache.shape
    slots, steps, _ = new_keys.shape
    me = lax.axis_index("serve")
    small = ((lengths_hbm, lengths), (owners_hbm, owners), (numbers_hbm, numbers),
             (queries_hbm, queries), (new_keys_hbm, new_keys), (new_values_hbm, new_values))
    copies = fetch(small, sems)
    for copy in copies:
        copy.wait()

    far_count, near_count = jnp.int32(0), jnp.int32(0)
    for p in range(blocks):
        owner, number = owners[p], numbers[p]
        device = lax.shift_right_logical(owner, 2)
        near = device == me
        at = jnp.where(near, blocks - 1 - near_count, far_count)
        table[at] = p
        table[64 + at] = jnp.where(near, lax.bitwise_and(owner, 3), column_first(device))
        table[128 + at] = number * span
        one = near.astype(jnp.int32)
        far_count, near_count = far_count + 1 - one, near_count + one
    table[192] = far_count
    for slot in range(slots):
        table[193 + slot] = lengths[slot]
    own_blocks = fetch(
        [(key_cache.at[table[blocks - 1 - k]], near_keys.at[k]) for k in range(slots)]
        + [(value_cache.at[table[blocks - 1 - k]], near_values.at[k]) for k in range(slots)],
        sems.at[pl.ds(8, 2 * slots)],
    )

    for slot in range(slots):
        pad_rows(lengths[slot], queries.at[slot], padded.at[slot])
    all_rows = padded[...].astype(BF16).reshape(slots * PAD, head_dim)
    nk = new_keys[...].astype(F32).reshape(slots * steps, head_dim).astype(BF16)
    nv = new_values[...].astype(F32).reshape(slots * steps, head_dim).astype(BF16)
    scores = lax.dot_general(all_rows, nk, (((1,), (1,)), ((), ())), preferred_element_type=F32)
    r2, c2 = iota(scores.shape, 0), iota(scores.shape, 1)
    seen = jnp.logical_and(r2 // PAD == c2 // steps, c2 % steps <= r2 % steps)
    scores = jnp.where(seen, scores, neg_fill)
    top = jnp.max(scores, axis=1, keepdims=True)
    weights = jnp.where(seen, jnp.exp2((scores - top) * scale2), 0.0).astype(BF16)
    total = jnp.sum(weights.astype(F32), axis=1, keepdims=True)
    out = lax.dot_general(weights, nv, (((1,), (0,)), ((), ())), preferred_element_type=F32)
    lse = jnp.broadcast_to(top * scale2 + jnp.log2(total), out.shape)
    local_out[...] = (out / total).reshape(local_out.shape)
    local_lse[...] = lse.reshape(local_lse.shape)

    def merge(slot, new_out, new):
        old = local_lse[slot]
        overall = jnp.maximum(old, new)
        a, b = jnp.exp2(old - overall), jnp.exp2(new - overall)
        total = a + b
        local_out[slot] = (a * local_out[slot] + b * new_out) / total
        local_lse[slot] = overall + jnp.log2(total)

    for copy in own_blocks:
        copy.wait()
    ats = [blocks - 1 - k for k in range(slots)]
    parts = []
    for k, at in enumerate(ats):
        slot = table[64 + at]
        limit = (lengths[slot] - table[128 + at]).astype(F32)
        parts.append(
            attend(padded[slot].astype(BF16), limit, near_keys[k], near_values[k], scale2)
        )
    for at, (new_out, new) in zip(ats, parts):
        merge(table[64 + at], new_out, jnp.broadcast_to(new, new_out.shape))

    def more(k, carry):
        at = blocks - 1 - k
        slot = table[64 + at]
        block = table[at]
        pair = ((key_cache.at[block], near_keys.at[0]), (value_cache.at[block], near_values.at[0]))
        for copy in fetch(pair, sems.at[pl.ds(8, 2)]):
            copy.wait()
        limit = (lengths[slot] - table[128 + at]).astype(F32)
        new_out, new = attend(
            padded[slot].astype(BF16), limit, near_keys[0], near_values[0], scale2
        )
        merge(slot, new_out, jnp.broadcast_to(new, new_out.shape))
        return carry

    lax.fori_loop(slots, near_count, more, 0)


def far_kernel(chunk, scale2, table, far, keys, values, back):
    blocks, span, head_dim = keys.shape
    rows = 28
    count = blocks - 4
    me = lax.axis_index("serve")
    far_count = table[192]
    row, lane = iota((PAD, head_dim), 0), iota((PAD, head_dim), 1)
    offset = lax.bitwise_and(me, 3) * PAD
    diagonal = jnp.logical_and(lane == offset + row, row < rows)
    in_span = jnp.logical_and(lane >= offset, lane < offset + rows)
    empty = jnp.where(jnp.logical_and(row == rows, in_span), neg_fill, 0.0).astype(BF16)
    back[...] = jnp.broadcast_to(empty[None], back.shape)
    unused = column_first(me)
    position = iota((PAD, span), 1).astype(F32)
    for c in range(count // chunk):
        ids = [table[k] for k in range(c * chunk, (c + 1) * chunk)]
        places = [
            jnp.where(k < far_count, table[64 + k], unused)
            for k in range(c * chunk, (c + 1) * chunk)
        ]
        raw = []
        for k in range(chunk):
            query = far[places[k]]
            lens = query[rows : rows + 2, :].astype(F32)
            length = lens[0:1, 0:1] * 64.0 + lens[1:2, 0:1]
            score = lax.dot_general(
                query, keys[ids[k]], (((1,), (1,)), ((), ())), preferred_element_type=F32
            )
            limit = length - table[128 + c * chunk + k].astype(F32)
            raw.append(jnp.where(position < limit, score, neg_fill))
        raw = jnp.concatenate(raw, axis=0)
        top = jnp.max(raw, axis=1, keepdims=True)
        weights = jnp.exp2((raw - top) * scale2).astype(BF16)
        total = jnp.sum(weights.astype(F32), axis=1, keepdims=True)
        lse = top * scale2 + jnp.log2(total)
        inverse = 1.0 / total
        for k in range(chunk):
            part = slice(k * PAD, (k + 1) * PAD)
            out = lax.dot_general(
                weights[part], values[ids[k]], (((1,), (0,)), ((), ())),
                preferred_element_type=F32,
            )
            flat = jnp.sum(jnp.where(diagonal, lse[part], 0.0), axis=0, keepdims=True)
            back[places[k]] = message_of(out * inverse[part], flat, rows)
    back[unused] = empty


def spread_kernel(column, copies):
    for k in range(copies.shape[0]):
        copies[k] = column[...]


def four_fold(x, op):
    x = op(x, pltpu.roll(x, 2 * PAD, 1))
    return op(x, pltpu.roll(x, PAD, 1))


def gathered_lse(groups, rows):
    part = iota(groups[0][0].shape, 0) + PAD // 2
    in_row = jnp.logical_and(part >= rows, part < rows + 3)
    out = []
    for group in groups:
        stats = sum(lower.astype(F32) for lower in group)
        out.append(jnp.sum(jnp.where(in_row, stats, 0.0), axis=0, keepdims=True))
    return jnp.concatenate(out, axis=0)


def stage_kernel(got, onward):
    sources, many, _, head_dim = got.shape
    rows = 28
    me = lax.axis_index("serve")
    lse = gathered_lse([[got[k, m, PAD // 2 :, :] for k in range(sources)] for m in range(many)], rows)
    top = four_fold(lse, jnp.maximum)
    weight = jnp.exp2(lse - top)
    total = four_fold(weight, jnp.add)
    weight = weight / total
    row, lane = iota((PAD, head_dim), 0), iota((PAD, head_dim), 1)
    same = jnp.logical_and(lane % PAD == row, row < rows)
    offset = lax.bitwise_and(lax.shift_right_logical(me, 2), 3) * PAD
    lane = iota((many, head_dim), 1)
    in_span = jnp.logical_and(lane >= offset, lane < offset + rows)
    lse = jnp.where(in_span, top + jnp.log2(total), 0.0)
    for m in range(many):
        spread = jnp.where(same, weight[m : m + 1], 0.0)
        high = spread.astype(BF16)
        low = (spread - high.astype(F32)).astype(BF16)
        both = jnp.concatenate([high, low], axis=0)
        block = got[:, m].reshape(sources * PAD, head_dim)
        out = lax.dot_general(both, block, (((1,), (0,)), ((), ())), preferred_element_type=F32)
        onward[m] = message_of(out[:PAD] + out[PAD:], lse[m : m + 1], rows)


def combine_kernel(table, got, local_out, local_lse, result):
    devices, _, head_dim = got.shape
    slots = local_out.shape[0]
    steps, groups, rows = 4, 7, 28
    depth = devices * PAD
    many = devices // 4
    flat = got[...].reshape(depth, head_dim)
    lse = gathered_lse(
        [[got[4 * g + k, PAD // 2 :, :] for k in range(4)] for g in range(many)], rows
    )
    top = jnp.max(lse, axis=0, keepdims=True)
    top = jnp.broadcast_to(top, (8, head_dim))
    top = four_fold(top, jnp.maximum)
    weight = jnp.exp2(lse - top[0:1])
    row, lane = iota((PAD, head_dim), 0), iota((PAD, head_dim), 1)
    same = jnp.logical_and(lane % PAD == row, row < rows)
    spread = jnp.concatenate(
        [jnp.where(same, weight[g : g + 1], 0.0) for g in range(many)], axis=1
    )
    high = spread.astype(BF16)
    low = (spread - high.astype(F32)).astype(BF16)
    both = jnp.concatenate([high, low], axis=0)
    out = lax.dot_general(both, flat, (((1,), (0,)), ((), ())), preferred_element_type=F32)
    out = out[:PAD] + out[PAD:]
    total = jnp.sum(spread, axis=1, keepdims=True)
    total = jnp.where(row[:, 0:1] < rows, total, 1.0)
    first = jnp.logical_and(lane == row, row < rows)
    column = jnp.sum(jnp.where(first, top[0:1], 0.0), axis=1, keepdims=True)
    far_out = out / total
    far_lse = jnp.broadcast_to(column + jnp.log2(total), far_out.shape)
    for slot in range(slots):
        far_here = jnp.where(table[193 + slot] > 256, far_lse, neg_fill)
        near = local_lse[slot]
        overall = jnp.maximum(far_here, near)
        a, b = jnp.exp2(far_here - overall), jnp.exp2(near - overall)
        final = ((a * far_out + b * local_out[slot]) / (a + b)).astype(BF16)
        for g in range(groups):
            columns = slice(g * head_dim, (g + 1) * head_dim)
            for half in range(2):
                start = g * steps + half * 2
                result[slot * 2 + half, :, columns] = final[start : start + 2]


VMEM = pl.BlockSpec(memory_space=pltpu.VMEM)
SMEM = pl.BlockSpec(memory_space=pltpu.SMEM)
HBM = pl.BlockSpec(memory_space=pltpu.HBM)


def shards(
    queries, new_keys, new_values, key_cache, value_cache, lengths, block_owner, block_number
):
    slots, steps, groups, head_dim = queries.shape
    blocks, span = key_cache.shape[:2]
    devices = lax.axis_size("serve")
    chunk = 32
    scale2 = head_dim**-0.5 * math.log2(math.e)
    queries = jnp.transpose(queries, (0, 2, 1, 3))
    new_keys = new_keys.reshape(slots, steps, head_dim)
    new_values = new_values.reshape(slots, steps, head_dim)
    key_cache = key_cache.reshape(blocks, span, head_dim)
    value_cache = value_cache.reshape(blocks, span, head_dim)

    along_z = [[4 * z + y for z in range(16)] for y in range(4)]
    along_y = [[4 * z + y for y in range(4)] for z in range(16)]
    exchange = functools.partial(
        lax.all_to_all, axis_name="serve", split_axis=0, concat_axis=0, tiled=True
    )
    in_hbm = functools.partial(pltpu.with_memory_space_constraint, memory_space=pltpu.HBM)
    in_smem = functools.partial(pltpu.with_memory_space_constraint, memory_space=pltpu.SMEM)
    in_vmem = functools.partial(pltpu.with_memory_space_constraint, memory_space=pltpu.VMEM)
    plain_keys, plain_values = key_cache, value_cache
    queries, new_keys, new_values, key_cache, value_cache, lengths, block_owner, block_number = map(
        in_hbm,
        (queries, new_keys, new_values, key_cache, value_cache, lengths, block_owner, block_number),
    )
    small = pltpu.CompilerParams(vmem_limit_bytes=8 << 20)
    message = pl.pallas_call(
        prep_kernel,
        out_shape=jax.ShapeDtypeStruct((16, PAD, head_dim), BF16),
        in_specs=[HBM, HBM],
        out_specs=VMEM,
        scratch_shapes=[
            pltpu.SMEM((slots,), jnp.int32),
            pltpu.VMEM(queries.shape, BF16),
            pltpu.VMEM((PAD, head_dim), F32),
            pltpu.SemaphoreType.DMA((2,)),
        ],
        compiler_params=small,
        name="prep",
    )(lengths, queries)
    table, local_out, local_lse = pl.pallas_call(
        functools.partial(local_kernel, scale2),
        out_shape=(
            pltpu.SMEM((256,), jnp.int32),
            jax.ShapeDtypeStruct((slots, PAD, head_dim), F32),
            jax.ShapeDtypeStruct((slots, PAD, head_dim), F32),
        ),
        in_specs=[HBM] * 8,
        out_specs=(SMEM, VMEM, VMEM),
        scratch_shapes=[
            pltpu.SMEM((slots,), jnp.int32),
            pltpu.SMEM((blocks,), jnp.int32),
            pltpu.SMEM((blocks,), jnp.int32),
            pltpu.VMEM(queries.shape, BF16),
            pltpu.VMEM(new_keys.shape, BF16),
            pltpu.VMEM(new_values.shape, BF16),
            pltpu.VMEM((slots, PAD, head_dim), F32),
            pltpu.VMEM((slots, span, head_dim), BF16),
            pltpu.VMEM((slots, span, head_dim), BF16),
            pltpu.SemaphoreType.DMA((8 + 2 * slots,)),
        ],
        compiler_params=small,
        cost_estimate=pl.CostEstimate(
            flops=1 << 28, bytes_accessed=key_cache.size * 2, transcendentals=1 << 18
        ),
        name="local",
    )(
        lengths, block_owner, block_number, queries, new_keys, new_values, key_cache, value_cache
    )
    column = exchange(message, axis_index_groups=along_z)
    column, local_out = lax.optimization_barrier((column, local_out))
    copies = pl.pallas_call(
        spread_kernel,
        out_shape=jax.ShapeDtypeStruct((4,) + column.shape, BF16),
        in_specs=[VMEM],
        out_specs=VMEM,
        compiler_params=small,
        cost_estimate=pl.CostEstimate(
            flops=1 << 32, bytes_accessed=1 << 20, transcendentals=0
        ),
        name="spread",
    )(column)
    far = exchange(copies, axis_index_groups=along_y)
    back = pl.pallas_call(
        functools.partial(far_kernel, chunk, scale2),
        out_shape=jax.ShapeDtypeStruct((devices, PAD, head_dim), BF16),
        in_specs=[SMEM, VMEM, VMEM, VMEM],
        out_specs=VMEM,
        compiler_params=small,
        name="far",
    )(in_smem(table), far.reshape(devices, PAD, head_dim), in_vmem(plain_keys), in_vmem(plain_values))
    back = back.reshape(4, 16, PAD, head_dim)
    row_got = exchange(back, axis_index_groups=along_y)
    onward = pl.pallas_call(
        stage_kernel,
        out_shape=jax.ShapeDtypeStruct((16, PAD, head_dim), BF16),
        in_specs=[VMEM],
        out_specs=VMEM,
        compiler_params=small,
        name="stage",
    )(row_got)
    got = exchange(onward, axis_index_groups=along_z)
    rows_out = pl.pallas_call(
        combine_kernel,
        out_shape=jax.ShapeDtypeStruct((8, 2, groups * head_dim), BF16),
        in_specs=[SMEM, VMEM, VMEM, VMEM],
        out_specs=VMEM,
        compiler_params=small,
        name="combine",
    )(in_smem(table), got, local_out, local_lse)
    swapped = lax.all_to_all(rows_out, "tensor", split_axis=0, concat_axis=0, tiled=True)
    return jnp.transpose(swapped, (1, 0, 2)).reshape(2, 8 * groups * head_dim)


def solution(mesh):
    placed = (
        P("serve", None, "tensor", None),
        P("serve", None, "tensor", None),
        P("serve", None, "tensor", None),
        P("serve", None, "tensor", None),
        P("serve", None, "tensor", None),
        P("serve"),
        P("serve"),
        P("serve"),
    )
    return jax.shard_map(
        shards, mesh=mesh, in_specs=placed, out_specs=P(("serve", "tensor"), None), check_vma=False
    )
```

```python
import functools
import math

import jax
import jax.numpy as jnp
from jax import lax
from jax.experimental import pallas as pl
from jax.experimental.pallas import tpu as pltpu
from jax.sharding import PartitionSpec as P

neg_fill = -1e30
PAD = 32
F32 = jnp.float32
BF16 = jnp.bfloat16


def iota(shape, dim):
    return lax.broadcasted_iota(jnp.int32, shape, dim)


SIDE = 8


def column_first(device):
    return lax.bitwise_and(device, SIDE - 1) * SIDE + lax.shift_right_logical(device, 3)


def message_of(out, lse, rows):
    row = iota(out.shape, 0)
    high = lse.astype(BF16).astype(F32)
    rest = lse - high
    middle = rest.astype(BF16).astype(F32)
    low = rest - middle
    stats = jnp.where(
        row == rows,
        high,
        jnp.where(row == rows + 1, middle, jnp.where(row == rows + 2, low, 0.0)),
    )
    return jnp.where(row < rows, out, stats).astype(BF16)


def pad_rows(length, query, padded):
    groups, steps, head_dim = query.shape
    rows = groups * steps
    for g in range(groups):
        padded[g * steps : (g + 1) * steps, :] = query[g].astype(F32)
    row = iota((PAD - rows, head_dim), 0)
    high = lax.shift_right_logical(length, 6).astype(F32)
    low = lax.bitwise_and(length, 63).astype(F32)
    padded[rows:PAD, :] = jnp.where(row == 0, high, jnp.where(row == 1, low, 0.0))


def fetch(pairs, sems):
    copies = [
        pltpu.make_async_copy(source, target, sems.at[i])
        for i, (source, target) in enumerate(pairs)
    ]
    for copy in copies:
        copy.start()
    return copies


def prep_kernel(lengths_hbm, queries_hbm, message, lengths, queries, padded, sems):
    copies = fetch(((lengths_hbm, lengths), (queries_hbm, queries)), sems)
    for copy in copies:
        copy.wait()
    long_slot, length = jnp.int32(0), lengths[0]
    for slot in range(1, queries.shape[0]):
        is_long = lengths[slot] > 256
        long_slot = jnp.where(is_long, slot, long_slot)
        length = jnp.where(is_long, lengths[slot], length)
    pad_rows(length, queries.at[long_slot], padded)
    message[...] = jnp.broadcast_to(padded[...].astype(BF16)[None], message.shape)


def attend(query, limit, keys, values, scale2):
    score = lax.dot_general(query, keys, (((1,), (1,)), ((), ())), preferred_element_type=F32)
    score = jnp.where(iota(score.shape, 1).astype(F32) < limit, score, neg_fill)
    top = jnp.max(score, axis=1, keepdims=True)
    weights = jnp.exp2((score - top) * scale2).astype(BF16)
    total = jnp.sum(weights.astype(F32), axis=1, keepdims=True)
    out = lax.dot_general(weights, values, (((1,), (0,)), ((), ())), preferred_element_type=F32)
    return out / total, top * scale2 + jnp.log2(total)


def local_kernel(
    scale2, lengths_hbm, owners_hbm, numbers_hbm, queries_hbm, new_keys_hbm, new_values_hbm,
    key_cache, value_cache,
    table, local_out, local_lse,
    lengths, owners, numbers, queries, new_keys, new_values, padded, near_keys, near_values, sems,
):
    blocks, span, head_dim = key_cache.shape
    slots, steps, _ = new_keys.shape
    me = lax.axis_index("serve")
    small = ((lengths_hbm, lengths), (owners_hbm, owners), (numbers_hbm, numbers),
             (queries_hbm, queries), (new_keys_hbm, new_keys), (new_values_hbm, new_values))
    copies = fetch(small, sems)
    for copy in copies:
        copy.wait()

    far_count, near_count = jnp.int32(0), jnp.int32(0)
    for p in range(blocks):
        owner, number = owners[p], numbers[p]
        device = lax.shift_right_logical(owner, 2)
        near = device == me
        at = jnp.where(near, blocks - 1 - near_count, far_count)
        table[at] = p
        table[64 + at] = jnp.where(near, lax.bitwise_and(owner, 3), column_first(device))
        table[128 + at] = number * span
        one = near.astype(jnp.int32)
        far_count, near_count = far_count + 1 - one, near_count + one
    table[192] = far_count
    for slot in range(slots):
        table[193 + slot] = lengths[slot]
    own_blocks = fetch(
        [(key_cache.at[table[blocks - 1 - k]], near_keys.at[k]) for k in range(slots)]
        + [(value_cache.at[table[blocks - 1 - k]], near_values.at[k]) for k in range(slots)],
        sems.at[pl.ds(8, 2 * slots)],
    )

    for slot in range(slots):
        pad_rows(lengths[slot], queries.at[slot], padded.at[slot])
    all_rows = padded[...].astype(BF16).reshape(slots * PAD, head_dim)
    nk = new_keys[...].astype(F32).reshape(slots * steps, head_dim).astype(BF16)
    nv = new_values[...].astype(F32).reshape(slots * steps, head_dim).astype(BF16)
    scores = lax.dot_general(all_rows, nk, (((1,), (1,)), ((), ())), preferred_element_type=F32)
    r2, c2 = iota(scores.shape, 0), iota(scores.shape, 1)
    seen = jnp.logical_and(r2 // PAD == c2 // steps, c2 % steps <= r2 % steps)
    scores = jnp.where(seen, scores, neg_fill)
    top = jnp.max(scores, axis=1, keepdims=True)
    weights = jnp.where(seen, jnp.exp2((scores - top) * scale2), 0.0).astype(BF16)
    total = jnp.sum(weights.astype(F32), axis=1, keepdims=True)
    out = lax.dot_general(weights, nv, (((1,), (0,)), ((), ())), preferred_element_type=F32)
    lse = jnp.broadcast_to(top * scale2 + jnp.log2(total), out.shape)
    local_out[...] = (out / total).reshape(local_out.shape)
    local_lse[...] = lse.reshape(local_lse.shape)

    def merge(slot, new_out, new):
        old = local_lse[slot]
        overall = jnp.maximum(old, new)
        a, b = jnp.exp2(old - overall), jnp.exp2(new - overall)
        total = a + b
        local_out[slot] = (a * local_out[slot] + b * new_out) / total
        local_lse[slot] = overall + jnp.log2(total)

    for copy in own_blocks:
        copy.wait()
    ats = [blocks - 1 - k for k in range(slots)]
    parts = []
    for k, at in enumerate(ats):
        slot = table[64 + at]
        limit = (lengths[slot] - table[128 + at]).astype(F32)
        parts.append(
            attend(padded[slot].astype(BF16), limit, near_keys[k], near_values[k], scale2)
        )
    for at, (new_out, new) in zip(ats, parts):
        merge(table[64 + at], new_out, jnp.broadcast_to(new, new_out.shape))

    def more(k, carry):
        at = blocks - 1 - k
        slot = table[64 + at]
        block = table[at]
        pair = ((key_cache.at[block], near_keys.at[0]), (value_cache.at[block], near_values.at[0]))
        for copy in fetch(pair, sems.at[pl.ds(8, 2)]):
            copy.wait()
        limit = (lengths[slot] - table[128 + at]).astype(F32)
        new_out, new = attend(
            padded[slot].astype(BF16), limit, near_keys[0], near_values[0], scale2
        )
        merge(slot, new_out, jnp.broadcast_to(new, new_out.shape))
        return carry

    lax.fori_loop(slots, near_count, more, 0)


def far_kernel(chunk, scale2, table, far, keys, values, back):
    blocks, span, head_dim = keys.shape
    rows = 28
    count = blocks - 4
    me = lax.axis_index("serve")
    far_count = table[192]
    row, lane = iota((PAD, head_dim), 0), iota((PAD, head_dim), 1)
    offset = lax.bitwise_and(me, 3) * PAD
    diagonal = jnp.logical_and(lane == offset + row, row < rows)
    in_span = jnp.logical_and(lane >= offset, lane < offset + rows)
    empty = jnp.where(jnp.logical_and(row == rows, in_span), neg_fill, 0.0).astype(BF16)
    back[...] = jnp.broadcast_to(empty[None], back.shape)
    unused = column_first(me)
    position = iota((PAD, span), 1).astype(F32)
    for c in range(count // chunk):
        ids = [table[k] for k in range(c * chunk, (c + 1) * chunk)]
        places = [
            jnp.where(k < far_count, table[64 + k], unused)
            for k in range(c * chunk, (c + 1) * chunk)
        ]
        raw = []
        for k in range(chunk):
            query = far[places[k]]
            lens = query[rows : rows + 2, :].astype(F32)
            length = lens[0:1, 0:1] * 64.0 + lens[1:2, 0:1]
            score = lax.dot_general(
                query, keys[ids[k]], (((1,), (1,)), ((), ())), preferred_element_type=F32
            )
            limit = length - table[128 + c * chunk + k].astype(F32)
            raw.append(jnp.where(position < limit, score, neg_fill))
        raw = jnp.concatenate(raw, axis=0)
        top = jnp.max(raw, axis=1, keepdims=True)
        weights = jnp.exp2((raw - top) * scale2).astype(BF16)
        total = jnp.sum(weights.astype(F32), axis=1, keepdims=True)
        lse = top * scale2 + jnp.log2(total)
        inverse = 1.0 / total
        for k in range(chunk):
            part = slice(k * PAD, (k + 1) * PAD)
            out = lax.dot_general(
                weights[part], values[ids[k]], (((1,), (0,)), ((), ())),
                preferred_element_type=F32,
            )
            flat = jnp.sum(jnp.where(diagonal, lse[part], 0.0), axis=0, keepdims=True)
            back[places[k]] = message_of(out * inverse[part], flat, rows)
    back[unused] = empty


def spread_kernel(column, copies):
    for k in range(copies.shape[0]):
        copies[k] = column[...]


def four_fold(x, op):
    x = op(x, pltpu.roll(x, 2 * PAD, 1))
    return op(x, pltpu.roll(x, PAD, 1))


def gathered_lse(groups, rows):
    part = iota(groups[0][0].shape, 0) + PAD // 2
    in_row = jnp.logical_and(part >= rows, part < rows + 3)
    out = []
    for group in groups:
        stats = sum(lower.astype(F32) for lower in group)
        out.append(jnp.sum(jnp.where(in_row, stats, 0.0), axis=0, keepdims=True))
    return jnp.concatenate(out, axis=0)


def stage_kernel(got, onward):
    sources, many, _, head_dim = got.shape
    rows = 28
    me = lax.axis_index("serve")
    lse = [
        gathered_lse(
            [[got[k, m, PAD // 2 :, :] for k in range(first, first + 4)] for m in range(many)], rows
        )
        for first in range(0, sources, 4)
    ]
    top = four_fold(functools.reduce(jnp.maximum, lse), jnp.maximum)
    weights = [jnp.exp2(part - top) for part in lse]
    total = four_fold(sum(weights), jnp.add)
    weights = [weight / total for weight in weights]
    row, lane = iota((PAD, head_dim), 0), iota((PAD, head_dim), 1)
    same = jnp.logical_and(lane % PAD == row, row < rows)
    offset = lax.bitwise_and(lax.shift_right_logical(me, 3), 3) * PAD
    lane = iota((many, head_dim), 1)
    in_span = jnp.logical_and(lane >= offset, lane < offset + rows)
    lse = jnp.where(in_span, top + jnp.log2(total), 0.0)
    for m in range(many):
        spread = jnp.concatenate(
            [jnp.where(same, weight[m : m + 1], 0.0) for weight in weights], axis=1
        )
        high = spread.astype(BF16)
        low = (spread - high.astype(F32)).astype(BF16)
        both = jnp.concatenate([high, low], axis=0)
        block = got[:, m].reshape(sources * PAD, head_dim)
        out = lax.dot_general(both, block, (((1,), (0,)), ((), ())), preferred_element_type=F32)
        onward[m] = message_of(out[:PAD] + out[PAD:], lse[m : m + 1], rows)


def combine_kernel(table, got, local_out, local_lse, result):
    devices, _, head_dim = got.shape
    slots = local_out.shape[0]
    steps, groups, rows = 4, 7, 28
    depth = devices * PAD
    many = devices // 4
    flat = got[...].reshape(depth, head_dim)
    lse = gathered_lse(
        [[got[4 * g + k, PAD // 2 :, :] for k in range(4)] for g in range(many)], rows
    )
    top = jnp.max(lse, axis=0, keepdims=True)
    top = jnp.broadcast_to(top, (8, head_dim))
    top = four_fold(top, jnp.maximum)
    weight = jnp.exp2(lse - top[0:1])
    row, lane = iota((PAD, head_dim), 0), iota((PAD, head_dim), 1)
    same = jnp.logical_and(lane % PAD == row, row < rows)
    spread = jnp.concatenate(
        [jnp.where(same, weight[g : g + 1], 0.0) for g in range(many)], axis=1
    )
    high = spread.astype(BF16)
    low = (spread - high.astype(F32)).astype(BF16)
    both = jnp.concatenate([high, low], axis=0)
    out = lax.dot_general(both, flat, (((1,), (0,)), ((), ())), preferred_element_type=F32)
    out = out[:PAD] + out[PAD:]
    total = jnp.sum(spread, axis=1, keepdims=True)
    total = jnp.where(row[:, 0:1] < rows, total, 1.0)
    first = jnp.logical_and(lane == row, row < rows)
    column = jnp.sum(jnp.where(first, top[0:1], 0.0), axis=1, keepdims=True)
    far_out = out / total
    far_lse = jnp.broadcast_to(column + jnp.log2(total), far_out.shape)
    for slot in range(slots):
        far_here = jnp.where(table[193 + slot] > 256, far_lse, neg_fill)
        near = local_lse[slot]
        overall = jnp.maximum(far_here, near)
        a, b = jnp.exp2(far_here - overall), jnp.exp2(near - overall)
        final = ((a * far_out + b * local_out[slot]) / (a + b)).astype(BF16)
        for g in range(groups):
            columns = slice(g * head_dim, (g + 1) * head_dim)
            for half in range(2):
                start = g * steps + half * 2
                result[slot * 2 + half, :, columns] = final[start : start + 2]


VMEM = pl.BlockSpec(memory_space=pltpu.VMEM)
SMEM = pl.BlockSpec(memory_space=pltpu.SMEM)
HBM = pl.BlockSpec(memory_space=pltpu.HBM)


def shards(
    queries, new_keys, new_values, key_cache, value_cache, lengths, block_owner, block_number
):
    slots, steps, groups, head_dim = queries.shape
    blocks, span = key_cache.shape[:2]
    devices = lax.axis_size("serve")
    chunk = 32
    scale2 = head_dim**-0.5 * math.log2(math.e)
    queries = jnp.transpose(queries, (0, 2, 1, 3))
    new_keys = new_keys.reshape(slots, steps, head_dim)
    new_values = new_values.reshape(slots, steps, head_dim)
    key_cache = key_cache.reshape(blocks, span, head_dim)
    value_cache = value_cache.reshape(blocks, span, head_dim)

    outer = [[SIDE * k + m for k in range(SIDE)] for m in range(SIDE)]
    inner = [[SIDE * k + m for m in range(SIDE)] for k in range(SIDE)]
    exchange = functools.partial(
        lax.all_to_all, axis_name="serve", split_axis=0, concat_axis=0, tiled=True
    )
    in_hbm = functools.partial(pltpu.with_memory_space_constraint, memory_space=pltpu.HBM)
    in_smem = functools.partial(pltpu.with_memory_space_constraint, memory_space=pltpu.SMEM)
    in_vmem = functools.partial(pltpu.with_memory_space_constraint, memory_space=pltpu.VMEM)
    plain_keys, plain_values = key_cache, value_cache
    queries, new_keys, new_values, key_cache, value_cache, lengths, block_owner, block_number = map(
        in_hbm,
        (queries, new_keys, new_values, key_cache, value_cache, lengths, block_owner, block_number),
    )
    small = pltpu.CompilerParams(vmem_limit_bytes=8 << 20)
    message = pl.pallas_call(
        prep_kernel,
        out_shape=jax.ShapeDtypeStruct((SIDE, PAD, head_dim), BF16),
        in_specs=[HBM, HBM],
        out_specs=VMEM,
        scratch_shapes=[
            pltpu.SMEM((slots,), jnp.int32),
            pltpu.VMEM(queries.shape, BF16),
            pltpu.VMEM((PAD, head_dim), F32),
            pltpu.SemaphoreType.DMA((2,)),
        ],
        compiler_params=small,
        name="prep",
    )(lengths, queries)
    table, local_out, local_lse = pl.pallas_call(
        functools.partial(local_kernel, scale2),
        out_shape=(
            pltpu.SMEM((256,), jnp.int32),
            jax.ShapeDtypeStruct((slots, PAD, head_dim), F32),
            jax.ShapeDtypeStruct((slots, PAD, head_dim), F32),
        ),
        in_specs=[HBM] * 8,
        out_specs=(SMEM, VMEM, VMEM),
        scratch_shapes=[
            pltpu.SMEM((slots,), jnp.int32),
            pltpu.SMEM((blocks,), jnp.int32),
            pltpu.SMEM((blocks,), jnp.int32),
            pltpu.VMEM(queries.shape, BF16),
            pltpu.VMEM(new_keys.shape, BF16),
            pltpu.VMEM(new_values.shape, BF16),
            pltpu.VMEM((slots, PAD, head_dim), F32),
            pltpu.VMEM((slots, span, head_dim), BF16),
            pltpu.VMEM((slots, span, head_dim), BF16),
            pltpu.SemaphoreType.DMA((8 + 2 * slots,)),
        ],
        compiler_params=small,
        cost_estimate=pl.CostEstimate(
            flops=1 << 28, bytes_accessed=key_cache.size * 2, transcendentals=1 << 18
        ),
        name="local",
    )(
        lengths, block_owner, block_number, queries, new_keys, new_values, key_cache, value_cache
    )
    column = exchange(message, axis_index_groups=outer)
    column, local_out = lax.optimization_barrier((column, local_out))
    copies = pl.pallas_call(
        spread_kernel,
        out_shape=jax.ShapeDtypeStruct((SIDE,) + column.shape, BF16),
        in_specs=[VMEM],
        out_specs=VMEM,
        compiler_params=small,
        cost_estimate=pl.CostEstimate(
            flops=1 << 32, bytes_accessed=1 << 20, transcendentals=0
        ),
        name="spread",
    )(column)
    far = exchange(copies, axis_index_groups=inner)
    back = pl.pallas_call(
        functools.partial(far_kernel, chunk, scale2),
        out_shape=jax.ShapeDtypeStruct((devices, PAD, head_dim), BF16),
        in_specs=[SMEM, VMEM, VMEM, VMEM],
        out_specs=VMEM,
        compiler_params=small,
        name="far",
    )(in_smem(table), far.reshape(devices, PAD, head_dim), in_vmem(plain_keys), in_vmem(plain_values))
    back = back.reshape(SIDE, SIDE, PAD, head_dim)
    row_got = exchange(back, axis_index_groups=inner)
    onward = pl.pallas_call(
        stage_kernel,
        out_shape=jax.ShapeDtypeStruct((SIDE, PAD, head_dim), BF16),
        in_specs=[VMEM],
        out_specs=VMEM,
        compiler_params=small,
        name="stage",
    )(row_got)
    got = exchange(onward, axis_index_groups=outer)
    rows_out = pl.pallas_call(
        combine_kernel,
        out_shape=jax.ShapeDtypeStruct((8, 2, groups * head_dim), BF16),
        in_specs=[SMEM, VMEM, VMEM, VMEM],
        out_specs=VMEM,
        compiler_params=small,
        name="combine",
    )(in_smem(table), got, local_out, local_lse)
    swapped = lax.all_to_all(rows_out, "tensor", split_axis=0, concat_axis=0, tiled=True)
    return jnp.transpose(swapped, (1, 0, 2)).reshape(2, 8 * groups * head_dim)


def solution(mesh):
    placed = (
        P("serve", None, "tensor", None),
        P("serve", None, "tensor", None),
        P("serve", None, "tensor", None),
        P("serve", None, "tensor", None),
        P("serve", None, "tensor", None),
        P("serve"),
        P("serve"),
        P("serve"),
    )
    return jax.shard_map(
        shards, mesh=mesh, in_specs=placed, out_specs=P(("serve", "tensor"), None), check_vma=False
    )
```

```python
import functools
import math

import jax
import jax.numpy as jnp
from jax import lax
from jax.experimental import pallas as pl
from jax.experimental.pallas import tpu as pltpu
from jax.sharding import PartitionSpec as P

neg_fill = -1e30
PAD = 32
F32 = jnp.float32
BF16 = jnp.bfloat16


def iota(shape, dim):
    return lax.broadcasted_iota(jnp.int32, shape, dim)


SIDE = 8


def column_first(device):
    return lax.bitwise_and(device, SIDE - 1) * SIDE + lax.shift_right_logical(device, 3)


def message_of(out, lse, rows):
    row = iota(out.shape, 0)
    high = lse.astype(BF16).astype(F32)
    rest = lse - high
    middle = rest.astype(BF16).astype(F32)
    low = rest - middle
    stats = jnp.where(
        row == rows,
        high,
        jnp.where(row == rows + 1, middle, jnp.where(row == rows + 2, low, 0.0)),
    )
    return jnp.where(row < rows, out, stats).astype(BF16)


def pad_rows(length, query, padded):
    groups, steps, head_dim = query.shape
    rows = groups * steps
    for g in range(groups):
        padded[g * steps : (g + 1) * steps, :] = query[g].astype(F32)
    row = iota((PAD - rows, head_dim), 0)
    high = lax.shift_right_logical(length, 6).astype(F32)
    low = lax.bitwise_and(length, 63).astype(F32)
    padded[rows:PAD, :] = jnp.where(row == 0, high, jnp.where(row == 1, low, 0.0))


def fetch(pairs, sems):
    copies = [
        pltpu.make_async_copy(source, target, sems.at[i])
        for i, (source, target) in enumerate(pairs)
    ]
    for copy in copies:
        copy.start()
    return copies


def prep_kernel(lengths_hbm, queries_hbm, message, lengths, queries, padded, sems):
    copies = fetch(((lengths_hbm, lengths), (queries_hbm, queries)), sems)
    for copy in copies:
        copy.wait()
    long_slot, length = jnp.int32(0), lengths[0]
    for slot in range(1, queries.shape[0]):
        is_long = lengths[slot] > 256
        long_slot = jnp.where(is_long, slot, long_slot)
        length = jnp.where(is_long, lengths[slot], length)
    pad_rows(length, queries.at[long_slot], padded)
    message[...] = jnp.broadcast_to(padded[...].astype(BF16)[None], message.shape)


def weigh(query, limit, keys, scale2):
    score = lax.dot_general(query, keys, (((1,), (1,)), ((), ())), preferred_element_type=F32)
    score = jnp.where(iota(score.shape, 1).astype(F32) < limit, score, neg_fill)
    top = jnp.max(score, axis=1, keepdims=True)
    weights = jnp.exp2((score - top) * scale2).astype(BF16)
    total = jnp.sum(weights.astype(F32), axis=1, keepdims=True)
    return weights, total, top * scale2 + jnp.log2(total)


def apply(weights, total, values):
    out = lax.dot_general(weights, values, (((1,), (0,)), ((), ())), preferred_element_type=F32)
    return out / total


def local_kernel(
    scale2, lengths_hbm, owners_hbm, numbers_hbm, queries_hbm, new_keys_hbm, new_values_hbm,
    key_cache, value_cache,
    table, local_out, local_lse,
    lengths, owners, numbers, queries, new_keys, new_values, padded, near_keys, near_values, sems,
):
    blocks, span, head_dim = key_cache.shape
    slots, steps, _ = new_keys.shape
    me = lax.axis_index("serve")
    small = ((lengths_hbm, lengths), (owners_hbm, owners), (numbers_hbm, numbers),
             (queries_hbm, queries), (new_keys_hbm, new_keys), (new_values_hbm, new_values))
    copies = fetch(small, sems)
    for copy in copies:
        copy.wait()

    far_count, near_count = jnp.int32(0), jnp.int32(0)
    for p in range(blocks):
        owner, number = owners[p], numbers[p]
        device = lax.shift_right_logical(owner, 2)
        near = device == me
        at = jnp.where(near, blocks - 1 - near_count, far_count)
        table[at] = p
        table[64 + at] = jnp.where(near, lax.bitwise_and(owner, 3), column_first(device))
        table[128 + at] = number * span
        one = near.astype(jnp.int32)
        far_count, near_count = far_count + 1 - one, near_count + one
    table[192] = far_count
    for slot in range(slots):
        table[193 + slot] = lengths[slot]
    own_blocks = fetch(
        [(key_cache.at[table[blocks - 1 - k]], near_keys.at[k]) for k in range(slots)]
        + [(value_cache.at[table[blocks - 1 - k]], near_values.at[k]) for k in range(slots)],
        sems.at[pl.ds(8, 2 * slots)],
    )

    for slot in range(slots):
        pad_rows(lengths[slot], queries.at[slot], padded.at[slot])
    all_rows = padded[...].astype(BF16).reshape(slots * PAD, head_dim)
    nk = new_keys[...].astype(F32).reshape(slots * steps, head_dim).astype(BF16)
    nv = new_values[...].astype(F32).reshape(slots * steps, head_dim).astype(BF16)
    scores = lax.dot_general(all_rows, nk, (((1,), (1,)), ((), ())), preferred_element_type=F32)
    r2, c2 = iota(scores.shape, 0), iota(scores.shape, 1)
    seen = jnp.logical_and(r2 // PAD == c2 // steps, c2 % steps <= r2 % steps)
    scores = jnp.where(seen, scores, neg_fill)
    top = jnp.max(scores, axis=1, keepdims=True)
    weights = jnp.where(seen, jnp.exp2((scores - top) * scale2), 0.0).astype(BF16)
    total = jnp.sum(weights.astype(F32), axis=1, keepdims=True)
    out = lax.dot_general(weights, nv, (((1,), (0,)), ((), ())), preferred_element_type=F32)
    lse = jnp.broadcast_to(top * scale2 + jnp.log2(total), out.shape)
    local_out[...] = (out / total).reshape(local_out.shape)
    local_lse[...] = lse.reshape(local_lse.shape)

    def merge(slot, new_out, new):
        old = local_lse[slot]
        overall = jnp.maximum(old, new)
        a, b = jnp.exp2(old - overall), jnp.exp2(new - overall)
        total = a + b
        local_out[slot] = (a * local_out[slot] + b * new_out) / total
        local_lse[slot] = overall + jnp.log2(total)

    for copy in own_blocks[:slots]:
        copy.wait()
    ats = [blocks - 1 - k for k in range(slots)]
    parts = []
    for k, at in enumerate(ats):
        slot = table[64 + at]
        limit = (lengths[slot] - table[128 + at]).astype(F32)
        parts.append(weigh(padded[slot].astype(BF16), limit, near_keys[k], scale2))
    for copy in own_blocks[slots:]:
        copy.wait()
    outs = [apply(part[0], part[1], near_values[k]) for k, part in enumerate(parts)]
    for at, part, new_out in zip(ats, parts, outs):
        merge(table[64 + at], new_out, jnp.broadcast_to(part[2], new_out.shape))

    def more(k, carry):
        at = blocks - 1 - k
        slot = table[64 + at]
        block = table[at]
        pair = ((key_cache.at[block], near_keys.at[0]), (value_cache.at[block], near_values.at[0]))
        for copy in fetch(pair, sems.at[pl.ds(8, 2)]):
            copy.wait()
        limit = (lengths[slot] - table[128 + at]).astype(F32)
        weights, total, new = weigh(padded[slot].astype(BF16), limit, near_keys[0], scale2)
        new_out = apply(weights, total, near_values[0])
        merge(slot, new_out, jnp.broadcast_to(new, new_out.shape))
        return carry

    lax.fori_loop(slots, near_count, more, 0)


def far_kernel(chunk, scale2, table, far, keys, values, back):
    blocks, span, head_dim = keys.shape
    rows = 28
    count = blocks - 4
    me = lax.axis_index("serve")
    far_count = table[192]
    row, lane = iota((PAD, head_dim), 0), iota((PAD, head_dim), 1)
    offset = lax.bitwise_and(me, 3) * PAD
    diagonal = jnp.logical_and(lane == offset + row, row < rows)
    in_span = jnp.logical_and(lane >= offset, lane < offset + rows)
    empty = jnp.where(jnp.logical_and(row == rows, in_span), neg_fill, 0.0).astype(BF16)
    back[...] = jnp.broadcast_to(empty[None], back.shape)
    unused = column_first(me)
    position = iota((PAD, span), 1).astype(F32)
    for c in range(count // chunk):
        ids = [table[k] for k in range(c * chunk, (c + 1) * chunk)]
        places = [
            jnp.where(k < far_count, table[64 + k], unused)
            for k in range(c * chunk, (c + 1) * chunk)
        ]
        raw = []
        for k in range(chunk):
            query = far[places[k]]
            lens = query[rows : rows + 2, :].astype(F32)
            length = lens[0:1, 0:1] * 64.0 + lens[1:2, 0:1]
            score = lax.dot_general(
                query, keys[ids[k]], (((1,), (1,)), ((), ())), preferred_element_type=F32
            )
            limit = length - table[128 + c * chunk + k].astype(F32)
            raw.append(jnp.where(position < limit, score, neg_fill))
        raw = jnp.concatenate(raw, axis=0)
        top = jnp.max(raw, axis=1, keepdims=True)
        weights = jnp.exp2((raw - top) * scale2).astype(BF16)
        total = jnp.sum(weights.astype(F32), axis=1, keepdims=True)
        lse = top * scale2 + jnp.log2(total)
        inverse = 1.0 / total
        for k in range(chunk):
            part = slice(k * PAD, (k + 1) * PAD)
            out = lax.dot_general(
                weights[part], values[ids[k]], (((1,), (0,)), ((), ())),
                preferred_element_type=F32,
            )
            flat = jnp.sum(jnp.where(diagonal, lse[part], 0.0), axis=0, keepdims=True)
            back[places[k]] = message_of(out * inverse[part], flat, rows)
    back[unused] = empty


def spread_kernel(column, copies):
    for k in range(copies.shape[0]):
        copies[k] = column[...]


def four_fold(x, op):
    x = op(x, pltpu.roll(x, 2 * PAD, 1))
    return op(x, pltpu.roll(x, PAD, 1))


def gathered_lse(groups, rows):
    part = iota(groups[0][0].shape, 0) + PAD // 2
    in_row = jnp.logical_and(part >= rows, part < rows + 3)
    out = []
    for group in groups:
        stats = sum(lower.astype(F32) for lower in group)
        out.append(jnp.sum(jnp.where(in_row, stats, 0.0), axis=0, keepdims=True))
    return jnp.concatenate(out, axis=0)


def stage_kernel(got, onward):
    sources, many, _, head_dim = got.shape
    rows = 28
    me = lax.axis_index("serve")
    lse = [
        gathered_lse(
            [[got[k, m, PAD // 2 :, :] for k in range(first, first + 4)] for m in range(many)], rows
        )
        for first in range(0, sources, 4)
    ]
    top = four_fold(functools.reduce(jnp.maximum, lse), jnp.maximum)
    weights = [jnp.exp2(part - top) for part in lse]
    total = four_fold(sum(weights), jnp.add)
    weights = [weight / total for weight in weights]
    row, lane = iota((PAD, head_dim), 0), iota((PAD, head_dim), 1)
    same = jnp.logical_and(lane % PAD == row, row < rows)
    offset = lax.bitwise_and(lax.shift_right_logical(me, 3), 3) * PAD
    lane = iota((many, head_dim), 1)
    in_span = jnp.logical_and(lane >= offset, lane < offset + rows)
    lse = jnp.where(in_span, top + jnp.log2(total), 0.0)
    for m in range(many):
        spread = jnp.concatenate(
            [jnp.where(same, weight[m : m + 1], 0.0) for weight in weights], axis=1
        )
        high = spread.astype(BF16)
        low = (spread - high.astype(F32)).astype(BF16)
        both = jnp.concatenate([high, low], axis=0)
        block = got[:, m].reshape(sources * PAD, head_dim)
        out = lax.dot_general(both, block, (((1,), (0,)), ((), ())), preferred_element_type=F32)
        onward[m] = message_of(out[:PAD] + out[PAD:], lse[m : m + 1], rows)


def combine_kernel(table, got, local_out, local_lse, result):
    devices, _, head_dim = got.shape
    slots = local_out.shape[0]
    steps, groups, rows = 4, 7, 28
    depth = devices * PAD
    many = devices // 4
    flat = got[...].reshape(depth, head_dim)
    lse = gathered_lse(
        [[got[4 * g + k, PAD // 2 :, :] for k in range(4)] for g in range(many)], rows
    )
    top = jnp.max(lse, axis=0, keepdims=True)
    top = jnp.broadcast_to(top, (8, head_dim))
    top = four_fold(top, jnp.maximum)
    weight = jnp.exp2(lse - top[0:1])
    row, lane = iota((PAD, head_dim), 0), iota((PAD, head_dim), 1)
    same = jnp.logical_and(lane % PAD == row, row < rows)
    spread = jnp.concatenate(
        [jnp.where(same, weight[g : g + 1], 0.0) for g in range(many)], axis=1
    )
    high = spread.astype(BF16)
    low = (spread - high.astype(F32)).astype(BF16)
    both = jnp.concatenate([high, low], axis=0)
    out = lax.dot_general(both, flat, (((1,), (0,)), ((), ())), preferred_element_type=F32)
    out = out[:PAD] + out[PAD:]
    total = jnp.sum(spread, axis=1, keepdims=True)
    total = jnp.where(row[:, 0:1] < rows, total, 1.0)
    first = jnp.logical_and(lane == row, row < rows)
    column = jnp.sum(jnp.where(first, top[0:1], 0.0), axis=1, keepdims=True)
    far_out = out / total
    far_lse = jnp.broadcast_to(column + jnp.log2(total), far_out.shape)
    for slot in range(slots):
        far_here = jnp.where(table[193 + slot] > 256, far_lse, neg_fill)
        near = local_lse[slot]
        overall = jnp.maximum(far_here, near)
        a, b = jnp.exp2(far_here - overall), jnp.exp2(near - overall)
        final = ((a * far_out + b * local_out[slot]) / (a + b)).astype(BF16)
        for g in range(groups):
            columns = slice(g * head_dim, (g + 1) * head_dim)
            for half in range(2):
                start = g * steps + half * 2
                result[slot * 2 + half, :, columns] = final[start : start + 2]


VMEM = pl.BlockSpec(memory_space=pltpu.VMEM)
SMEM = pl.BlockSpec(memory_space=pltpu.SMEM)
HBM = pl.BlockSpec(memory_space=pltpu.HBM)


def shards(
    queries, new_keys, new_values, key_cache, value_cache, lengths, block_owner, block_number
):
    slots, steps, groups, head_dim = queries.shape
    blocks, span = key_cache.shape[:2]
    devices = lax.axis_size("serve")
    chunk = 32
    scale2 = head_dim**-0.5 * math.log2(math.e)
    queries = jnp.transpose(queries, (0, 2, 1, 3))
    new_keys = new_keys.reshape(slots, steps, head_dim)
    new_values = new_values.reshape(slots, steps, head_dim)
    key_cache = key_cache.reshape(blocks, span, head_dim)
    value_cache = value_cache.reshape(blocks, span, head_dim)

    outer = [[SIDE * k + m for k in range(SIDE)] for m in range(SIDE)]
    inner = [[SIDE * k + m for m in range(SIDE)] for k in range(SIDE)]
    exchange = functools.partial(
        lax.all_to_all, axis_name="serve", split_axis=0, concat_axis=0, tiled=True
    )
    in_hbm = functools.partial(pltpu.with_memory_space_constraint, memory_space=pltpu.HBM)
    in_smem = functools.partial(pltpu.with_memory_space_constraint, memory_space=pltpu.SMEM)
    in_vmem = functools.partial(pltpu.with_memory_space_constraint, memory_space=pltpu.VMEM)
    plain_keys, plain_values = key_cache, value_cache
    queries, new_keys, new_values, key_cache, value_cache, lengths, block_owner, block_number = map(
        in_hbm,
        (queries, new_keys, new_values, key_cache, value_cache, lengths, block_owner, block_number),
    )
    small = pltpu.CompilerParams(vmem_limit_bytes=8 << 20)
    message = pl.pallas_call(
        prep_kernel,
        out_shape=jax.ShapeDtypeStruct((SIDE, PAD, head_dim), BF16),
        in_specs=[HBM, HBM],
        out_specs=VMEM,
        scratch_shapes=[
            pltpu.SMEM((slots,), jnp.int32),
            pltpu.VMEM(queries.shape, BF16),
            pltpu.VMEM((PAD, head_dim), F32),
            pltpu.SemaphoreType.DMA((2,)),
        ],
        compiler_params=small,
        name="prep",
    )(lengths, queries)
    table, local_out, local_lse = pl.pallas_call(
        functools.partial(local_kernel, scale2),
        out_shape=(
            pltpu.SMEM((256,), jnp.int32),
            jax.ShapeDtypeStruct((slots, PAD, head_dim), F32),
            jax.ShapeDtypeStruct((slots, PAD, head_dim), F32),
        ),
        in_specs=[HBM] * 8,
        out_specs=(SMEM, VMEM, VMEM),
        scratch_shapes=[
            pltpu.SMEM((slots,), jnp.int32),
            pltpu.SMEM((blocks,), jnp.int32),
            pltpu.SMEM((blocks,), jnp.int32),
            pltpu.VMEM(queries.shape, BF16),
            pltpu.VMEM(new_keys.shape, BF16),
            pltpu.VMEM(new_values.shape, BF16),
            pltpu.VMEM((slots, PAD, head_dim), F32),
            pltpu.VMEM((slots, span, head_dim), BF16),
            pltpu.VMEM((slots, span, head_dim), BF16),
            pltpu.SemaphoreType.DMA((8 + 2 * slots,)),
        ],
        compiler_params=small,
        cost_estimate=pl.CostEstimate(
            flops=1 << 28, bytes_accessed=key_cache.size * 2, transcendentals=1 << 18
        ),
        name="local",
    )(
        lengths, block_owner, block_number, queries, new_keys, new_values, key_cache, value_cache
    )
    column = exchange(message, axis_index_groups=outer)
    column, local_out = lax.optimization_barrier((column, local_out))
    copies = pl.pallas_call(
        spread_kernel,
        out_shape=jax.ShapeDtypeStruct((SIDE,) + column.shape, BF16),
        in_specs=[VMEM],
        out_specs=VMEM,
        compiler_params=small,
        cost_estimate=pl.CostEstimate(
            flops=1 << 32, bytes_accessed=1 << 20, transcendentals=0
        ),
        name="spread",
    )(column)
    far = exchange(copies, axis_index_groups=inner)
    back = pl.pallas_call(
        functools.partial(far_kernel, chunk, scale2),
        out_shape=jax.ShapeDtypeStruct((devices, PAD, head_dim), BF16),
        in_specs=[SMEM, VMEM, VMEM, VMEM],
        out_specs=VMEM,
        compiler_params=small,
        name="far",
    )(in_smem(table), far.reshape(devices, PAD, head_dim), in_vmem(plain_keys), in_vmem(plain_values))
    back = back.reshape(SIDE, SIDE, PAD, head_dim)
    row_got = exchange(back, axis_index_groups=inner)
    onward = pl.pallas_call(
        stage_kernel,
        out_shape=jax.ShapeDtypeStruct((SIDE, PAD, head_dim), BF16),
        in_specs=[VMEM],
        out_specs=VMEM,
        compiler_params=small,
        name="stage",
    )(row_got)
    got = exchange(onward, axis_index_groups=outer)
    rows_out = pl.pallas_call(
        combine_kernel,
        out_shape=jax.ShapeDtypeStruct((8, 2, groups * head_dim), BF16),
        in_specs=[SMEM, VMEM, VMEM, VMEM],
        out_specs=VMEM,
        compiler_params=small,
        name="combine",
    )(in_smem(table), got, local_out, local_lse)
    swapped = lax.all_to_all(rows_out, "tensor", split_axis=0, concat_axis=0, tiled=True)
    return jnp.transpose(swapped, (1, 0, 2)).reshape(2, 8 * groups * head_dim)


def solution(mesh):
    placed = (
        P("serve", None, "tensor", None),
        P("serve", None, "tensor", None),
        P("serve", None, "tensor", None),
        P("serve", None, "tensor", None),
        P("serve", None, "tensor", None),
        P("serve"),
        P("serve"),
        P("serve"),
    )
    return jax.shard_map(
        shards, mesh=mesh, in_specs=placed, out_specs=P(("serve", "tensor"), None), check_vma=False
    )
```

```python
import functools
import math

import jax
import jax.numpy as jnp
from jax import lax
from jax.experimental import pallas as pl
from jax.experimental.pallas import tpu as pltpu
from jax.sharding import PartitionSpec as P

neg_fill = -1e30
PAD = 32
F32 = jnp.float32
BF16 = jnp.bfloat16


def iota(shape, dim):
    return lax.broadcasted_iota(jnp.int32, shape, dim)


SIDE = 8


def column_first(device):
    return lax.bitwise_and(device, SIDE - 1) * SIDE + lax.shift_right_logical(device, 3)


def message_of(out, lse, rows):
    row = iota(out.shape, 0)
    high = lse.astype(BF16).astype(F32)
    rest = lse - high
    middle = rest.astype(BF16).astype(F32)
    low = rest - middle
    stats = jnp.where(
        row == rows,
        high,
        jnp.where(row == rows + 1, middle, jnp.where(row == rows + 2, low, 0.0)),
    )
    return jnp.where(row < rows, out, stats).astype(BF16)


def pad_rows(length, query, padded):
    groups, steps, head_dim = query.shape
    rows = groups * steps
    for g in range(groups):
        padded[g * steps : (g + 1) * steps, :] = query[g].astype(F32)
    row = iota((PAD - rows, head_dim), 0)
    high = lax.shift_right_logical(length, 6).astype(F32)
    low = lax.bitwise_and(length, 63).astype(F32)
    padded[rows:PAD, :] = jnp.where(row == 0, high, jnp.where(row == 1, low, 0.0))


def fetch(pairs, sems):
    copies = [
        pltpu.make_async_copy(source, target, sems.at[i])
        for i, (source, target) in enumerate(pairs)
    ]
    for copy in copies:
        copy.start()
    return copies


def prep_kernel(lengths_hbm, queries_hbm, message, lengths, queries, padded, sems):
    copies = fetch(((lengths_hbm, lengths), (queries_hbm, queries)), sems)
    for copy in copies:
        copy.wait()
    long_slot, length = jnp.int32(0), lengths[0]
    for slot in range(1, queries.shape[0]):
        is_long = lengths[slot] > 256
        long_slot = jnp.where(is_long, slot, long_slot)
        length = jnp.where(is_long, lengths[slot], length)
    pad_rows(length, queries.at[long_slot], padded)
    message[...] = jnp.broadcast_to(padded[...].astype(BF16)[None], message.shape)


def weigh(query, limit, keys, scale2):
    score = lax.dot_general(query, keys, (((1,), (1,)), ((), ())), preferred_element_type=F32)
    score = jnp.where(iota(score.shape, 1).astype(F32) < limit, score, neg_fill)
    top = jnp.max(score, axis=1, keepdims=True)
    weights = jnp.exp2((score - top) * scale2).astype(BF16)
    total = jnp.sum(weights.astype(F32), axis=1, keepdims=True)
    return weights, total, top * scale2 + jnp.log2(total)


def apply(weights, total, values):
    out = lax.dot_general(weights, values, (((1,), (0,)), ((), ())), preferred_element_type=F32)
    return out / total


def local_kernel(
    scale2, lengths_hbm, owners_hbm, numbers_hbm, queries_hbm, new_keys_hbm, new_values_hbm,
    key_cache, value_cache,
    table, local_out, local_lse,
    lengths, owners, numbers, queries, new_keys, new_values, padded, near_keys, near_values, sems,
):
    blocks, span, head_dim = key_cache.shape
    slots, steps, _ = new_keys.shape
    me = lax.axis_index("serve")
    small = ((lengths_hbm, lengths), (owners_hbm, owners), (numbers_hbm, numbers),
             (queries_hbm, queries), (new_keys_hbm, new_keys), (new_values_hbm, new_values))
    copies = fetch(small, sems)
    for copy in copies:
        copy.wait()

    far_count, near_count = jnp.int32(0), jnp.int32(0)
    for p in range(blocks):
        owner, number = owners[p], numbers[p]
        device = lax.shift_right_logical(owner, 2)
        near = device == me
        at = jnp.where(near, blocks - 1 - near_count, far_count)
        table[at] = p
        table[64 + at] = jnp.where(near, lax.bitwise_and(owner, 3), column_first(device))
        table[128 + at] = number * span
        one = near.astype(jnp.int32)
        far_count, near_count = far_count + 1 - one, near_count + one
    table[192] = far_count
    for slot in range(slots):
        table[193 + slot] = lengths[slot]
    own_blocks = fetch(
        [(key_cache.at[table[blocks - 1 - k]], near_keys.at[k]) for k in range(slots)]
        + [(value_cache.at[table[blocks - 1 - k]], near_values.at[k]) for k in range(slots)],
        sems.at[pl.ds(8, 2 * slots)],
    )

    for slot in range(slots):
        pad_rows(lengths[slot], queries.at[slot], padded.at[slot])
    all_rows = padded[...].astype(BF16).reshape(slots * PAD, head_dim)
    nk = new_keys[...].astype(F32).reshape(slots * steps, head_dim).astype(BF16)
    nv = new_values[...].astype(F32).reshape(slots * steps, head_dim).astype(BF16)
    scores = lax.dot_general(all_rows, nk, (((1,), (1,)), ((), ())), preferred_element_type=F32)
    r2, c2 = iota(scores.shape, 0), iota(scores.shape, 1)
    seen = jnp.logical_and(r2 // PAD == c2 // steps, c2 % steps <= r2 % steps)
    scores = jnp.where(seen, scores, neg_fill)
    top = jnp.max(scores, axis=1, keepdims=True)
    weights = jnp.where(seen, jnp.exp2((scores - top) * scale2), 0.0).astype(BF16)
    total = jnp.sum(weights.astype(F32), axis=1, keepdims=True)
    out = lax.dot_general(weights, nv, (((1,), (0,)), ((), ())), preferred_element_type=F32)
    lse = jnp.broadcast_to(top * scale2 + jnp.log2(total), out.shape)
    local_out[...] = (out / total).reshape(local_out.shape)
    local_lse[...] = lse.reshape(local_lse.shape)

    def merge(slot, new_out, new):
        old = local_lse[slot]
        overall = jnp.maximum(old, new)
        a, b = jnp.exp2(old - overall), jnp.exp2(new - overall)
        total = a + b
        local_out[slot] = (a * local_out[slot] + b * new_out) / total
        local_lse[slot] = overall + jnp.log2(total)

    for copy in own_blocks[:slots]:
        copy.wait()
    ats = [blocks - 1 - k for k in range(slots)]
    parts = []
    for k, at in enumerate(ats):
        slot = table[64 + at]
        limit = (lengths[slot] - table[128 + at]).astype(F32)
        parts.append(weigh(padded[slot].astype(BF16), limit, near_keys[k], scale2))
    for copy in own_blocks[slots:]:
        copy.wait()
    outs = [apply(part[0], part[1], near_values[k]) for k, part in enumerate(parts)]
    for at, part, new_out in zip(ats, parts, outs):
        merge(table[64 + at], new_out, jnp.broadcast_to(part[2], new_out.shape))

    def more(k, carry):
        at = blocks - 1 - k
        slot = table[64 + at]
        block = table[at]
        pair = ((key_cache.at[block], near_keys.at[0]), (value_cache.at[block], near_values.at[0]))
        for copy in fetch(pair, sems.at[pl.ds(8, 2)]):
            copy.wait()
        limit = (lengths[slot] - table[128 + at]).astype(F32)
        weights, total, new = weigh(padded[slot].astype(BF16), limit, near_keys[0], scale2)
        new_out = apply(weights, total, near_values[0])
        merge(slot, new_out, jnp.broadcast_to(new, new_out.shape))
        return carry

    lax.fori_loop(slots, near_count, more, 0)


def far_kernel(chunk, scale2, table, far, keys, values, back):
    blocks, span, head_dim = keys.shape
    rows = 28
    count = blocks - 4
    me = lax.axis_index("serve")
    far_count = table[192]
    row, lane = iota((PAD, head_dim), 0), iota((PAD, head_dim), 1)
    offset = lax.bitwise_and(me, 3) * PAD
    diagonal = jnp.logical_and(lane == offset + row, row < rows)
    in_span = jnp.logical_and(lane >= offset, lane < offset + rows)
    empty = jnp.where(jnp.logical_and(row == rows, in_span), neg_fill, 0.0).astype(BF16)
    back[...] = jnp.broadcast_to(empty[None], back.shape)
    unused = column_first(me)
    position = iota((PAD, span), 1).astype(F32)
    for c in range(count // chunk):
        ids = [table[k] for k in range(c * chunk, (c + 1) * chunk)]
        places = [
            jnp.where(k < far_count, table[64 + k], unused)
            for k in range(c * chunk, (c + 1) * chunk)
        ]
        raw = []
        for k in range(chunk):
            query = far[places[k]]
            lens = query[rows : rows + 2, :].astype(F32)
            length = lens[0:1, 0:1] * 64.0 + lens[1:2, 0:1]
            score = lax.dot_general(
                query, keys[ids[k]], (((1,), (1,)), ((), ())), preferred_element_type=F32
            )
            limit = length - table[128 + c * chunk + k].astype(F32)
            raw.append(jnp.where(position < limit, score, neg_fill))
        raw = jnp.concatenate(raw, axis=0)
        top = jnp.max(raw, axis=1, keepdims=True)
        weights = jnp.exp2((raw - top) * scale2).astype(BF16)
        total = jnp.sum(weights.astype(F32), axis=1, keepdims=True)
        lse = top * scale2 + jnp.log2(total)
        inverse = 1.0 / total
        for k in range(chunk):
            part = slice(k * PAD, (k + 1) * PAD)
            out = lax.dot_general(
                weights[part], values[ids[k]], (((1,), (0,)), ((), ())),
                preferred_element_type=F32,
            )
            flat = jnp.sum(jnp.where(diagonal, lse[part], 0.0), axis=0, keepdims=True)
            back[places[k]] = message_of(out * inverse[part], flat, rows)
    back[unused] = empty


def spread_kernel(column, copies):
    for k in range(copies.shape[0]):
        copies[k] = column[...]


def four_fold(x, op):
    x = op(x, pltpu.roll(x, 2 * PAD, 1))
    return op(x, pltpu.roll(x, PAD, 1))


def gathered_lse(groups, rows):
    part = iota(groups[0][0].shape, 0) + PAD // 2
    in_row = jnp.logical_and(part >= rows, part < rows + 3)
    out = []
    for group in groups:
        stats = sum(lower.astype(F32) for lower in group)
        out.append(jnp.sum(jnp.where(in_row, stats, 0.0), axis=0, keepdims=True))
    return jnp.concatenate(out, axis=0)


def stage_kernel(got, onward):
    sources, many, _, head_dim = got.shape
    rows = 28
    me = lax.axis_index("serve")
    lse = [
        gathered_lse(
            [[got[k, m, PAD // 2 :, :] for k in range(first, first + 4)] for m in range(many)], rows
        )
        for first in range(0, sources, 4)
    ]
    top = four_fold(functools.reduce(jnp.maximum, lse), jnp.maximum)
    weights = [jnp.exp2(part - top) for part in lse]
    total = four_fold(sum(weights), jnp.add)
    weights = [weight / total for weight in weights]
    row, lane = iota((PAD, head_dim), 0), iota((PAD, head_dim), 1)
    same = jnp.logical_and(lane % PAD == row, row < rows)
    offset = lax.bitwise_and(lax.shift_right_logical(me, 3), 3) * PAD
    lane = iota((many, head_dim), 1)
    in_span = jnp.logical_and(lane >= offset, lane < offset + rows)
    lse = jnp.where(in_span, top + jnp.log2(total), 0.0)
    for m in range(many):
        spread = jnp.concatenate(
            [jnp.where(same, weight[m : m + 1], 0.0) for weight in weights], axis=1
        )
        block = got[:, m].reshape(sources * PAD, head_dim)
        out = lax.dot_general(
            spread.astype(BF16), block, (((1,), (0,)), ((), ())), preferred_element_type=F32
        )
        onward[m] = message_of(out, lse[m : m + 1], rows)


def combine_kernel(table, got, local_out, local_lse, result):
    devices, _, head_dim = got.shape
    slots = local_out.shape[0]
    steps, groups, rows = 4, 7, 28
    depth = devices * PAD
    many = devices // 4
    flat = got[...].reshape(depth, head_dim)
    lse = gathered_lse(
        [[got[4 * g + k, PAD // 2 :, :] for k in range(4)] for g in range(many)], rows
    )
    top = jnp.max(lse, axis=0, keepdims=True)
    top = jnp.broadcast_to(top, (8, head_dim))
    top = four_fold(top, jnp.maximum)
    weight = jnp.exp2(lse - top[0:1])
    row, lane = iota((PAD, head_dim), 0), iota((PAD, head_dim), 1)
    same = jnp.logical_and(lane % PAD == row, row < rows)
    spread = jnp.concatenate(
        [jnp.where(same, weight[g : g + 1], 0.0) for g in range(many)], axis=1
    )
    high = spread.astype(BF16)
    low = (spread - high.astype(F32)).astype(BF16)
    both = jnp.concatenate([high, low], axis=0)
    out = lax.dot_general(both, flat, (((1,), (0,)), ((), ())), preferred_element_type=F32)
    out = out[:PAD] + out[PAD:]
    total = jnp.sum(spread, axis=1, keepdims=True)
    total = jnp.where(row[:, 0:1] < rows, total, 1.0)
    first = jnp.logical_and(lane == row, row < rows)
    column = jnp.sum(jnp.where(first, top[0:1], 0.0), axis=1, keepdims=True)
    far_out = out / total
    far_lse = jnp.broadcast_to(column + jnp.log2(total), far_out.shape)
    for slot in range(slots):
        far_here = jnp.where(table[193 + slot] > 256, far_lse, neg_fill)
        near = local_lse[slot]
        overall = jnp.maximum(far_here, near)
        a, b = jnp.exp2(far_here - overall), jnp.exp2(near - overall)
        final = ((a * far_out + b * local_out[slot]) / (a + b)).astype(BF16)
        for g in range(groups):
            columns = slice(g * head_dim, (g + 1) * head_dim)
            for half in range(2):
                start = g * steps + half * 2
                result[slot * 2 + half, :, columns] = final[start : start + 2]


VMEM = pl.BlockSpec(memory_space=pltpu.VMEM)
SMEM = pl.BlockSpec(memory_space=pltpu.SMEM)
HBM = pl.BlockSpec(memory_space=pltpu.HBM)


def shards(
    queries, new_keys, new_values, key_cache, value_cache, lengths, block_owner, block_number
):
    slots, steps, groups, head_dim = queries.shape
    blocks, span = key_cache.shape[:2]
    devices = lax.axis_size("serve")
    chunk = 32
    scale2 = head_dim**-0.5 * math.log2(math.e)
    queries = jnp.transpose(queries, (0, 2, 1, 3))
    new_keys = new_keys.reshape(slots, steps, head_dim)
    new_values = new_values.reshape(slots, steps, head_dim)
    key_cache = key_cache.reshape(blocks, span, head_dim)
    value_cache = value_cache.reshape(blocks, span, head_dim)

    outer = [[SIDE * k + m for k in range(SIDE)] for m in range(SIDE)]
    inner = [[SIDE * k + m for m in range(SIDE)] for k in range(SIDE)]
    exchange = functools.partial(
        lax.all_to_all, axis_name="serve", split_axis=0, concat_axis=0, tiled=True
    )
    in_hbm = functools.partial(pltpu.with_memory_space_constraint, memory_space=pltpu.HBM)
    in_smem = functools.partial(pltpu.with_memory_space_constraint, memory_space=pltpu.SMEM)
    in_vmem = functools.partial(pltpu.with_memory_space_constraint, memory_space=pltpu.VMEM)
    plain_keys, plain_values = key_cache, value_cache
    queries, new_keys, new_values, key_cache, value_cache, lengths, block_owner, block_number = map(
        in_hbm,
        (queries, new_keys, new_values, key_cache, value_cache, lengths, block_owner, block_number),
    )
    small = pltpu.CompilerParams(vmem_limit_bytes=8 << 20)
    message = pl.pallas_call(
        prep_kernel,
        out_shape=jax.ShapeDtypeStruct((SIDE, PAD, head_dim), BF16),
        in_specs=[HBM, HBM],
        out_specs=VMEM,
        scratch_shapes=[
            pltpu.SMEM((slots,), jnp.int32),
            pltpu.VMEM(queries.shape, BF16),
            pltpu.VMEM((PAD, head_dim), F32),
            pltpu.SemaphoreType.DMA((2,)),
        ],
        compiler_params=small,
        name="prep",
    )(lengths, queries)
    table, local_out, local_lse = pl.pallas_call(
        functools.partial(local_kernel, scale2),
        out_shape=(
            pltpu.SMEM((256,), jnp.int32),
            jax.ShapeDtypeStruct((slots, PAD, head_dim), F32),
            jax.ShapeDtypeStruct((slots, PAD, head_dim), F32),
        ),
        in_specs=[HBM] * 8,
        out_specs=(SMEM, VMEM, VMEM),
        scratch_shapes=[
            pltpu.SMEM((slots,), jnp.int32),
            pltpu.SMEM((blocks,), jnp.int32),
            pltpu.SMEM((blocks,), jnp.int32),
            pltpu.VMEM(queries.shape, BF16),
            pltpu.VMEM(new_keys.shape, BF16),
            pltpu.VMEM(new_values.shape, BF16),
            pltpu.VMEM((slots, PAD, head_dim), F32),
            pltpu.VMEM((slots, span, head_dim), BF16),
            pltpu.VMEM((slots, span, head_dim), BF16),
            pltpu.SemaphoreType.DMA((8 + 2 * slots,)),
        ],
        compiler_params=small,
        cost_estimate=pl.CostEstimate(
            flops=1 << 28, bytes_accessed=key_cache.size * 2, transcendentals=1 << 18
        ),
        name="local",
    )(
        lengths, block_owner, block_number, queries, new_keys, new_values, key_cache, value_cache
    )
    column = exchange(message, axis_index_groups=outer)
    column, local_out = lax.optimization_barrier((column, local_out))
    copies = pl.pallas_call(
        spread_kernel,
        out_shape=jax.ShapeDtypeStruct((SIDE,) + column.shape, BF16),
        in_specs=[VMEM],
        out_specs=VMEM,
        compiler_params=small,
        cost_estimate=pl.CostEstimate(
            flops=1 << 32, bytes_accessed=1 << 20, transcendentals=0
        ),
        name="spread",
    )(column)
    far = exchange(copies, axis_index_groups=inner)
    back = pl.pallas_call(
        functools.partial(far_kernel, chunk, scale2),
        out_shape=jax.ShapeDtypeStruct((devices, PAD, head_dim), BF16),
        in_specs=[SMEM, VMEM, VMEM, VMEM],
        out_specs=VMEM,
        compiler_params=small,
        name="far",
    )(in_smem(table), far.reshape(devices, PAD, head_dim), in_vmem(plain_keys), in_vmem(plain_values))
    back = back.reshape(SIDE, SIDE, PAD, head_dim)
    row_got = exchange(back, axis_index_groups=inner)
    onward = pl.pallas_call(
        stage_kernel,
        out_shape=jax.ShapeDtypeStruct((SIDE, PAD, head_dim), BF16),
        in_specs=[VMEM],
        out_specs=VMEM,
        compiler_params=small,
        name="stage",
    )(row_got)
    got = exchange(onward, axis_index_groups=outer)
    rows_out = pl.pallas_call(
        combine_kernel,
        out_shape=jax.ShapeDtypeStruct((8, 2, groups * head_dim), BF16),
        in_specs=[SMEM, VMEM, VMEM, VMEM],
        out_specs=VMEM,
        compiler_params=small,
        name="combine",
    )(in_smem(table), got, local_out, local_lse)
    swapped = lax.all_to_all(rows_out, "tensor", split_axis=0, concat_axis=0, tiled=True)
    return jnp.transpose(swapped, (1, 0, 2)).reshape(2, 8 * groups * head_dim)


def solution(mesh):
    placed = (
        P("serve", None, "tensor", None),
        P("serve", None, "tensor", None),
        P("serve", None, "tensor", None),
        P("serve", None, "tensor", None),
        P("serve", None, "tensor", None),
        P("serve"),
        P("serve"),
        P("serve"),
    )
    return jax.shard_map(
        shards, mesh=mesh, in_specs=placed, out_specs=P(("serve", "tensor"), None), check_vma=False
    )
```
